32 devices in a mesh: dp: 8 (over y, x, core), pipe: 4 (over z).
Axes of the slice: x: 2, y: 2, z: 4, core: 2. Of those that a mesh axis runs over, the one named last changes fastest.
Arguments:
- layer_input: bfloat16 [64, 128, 768], P('dp'), may hold values from -6 to 6
- lengths: int32 [64], P('dp'), may hold values from 8 to 128
- regions: int32 [64, 128], P('dp'), may hold values 0 or 1
- cotangent: bfloat16 [64, 128, 768], P('dp'), may hold values from -6 to 6
- attend_weight: bfloat16 [4, 768, 2304], P('pipe'), may hold values from -0.3125 to 0.3125
- attend_bias: bfloat16 [4, 1536], P('pipe'), may hold values from -4 to 4
- output_weight: bfloat16 [4, 768, 768], P('pipe'), may hold values from -0.875 to 0.875
- output_bias: bfloat16 [4, 768], P('pipe'), may hold values from -3 to 3
- first_gain: bfloat16 [4, 768], P('pipe'), may hold values from 0.5 to 1.5
- first_shift: bfloat16 [4, 768], P('pipe'), may hold values from -3 to 3
- expand_weight: bfloat16 [4, 768, 3072], P('pipe'), may hold values from -0.21875 to 0.21875
- expand_bias: bfloat16 [4, 3072], P('pipe'), may hold values from -6 to 6
- reduce_weight: bfloat16 [4, 3072, 768], P('pipe'), may hold values from -0.109375 to 0.109375
- reduce_bias: bfloat16 [4, 768], P('pipe'), may hold values from -3 to 3
- second_gain: bfloat16 [4, 768], P('pipe'), may hold values from 0.5 to 1.5
- second_shift: bfloat16 [4, 768], P('pipe'), may hold values from -3 to 3
Outputs:
- layer_outputs: bfloat16 [4, 64, 128, 768], P('pipe', 'dp')
- input_grads: float32 [4, 64, 128, 768], P('pipe', 'dp')
- attend_weight_grad: float32 [4, 768, 2304], P('pipe')
- attend_bias_grad: float32 [4, 1536], P('pipe')
- output_weight_grad: float32 [4, 768, 768], P('pipe')
- output_bias_grad: float32 [4, 768], P('pipe')
- first_gain_grad: float32 [4, 768], P('pipe')
- first_shift_grad: float32 [4, 768], P('pipe')
- expand_weight_grad: float32 [4, 768, 3072], P('pipe')
- expand_bias_grad: float32 [4, 3072], P('pipe')
- reduce_weight_grad: float32 [4, 3072, 768], P('pipe')
- reduce_bias_grad: float32 [4, 768], P('pipe')
- second_gain_grad: float32 [4, 768], P('pipe')
- second_shift_grad: float32 [4, 768], P('pipe')
The draws below stay inside these ranges and needn't reach their ends.
All inputs are finite; a program needn't handle non-finite values. No bound on the sum of `regions` on one device may be relied on, other than what follows from the above.
Results may differ from the reference program's by a relative error of at most 0.035.
Values may be sent and summed in bfloat16 or wider, within the bound.
A program may use at most 256 MiB of HBM per device.

```python
import jax
import jax.numpy as jnp
from jax import lax

D = 768
HEADS = 12
HEAD = 64
FF = 3072
SLOTS = 128
SEQ_DEV = 8
SEQS = 64
LAYERS = 4
N_DP = 8


def place_ends(array, key, low, largest):
    dims = array.shape
    place = [jax.random.randint(jax.random.fold_in(key, axis), (), 0, dims[axis]) for axis in range(len(dims))]
    array = array.at[tuple(place)].set(low)
    longest = dims.index(max(dims))
    place[longest] = (place[longest] + 1) % dims[longest]
    return array.at[tuple(place)].set(largest)


def level_of(stream_key, dims, pieces, smallest, largest):
    def one(position, blocks):
        draws = jax.random.uniform(jax.random.fold_in(jax.random.fold_in(stream_key, 6), position), (blocks,), jnp.float32, smallest / len(pieces), largest / len(pieces))
        return jnp.repeat(jnp.exp(draws), dims[position] // blocks).reshape((-1,) + (1,) * (len(dims) - position - 1))

    level = one(*pieces[0])
    for cut in pieces[1:]:
        level = level * one(*cut)
    return level


def normal_values(stream_key, dims, width, limit, shards=(), kind=jnp.bfloat16):
    values = jax.random.normal(stream_key, dims, jnp.float32) * width
    if len(shards) > 0:
        values = level_of(stream_key, dims, shards, -0.22, 0.18) * values
    return jnp.clip(values, min=-limit, max=limit).astype(kind)


def setup_inputs(seed: int = 0) -> dict:
    key_of = jax.random.split(jax.random.key(seed), 17)
    layer_input = normal_values(key_of[0], (SEQS, SLOTS, D), 1.0, 6.0, ((0, 8),))
    lengths = place_ends(jax.random.randint(key_of[1], (SEQS,), 8, SLOTS + 1), jax.random.fold_in(key_of[1], 1), 8, SLOTS).astype(jnp.int32)
    regions = place_ends((jax.random.randint(key_of[2], (SEQS, SLOTS), 0, 2) < 1).astype(jnp.int32), jax.random.fold_in(key_of[2], 1), 0, 1)
    cotangent = normal_values(key_of[3], (SEQS, SLOTS, D), 1.0, 6.0, ((0, 8),))
    attend_weight = normal_values(key_of[4], (LAYERS, D, 3 * D), (D // 2) ** -0.5, 0.3125, ((0, 4),))
    attend_bias = normal_values(key_of[5], (LAYERS, 2 * D), 0.3, 4.0, ((0, 4),))
    output_weight = normal_values(key_of[6], (LAYERS, D, D), (D // 16) ** -0.5, 0.875, ((0, 4),))
    output_bias = normal_values(key_of[7], (LAYERS, D), 0.2, 3.0, ((0, 4),))
    first_gain = jnp.clip(1.0 + 0.1 * jax.random.normal(key_of[8], (LAYERS, D), jnp.float32), 0.5, 1.5).astype(jnp.bfloat16)
    first_shift = normal_values(key_of[9], (LAYERS, D), 0.2, 3.0, ((0, 4),))
    expand_weight = normal_values(key_of[10], (LAYERS, D, FF), D ** -0.5, 0.21875, ((0, 4),))
    expand_bias = normal_values(key_of[11], (LAYERS, FF), 0.5, 6.0, ((0, 4),))
    reduce_weight = normal_values(key_of[12], (LAYERS, FF, D), FF ** -0.5, 0.109375, ((0, 4),))
    reduce_bias = normal_values(key_of[13], (LAYERS, D), 0.2, 3.0, ((0, 4),))
    second_gain = jnp.clip(1.0 + 0.1 * jax.random.normal(key_of[14], (LAYERS, D), jnp.float32), 0.5, 1.5).astype(jnp.bfloat16)
    second_shift = normal_values(key_of[15], (LAYERS, D), 0.2, 3.0, ((0, 4),))
    return {"layer_input": layer_input, "lengths": lengths, "regions": regions, "cotangent": cotangent, "attend_weight": attend_weight, "attend_bias": attend_bias, "output_weight": output_weight, "output_bias": output_bias, "first_gain": first_gain, "first_shift": first_shift, "expand_weight": expand_weight, "expand_bias": expand_bias, "reduce_weight": reduce_weight, "reduce_bias": reduce_bias, "second_gain": second_gain, "second_shift": second_shift}


@jax.custom_vjp
def low(v):
    return lax.optimization_barrier(v.astype(jnp.bfloat16)).astype(jnp.float32)

@jax.custom_vjp
def low_back(v):
    return v

def low_keep(v):
    return (low(v), None)

def low_pass(kept, grad):
    return (grad,)

def back_keep(v):
    return (v, None)

def back_low(kept, grad):
    return (low(grad),)
low.defvjp(low_keep, low_pass)
low_back.defvjp(back_keep, back_low)

def matmul(left, right):
    return jnp.dot(left, right, precision=lax.Precision.HIGHEST, preferred_element_type=jnp.float32)

def layer_norm(entries, norm_gain, norm_shift):
    centre = entries - lax.optimization_barrier(jnp.mean(entries, -1, keepdims=True))
    scale_inv = lax.rsqrt(lax.optimization_barrier(jnp.mean(centre * centre, -1, keepdims=True)) + 1e-05)
    return centre * scale_inv * norm_gain + norm_shift

def attend(batch):
    queries, key_rows, values, key_valid = batch
    scores = jnp.einsum('gqhe,gkhe->ghqk', queries, key_rows, precision=lax.Precision.HIGHEST) * HEAD ** (-0.5)
    scores = low_back(jnp.where(key_valid[:, None, None, :], scores, -1000000000.0))
    shares = low(jax.nn.softmax(scores, axis=-1))
    return jnp.einsum('ghqk,gkhe->gqhe', shares, values, precision=lax.Precision.HIGHEST)

def grouped(entries):
    return entries.reshape(N_DP, SEQ_DEV, SLOTS, HEADS, HEAD)

def run_layer(hidden, weights, key_valid):
    attend_weight, attend_bias, output_weight, output_bias, first_gain, first_shift, expand_weight, expand_bias, reduce_weight, reduce_bias, second_gain, second_shift = weights
    token_rows = hidden.reshape(SEQS * SLOTS, D)
    projected = matmul(token_rows, attend_weight)
    queries = low_back(low(projected[:, :D] + attend_bias[:D]))
    key_rows = low_back(low(projected[:, D:2 * D]))
    values = low_back(low(projected[:, 2 * D:] + attend_bias[D:]))
    context = lax.map(jax.checkpoint(attend), (grouped(queries), grouped(key_rows), grouped(values), key_valid.reshape(N_DP, SEQ_DEV, SLOTS)))
    context = low_back(low(context.reshape(SEQS * SLOTS, D)))
    attended = low_back(matmul(context, output_weight) + output_bias)
    first_out = layer_norm(token_rows + attended, first_gain, first_shift)
    expanded = low_back(matmul(low(first_out), expand_weight) + expand_bias)
    active = low(jax.nn.gelu(expanded, approximate=False))
    reduced = low_back(matmul(active, reduce_weight) + reduce_bias)
    return layer_norm(first_out + reduced, second_gain, second_shift).reshape(SEQS, SLOTS, D)

def forward_run(params, shifts, start_rows, key_valid):
    hidden = start_rows
    layer_list = []
    for layer_at in range(LAYERS):
        hidden = hidden + shifts[layer_at]
        hidden = run_layer(hidden, tuple((weight[layer_at] for weight in params)), key_valid)
        hidden = low(low_back(hidden))
        layer_list.append(hidden)
    return (hidden, jnp.stack(layer_list))

def reference(layer_input, lengths, regions, cotangent, attend_weight, attend_bias, output_weight, output_bias, first_gain, first_shift, expand_weight, expand_bias, reduce_weight, reduce_bias, second_gain, second_shift):
    positions = jnp.arange(SLOTS, dtype=jnp.int32)
    key_valid = (positions[None, :] < lengths[:, None]) | (regions == 1)
    params = tuple((weight.astype(jnp.float32) for weight in (attend_weight, attend_bias, output_weight, output_bias, first_gain, first_shift, expand_weight, expand_bias, reduce_weight, reduce_bias, second_gain, second_shift)))
    start_rows = layer_input.astype(jnp.float32)
    shifts = jnp.zeros((LAYERS, SEQS, SLOTS, D), jnp.float32)

    def closed_run(params, shifts):
        return forward_run(params, shifts, start_rows, key_valid)
    final_out, pull_back, layer_list = jax.vjp(closed_run, params, shifts, has_aux=True)
    param_grads, shift_grads = pull_back(cotangent.astype(jnp.float32))
    return (layer_list.astype(jnp.bfloat16), shift_grads, param_grads[0], param_grads[1], param_grads[2], param_grads[3], param_grads[4], param_grads[5], param_grads[6], param_grads[7], param_grads[8], param_grads[9], param_grads[10], param_grads[11])
```

```python
import functools

import jax
import jax.numpy as jnp
from jax import lax
from jax.experimental import pallas as pl
from jax.experimental.pallas import tpu as pltpu
from jax.sharding import PartitionSpec as P

HEADS = 12
GROUP = 2
BLOCK = 32
CHUNK = 512
epsilon = 1e-05
neg_large = -1000000000.0
MESH = pl.DeviceIdType.MESH
f32 = jnp.float32
bf16 = jnp.bfloat16


def nn(left, right):
    return jnp.dot(left, right, preferred_element_type=f32)


def nt(left, right):
    return lax.dot_general(left, right, (((1,), (1,)), ((), ())), preferred_element_type=f32)


def tn(left, right):
    return lax.dot_general(left, right, (((0,), (0,)), ((), ())), preferred_element_type=f32)


def gelu_pair(x):
    z = jnp.abs(x) * 0.7071067811865476
    t = 1.0 / (1.0 + 0.3275911 * z)
    e = jnp.exp(-0.5 * (x * x))
    poly = t * (0.127414796 + t * (-0.142248368 + t * (0.7107068705 + t * (-0.7265760135 + t * 0.5307027145))))
    tail = poly * e
    phi = jnp.where(x >= 0, 1.0 - tail, tail)
    return x * phi, phi + (x * 0.3989422804014327) * e


def fold(v):
    rows, cols = v.shape
    return jnp.sum(v.reshape(rows // 8, 8, cols), 0)


def pipeline_kernel(
    micro,
    x_any, ct_any, valid, aw, ow, ew, rw, ab, ob, g1, s1, eb, rb, g2, s2,
    y_out, gin_out, h_out, ctx_out, low_out, act_out, gred_out, gexp_out, gatt_out, gproj_out, sums,
    h_ref, g_ref, y_ref, gb_ref, qkv, shares, gp, n1, r1, n2, r2,
    ctx, low, act, gred, gexp, gatt, gproj, gin, acc, mid,
    h_sem, g_sem, ysend_sem, yrecv_sem, gsend_sem, grecv_sem, y_sem, hs_sem,
    ctx_sem, low_sem, act_sem, gred_sem, gexp_sem, gatt_sem, gproj_sem, gin_sem,
):
    stage = lax.axis_index("pipe")
    count = lax.axis_size("pipe")
    last = count - 1
    slots = valid.shape[2]
    rows = h_ref.shape[1]
    groups = rows // slots
    width = h_ref.shape[2]
    hidden = ew.shape[1]
    pairs = width // 128
    before = jnp.maximum(stage - 1, 0)
    after = jnp.minimum(stage + 1, last)

    def send_y(m):
        return pltpu.make_async_remote_copy(
            src_ref=y_ref.at[m], dst_ref=h_ref.at[m], send_sem=ysend_sem.at[m], recv_sem=yrecv_sem.at[m],
            device_id={"pipe": after}, device_id_type=MESH)

    def send_g(m):
        return pltpu.make_async_remote_copy(
            src_ref=gb_ref.at[m], dst_ref=g_ref.at[m], send_sem=gsend_sem.at[m], recv_sem=grecv_sem.at[m],
            device_id={"pipe": before}, device_id_type=MESH)

    def load_h(m):
        return pltpu.make_async_copy(x_any.at[pl.ds(m * rows, rows)], h_ref.at[m], h_sem.at[m])

    def load_g(m):
        return pltpu.make_async_copy(ct_any.at[pl.ds(m * rows, rows)], g_ref.at[m], g_sem.at[m])

    def store(src, dst, sem, m, slot):
        return pltpu.make_async_copy(src.at[slot], dst.at[pl.ds(m * rows, rows)], sem.at[slot])

    @pl.when(stage == 0)
    def _():
        for m in range(micro):
            load_h(m).start()

    @pl.when(stage == last)
    def _():
        for m in range(micro):
            load_g(m).start()

    barrier = pltpu.get_barrier_semaphore()

    @pl.when(stage > 0)
    def _():
        pl.semaphore_signal(barrier, inc=1, device_id={"pipe": before}, device_id_type=MESH)

    @pl.when(stage < last)
    def _():
        pl.semaphore_signal(barrier, inc=1, device_id={"pipe": after}, device_id_type=MESH)

    inside = (stage > 0) & (stage < last)

    @pl.when(inside)
    def _():
        pl.semaphore_wait(barrier, 2)

    @pl.when(jnp.logical_not(inside))
    def _():
        pl.semaphore_wait(barrier, 1)

    sums[...] = jnp.zeros_like(sums)
    lane = lax.broadcasted_iota(jnp.int32, (slots, 128), 1)
    first_half = lane < 64

    def stack(v):
        zero = jnp.zeros_like(v)
        return jnp.concatenate([jnp.where(first_half, v, zero), jnp.where(first_half, zero, v)], 0)

    def unstack(v):
        return jnp.where(first_half, v[:slots], v[slots:])

    o_g2, o_s2, o_rb = 0, width, 2 * width
    o_eb = 3 * width
    o_g1 = o_eb + hidden
    o_s1 = o_g1 + width
    o_ob = o_s1 + width
    o_q = o_ob + width
    o_v = o_q + width

    staged_f = ((ctx, ctx_out, ctx_sem), (low, low_out, low_sem), (act, act_out, act_sem))
    staged_b = ((gred, gred_out, gred_sem), (gexp, gexp_out, gexp_sem), (gatt, gatt_out, gatt_sem),
                (gproj, gproj_out, gproj_sem), (gin, gin_out, gin_sem))

    def forward(m):
        slot = lax.rem(m, 2)

        @pl.when(stage == 0)
        def _():
            load_h(m).wait()

        @pl.when(stage > 0)
        def _():
            send_y(m).wait_recv()

        store(h_ref, h_out, hs_sem, m, m).start()

        @pl.when(m >= 2)
        def _():
            for src, dst, sem in staged_f:
                store(src, dst, sem, m - 2, slot).wait()

        h = h_ref[m]
        for c in range(0, 3 * width, 256):
            p = nn(h, aw[:, c:c + 256]) + ab[:, c:c + 256]
            if c < width:
                p = p * 0.125
            qkv[m, :, c:c + 256] = p.astype(bf16)
        for g in range(groups):
            ok = valid[m * groups + g] > 0
            rs = slice(g * slots, (g + 1) * slots)
            for p in range(pairs):
                q = qkv[m, rs, p * 128:(p + 1) * 128]
                k = qkv[m, rs, width + p * 128:width + (p + 1) * 128]
                v = qkv[m, rs, 2 * width + p * 128:2 * width + (p + 1) * 128]
                s = nt(stack(q), k)
                s = jnp.where(ok, s, neg_large)
                e = jnp.exp(s - jnp.max(s, -1, keepdims=True))
                sh = (e * (1.0 / jnp.sum(e, -1, keepdims=True))).astype(bf16)
                shares[m, g * pairs + p] = sh
                ctx[slot, rs, p * 128:(p + 1) * 128] = unstack(nn(sh, v)).astype(bf16)
        store(ctx, ctx_out, ctx_sem, m, slot).start()
        c_all = ctx[slot]
        for c in range(0, width, 256):
            acc[:, c:c + 256] = nn(c_all, ow[:, c:c + 256]) + ob[:, c:c + 256]
        for b in range(0, rows, BLOCK):
            bs = slice(b, b + BLOCK)
            v = acc[bs, :] + h_ref[m, bs, :].astype(f32)
            centre = v - jnp.mean(v, -1, keepdims=True)
            inv = lax.rsqrt(jnp.mean(centre * centre, -1, keepdims=True) + epsilon)
            normed = centre * inv
            out = normed * g1[...] + s1[...]
            n1[m, bs, :] = normed.astype(bf16)
            r1[m, bs, :] = jnp.broadcast_to(inv, (BLOCK, 128))
            mid[bs, :] = out
            low[slot, bs, :] = out.astype(bf16)
        store(low, low_out, low_sem, m, slot).start()
        l_all = low[slot]
        for c in range(0, hidden, CHUNK):
            x = nn(l_all, ew[:, c:c + CHUNK]) + eb[:, c:c + CHUNK]
            a, d = gelu_pair(x)
            act[slot, :, c:c + CHUNK] = a.astype(bf16)
            gp[m, :, c:c + CHUNK] = d.astype(bf16)
        store(act, act_out, act_sem, m, slot).start()
        a_all = act[slot]
        for c in range(0, width, 256):
            acc[:, c:c + 256] = nn(a_all, rw[:, c:c + 256]) + rb[:, c:c + 256]
        for b in range(0, rows, BLOCK):
            bs = slice(b, b + BLOCK)
            v = acc[bs, :] + mid[bs, :]
            centre = v - jnp.mean(v, -1, keepdims=True)
            inv = lax.rsqrt(jnp.mean(centre * centre, -1, keepdims=True) + epsilon)
            normed = centre * inv
            n2[m, bs, :] = normed.astype(bf16)
            r2[m, bs, :] = jnp.broadcast_to(inv, (BLOCK, 128))
            y_ref[m, bs, :] = (normed * g2[...] + s2[...]).astype(bf16)

        @pl.when(stage < last)
        def _():
            send_y(m).start()

        store(y_ref, y_out, y_sem, m, m).start()

    def norm_back(grad, normed, inv, gain):
        scaled = grad * gain
        return inv * (scaled - jnp.mean(scaled, -1, keepdims=True)
                      - normed * jnp.mean(scaled * normed, -1, keepdims=True))

    def backward(m):
        slot = lax.rem(m, 2)

        @pl.when(stage == last)
        def _():
            load_g(m).wait()

        @pl.when(stage < last)
        def _():
            send_g(m).wait_recv()

        @pl.when(m >= 2)
        def _():
            for src, dst, sem in staged_b:
                store(src, dst, sem, m - 2, slot).wait()

        for b in range(0, rows, BLOCK):
            bs = slice(b, b + BLOCK)
            go = g_ref[m, bs, :].astype(f32)
            normed = n2[m, bs, :].astype(f32)
            mix = norm_back(go, normed, r2[m, bs, 0:1], g2[...])
            mid[bs, :] = mix
            gred[slot, bs, :] = mix.astype(bf16)
            sums[:, o_g2:o_g2 + width] += fold(go * normed)
            sums[:, o_s2:o_s2 + width] += fold(go)
            sums[:, o_rb:o_rb + width] += fold(mix)
        store(gred, gred_out, gred_sem, m, slot).start()
        r_all = gred[slot]
        for c in range(0, hidden, CHUNK):
            ge = nt(r_all, rw[c:c + CHUNK, :]) * gp[m, :, c:c + CHUNK].astype(f32)
            gexp[slot, :, c:c + CHUNK] = ge.astype(bf16)
            sums[:, o_eb + c:o_eb + c + CHUNK] += fold(ge)
        store(gexp, gexp_out, gexp_sem, m, slot).start()
        e_all = gexp[slot]
        for c in range(0, width, 256):
            acc[:, c:c + 256] = nt(e_all, ew[c:c + 256, :])
        for b in range(0, rows, BLOCK):
            bs = slice(b, b + BLOCK)
            gf = acc[bs, :] + mid[bs, :]
            normed = n1[m, bs, :].astype(f32)
            gm = norm_back(gf, normed, r1[m, bs, 0:1], g1[...])
            mid[bs, :] = gm
            gatt[slot, bs, :] = gm.astype(bf16)
            sums[:, o_g1:o_g1 + width] += fold(gf * normed)
            sums[:, o_s1:o_s1 + width] += fold(gf)
            sums[:, o_ob:o_ob + width] += fold(gm)
        store(gatt, gatt_out, gatt_sem, m, slot).start()
        t_all = gatt[slot]
        for c in range(0, width, 256):
            gc_all = nt(t_all, ow[c:c + 256, :]).astype(bf16)
            for g in range(groups):
                rs = slice(g * slots, (g + 1) * slots)
                for half in range(2):
                    p = c // 128 + half
                    q = qkv[m, rs, p * 128:(p + 1) * 128]
                    k = qkv[m, rs, width + p * 128:width + (p + 1) * 128]
                    v = qkv[m, rs, 2 * width + p * 128:2 * width + (p + 1) * 128]
                    shb = shares[m, g * pairs + p]
                    sh = shb.astype(f32)
                    gc2 = stack(gc_all[rs, half * 128:(half + 1) * 128])
                    gs = nt(gc2, v)
                    gv = tn(shb, gc2)
                    gsc = (sh * (gs - jnp.sum(gs * sh, -1, keepdims=True))).astype(bf16)
                    gq = unstack(nn(gsc, k)) * 0.125
                    gk = tn(gsc, stack(q))
                    gproj[slot, rs, p * 128:(p + 1) * 128] = gq.astype(bf16)
                    gproj[slot, rs, width + p * 128:width + (p + 1) * 128] = gk.astype(bf16)
                    gproj[slot, rs, 2 * width + p * 128:2 * width + (p + 1) * 128] = gv.astype(bf16)
                    sums[:, o_q + p * 128:o_q + (p + 1) * 128] += fold(gq)
                    sums[:, o_v + p * 128:o_v + (p + 1) * 128] += fold(gv)
        store(gproj, gproj_out, gproj_sem, m, slot).start()
        p_all = gproj[slot]
        for c in range(0, width, 256):
            gi = nt(p_all, aw[c:c + 256, :]) + mid[:, c:c + 256]
            gin[slot, :, c:c + 256] = gi
            gb_ref[m, :, c:c + 256] = gi.astype(bf16)

        @pl.when(stage > 0)
        def _():
            send_g(m).start()

        store(gin, gin_out, gin_sem, m, slot).start()

    def tick(i, carry):
        @pl.when(i < micro)
        def _():
            forward(i)

        j = i - (last - stage)

        @pl.when((j >= 0) & (j < micro))
        def _():
            backward(j)

        return carry

    lax.fori_loop(0, micro + last, tick, 0)

    for m in range(micro):
        store(h_ref, h_out, hs_sem, m, m).wait()
        store(y_ref, y_out, y_sem, m, m).wait()

        @pl.when(stage < last)
        def _():
            send_y(m).wait_send()

        @pl.when(stage > 0)
        def _():
            send_g(m).wait_send()

    for m in range(max(0, micro - 2), micro):
        for src, dst, sem in staged_f + staged_b:
            store(src, dst, sem, m, m % 2).wait()


def run_pipeline(rows_in, tangents, valid, weights, vectors):
    total, width = rows_in.shape
    slots = valid.shape[2]
    rows = GROUP * slots
    micro = total // rows
    aw, ow, ew, rw = weights
    hidden = ew.shape[1]
    pairs = width // 128
    wide = 3 * width
    sum_width = 8 * width + hidden
    hbm = pl.BlockSpec(memory_space=pl.ANY)
    vmem = pl.BlockSpec(memory_space=pltpu.VMEM)
    dma = pltpu.SemaphoreType.DMA
    shape = jax.ShapeDtypeStruct
    flops = 4 * total * (4 * width * width + 2 * width * hidden)
    return pl.pallas_call(
        functools.partial(pipeline_kernel, micro),
        out_shape=(
            shape((total, width), bf16), shape((total, width), f32), shape((total, width), bf16),
            shape((total, width), bf16), shape((total, width), bf16), shape((total, hidden), bf16),
            shape((total, width), bf16), shape((total, hidden), bf16), shape((total, width), bf16),
            shape((total, wide), bf16), shape((8, sum_width), f32),
        ),
        in_specs=[hbm, hbm] + [vmem] * 13,
        out_specs=(hbm,) * 10 + (vmem,),
        scratch_shapes=[
            pltpu.VMEM((micro, rows, width), bf16),
            pltpu.VMEM((micro, rows, width), bf16),
            pltpu.VMEM((micro, rows, width), bf16),
            pltpu.VMEM((micro, rows, width), bf16),
            pltpu.VMEM((micro, rows, wide), bf16),
            pltpu.VMEM((micro, GROUP * pairs, 2 * slots, slots), bf16),
            pltpu.VMEM((micro, rows, hidden), bf16),
            pltpu.VMEM((micro, rows, width), bf16),
            pltpu.VMEM((micro, rows, 128), f32),
            pltpu.VMEM((micro, rows, width), bf16),
            pltpu.VMEM((micro, rows, 128), f32),
            pltpu.VMEM((2, rows, width), bf16),
            pltpu.VMEM((2, rows, width), bf16),
            pltpu.VMEM((2, rows, hidden), bf16),
            pltpu.VMEM((2, rows, width), bf16),
            pltpu.VMEM((2, rows, hidden), bf16),
            pltpu.VMEM((2, rows, width), bf16),
            pltpu.VMEM((2, rows, wide), bf16),
            pltpu.VMEM((2, rows, width), f32),
            pltpu.VMEM((rows, width), f32),
            pltpu.VMEM((rows, width), f32),
        ] + [dma((micro,))] * 8 + [dma((2,))] * 8,
        compiler_params=pltpu.CompilerParams(
            collective_id=0, has_side_effects=True, vmem_limit_bytes=63 * 1024 * 1024),
        cost_estimate=pl.CostEstimate(flops=flops, bytes_accessed=40_000_000, transcendentals=total * hidden),
    )(rows_in, tangents, valid, aw, ow, ew, rw, *vectors)


def outer_sum(left, right):
    return tn(left, right)


def local(
    layer_input, lengths, regions, cotangent,
    attend_weight, attend_bias, output_weight, output_bias, first_gain, first_shift,
    expand_weight, expand_bias, reduce_weight, reduce_bias, second_gain, second_shift,
):
    seqs, slots, width = layer_input.shape
    hidden = expand_weight.shape[2]
    total = seqs * slots
    positions = jnp.arange(slots, dtype=jnp.int32)
    valid = ((positions[None, :] < lengths[:, None]) | (regions == 1)).astype(f32)[:, None, :]
    bias = attend_bias.astype(f32)
    bias = jnp.concatenate([bias[:, :width], jnp.zeros((1, width), f32), bias[:, width:]], 1)
    vectors = (bias,) + tuple(
        v.astype(f32)
        for v in (output_bias, first_gain, first_shift, expand_bias, reduce_bias, second_gain, second_shift)
    )
    weights = (attend_weight[0], output_weight[0], expand_weight[0], reduce_weight[0])
    y, gin, h, ctx, low, act, gred, gexp, gatt, gproj, sums = run_pipeline(
        layer_input.reshape(total, width), cotangent.reshape(total, width), valid, weights, vectors)

    def reduced(v):
        return lax.psum(v.astype(bf16), "dp").astype(f32)

    rw_g = reduced(outer_sum(act, gred))
    ew_g = reduced(outer_sum(low, gexp))
    ow_g = reduced(outer_sum(ctx, gatt))
    aw_g = reduced(outer_sum(h, gproj))
    flat = reduced(jnp.sum(sums, 0))[None]
    at = [0, width, 2 * width, 3 * width, 3 * width + hidden]
    o1 = at[4]
    return (
        y.reshape(1, seqs, slots, width),
        gin.reshape(1, seqs, slots, width),
        aw_g[None],
        flat[:, o1 + 3 * width:],
        ow_g[None],
        flat[:, o1 + 2 * width:o1 + 3 * width],
        flat[:, o1:o1 + width],
        flat[:, o1 + width:o1 + 2 * width],
        ew_g[None],
        flat[:, 3 * width:o1],
        rw_g[None],
        flat[:, 2 * width:3 * width],
        flat[:, :width],
        flat[:, width:2 * width],
    )


def solution(mesh):
    rows = P("dp", None, None)
    cube = P("pipe", None, None)
    flat = P("pipe", None)
    grads = P("pipe", "dp", None, None)
    return jax.shard_map(
        local,
        mesh=mesh,
        in_specs=(rows, P("dp"), P("dp", None), rows, cube, flat, cube, flat, flat, flat, cube, flat, cube, flat, flat, flat),
        out_specs=(grads, grads, cube, flat, cube, flat, flat, flat, cube, flat, cube, flat, flat, flat),
        check_vma=False,
    )
```

```python
import functools

import jax
import jax.numpy as jnp
from jax import lax
from jax.experimental import pallas as pl
from jax.experimental.pallas import tpu as pltpu
from jax.sharding import PartitionSpec as P

HEADS = 12
GROUP = 2
BLOCK = 32
CHUNK = 512
epsilon = 1e-05
neg_large = -1000000000.0
MESH = pl.DeviceIdType.MESH
f32 = jnp.float32
bf16 = jnp.bfloat16


def nn(left, right):
    return jnp.dot(left, right, preferred_element_type=f32)


def nt(left, right):
    return lax.dot_general(left, right, (((1,), (1,)), ((), ())), preferred_element_type=f32)


def tn(left, right):
    return lax.dot_general(left, right, (((0,), (0,)), ((), ())), preferred_element_type=f32)


def gelu_pair(x):
    z = jnp.abs(x) * 0.7071067811865476
    t = 1.0 / (1.0 + 0.3275911 * z)
    e = jnp.exp(-0.5 * (x * x))
    poly = t * (0.127414796 + t * (-0.142248368 + t * (0.7107068705 + t * (-0.7265760135 + t * 0.5307027145))))
    tail = poly * e
    phi = jnp.where(x >= 0, 1.0 - tail, tail)
    return x * phi, phi + (x * 0.3989422804014327) * e


def fold(v):
    rows, cols = v.shape
    return jnp.sum(v.reshape(rows // 8, 8, cols), 0)


def pipeline_kernel(
    micro,
    x_any, ct_any, lengths, regions, aw, ow, ew, rw, ab_in, ob_in, g1_in, s1_in, eb_in, rb_in, g2_in, s2_in,
    y_out, gin_out, h_out, ctx_out, low_out, act_out, gred_out, gexp_out, gatt_out, gproj_out, sums,
    ab, ob, g1, s1, eb, rb, g2, s2,
    h_ref, g_ref, y_ref, gb_ref, qkv, shares, gp, n1, r1, n2, r2,
    ctx, low, act, gred, gexp, gatt, gproj, gin, acc, mid,
    h_sem, g_sem, ysend_sem, yrecv_sem, gsend_sem, grecv_sem, y_sem, hs_sem,
    ctx_sem, low_sem, act_sem, gred_sem, gexp_sem, gatt_sem, gproj_sem, gin_sem,
):
    stage = lax.axis_index("pipe")
    count = lax.axis_size("pipe")
    last = count - 1
    slots = regions.shape[1]
    rows = h_ref.shape[1]
    groups = rows // slots
    width = h_ref.shape[2]
    hidden = ew.shape[1]
    pairs = width // 128
    before = jnp.maximum(stage - 1, 0)
    after = jnp.minimum(stage + 1, last)

    def send_y(m):
        return pltpu.make_async_remote_copy(
            src_ref=y_ref.at[m], dst_ref=h_ref.at[m], send_sem=ysend_sem.at[m], recv_sem=yrecv_sem.at[m],
            device_id={"pipe": after}, device_id_type=MESH)

    def send_g(m):
        return pltpu.make_async_remote_copy(
            src_ref=gb_ref.at[m], dst_ref=g_ref.at[m], send_sem=gsend_sem.at[m], recv_sem=grecv_sem.at[m],
            device_id={"pipe": before}, device_id_type=MESH)

    def load_h(m):
        return pltpu.make_async_copy(x_any.at[pl.ds(m * rows, rows)], h_ref.at[m], h_sem.at[m])

    def load_g(m):
        return pltpu.make_async_copy(ct_any.at[pl.ds(m * rows, rows)], g_ref.at[m], g_sem.at[m])

    def store(src, dst, sem, m, slot):
        return pltpu.make_async_copy(src.at[slot], dst.at[pl.ds(m * rows, rows)], sem.at[slot])

    @pl.when(stage == 0)
    def _():
        for m in range(micro):
            load_h(m).start()

    @pl.when(stage == last)
    def _():
        for m in range(micro):
            load_g(m).start()

    barrier = pltpu.get_barrier_semaphore()

    @pl.when(stage > 0)
    def _():
        pl.semaphore_signal(barrier, inc=1, device_id={"pipe": before}, device_id_type=MESH)

    @pl.when(stage < last)
    def _():
        pl.semaphore_signal(barrier, inc=1, device_id={"pipe": after}, device_id_type=MESH)

    inside = (stage > 0) & (stage < last)

    @pl.when(inside)
    def _():
        pl.semaphore_wait(barrier, 2)

    @pl.when(jnp.logical_not(inside))
    def _():
        pl.semaphore_wait(barrier, 1)

    sums[...] = jnp.zeros_like(sums)
    ab[:, :width] = ab_in[:, :width].astype(f32)
    ab[:, width:2 * width] = jnp.zeros((1, width), f32)
    ab[:, 2 * width:] = ab_in[:, width:].astype(f32)
    for dst, src in ((ob, ob_in), (g1, g1_in), (s1, s1_in), (eb, eb_in), (rb, rb_in), (g2, g2_in), (s2, s2_in)):
        dst[...] = src[...].astype(f32)
    position = lax.broadcasted_iota(jnp.int32, (1, slots), 1)
    lane = lax.broadcasted_iota(jnp.int32, (slots, 128), 1)
    first_half = lane < 64

    def stack(v):
        zero = jnp.zeros_like(v)
        return jnp.concatenate([jnp.where(first_half, v, zero), jnp.where(first_half, zero, v)], 0)

    def unstack(v):
        return jnp.where(first_half, v[:slots], v[slots:])

    o_g2, o_s2, o_rb = 0, width, 2 * width
    o_eb = 3 * width
    o_g1 = o_eb + hidden
    o_s1 = o_g1 + width
    o_ob = o_s1 + width
    o_q = o_ob + width
    o_v = o_q + width

    staged_f = ((ctx, ctx_out, ctx_sem), (low, low_out, low_sem), (act, act_out, act_sem))
    staged_b = ((gred, gred_out, gred_sem), (gexp, gexp_out, gexp_sem), (gatt, gatt_out, gatt_sem),
                (gproj, gproj_out, gproj_sem), (gin, gin_out, gin_sem))

    def forward(m):
        slot = lax.rem(m, 2)

        @pl.when(stage == 0)
        def _():
            load_h(m).wait()

        @pl.when(stage > 0)
        def _():
            send_y(m).wait_recv()

        store(h_ref, h_out, hs_sem, m, m).start()

        @pl.when(m >= 2)
        def _():
            for src, dst, sem in staged_f:
                store(src, dst, sem, m - 2, slot).wait()

        h = h_ref[m]
        for c in range(0, 3 * width, 256):
            p = nn(h, aw[:, c:c + 256]) + ab[:, c:c + 256]
            if c < width:
                p = p * 0.125
            qkv[m, :, c:c + 256] = p.astype(bf16)
        for g in range(groups):
            seq = m * groups + g
            ok = (position < lengths[seq]) | (regions[pl.ds(seq, 1), :] == 1)
            rs = slice(g * slots, (g + 1) * slots)
            for p in range(pairs):
                q = qkv[m, rs, p * 128:(p + 1) * 128]
                k = qkv[m, rs, width + p * 128:width + (p + 1) * 128]
                v = qkv[m, rs, 2 * width + p * 128:2 * width + (p + 1) * 128]
                s = nt(stack(q), k)
                s = jnp.where(ok, s, neg_large)
                e = jnp.exp(s - jnp.max(s, -1, keepdims=True))
                sh = (e * (1.0 / jnp.sum(e, -1, keepdims=True))).astype(bf16)
                shares[m, g * pairs + p] = sh
                ctx[slot, rs, p * 128:(p + 1) * 128] = unstack(nn(sh, v)).astype(bf16)
        store(ctx, ctx_out, ctx_sem, m, slot).start()
        c_all = ctx[slot]
        for c in range(0, width, 256):
            acc[:, c:c + 256] = nn(c_all, ow[:, c:c + 256]) + ob[:, c:c + 256]
        for b in range(0, rows, BLOCK):
            bs = slice(b, b + BLOCK)
            v = acc[bs, :] + h_ref[m, bs, :].astype(f32)
            centre = v - jnp.mean(v, -1, keepdims=True)
            inv = lax.rsqrt(jnp.mean(centre * centre, -1, keepdims=True) + epsilon)
            normed = centre * inv
            out = normed * g1[...] + s1[...]
            n1[m, bs, :] = normed.astype(bf16)
            r1[m, bs, :] = jnp.broadcast_to(inv, (BLOCK, 128))
            mid[bs, :] = out
            low[slot, bs, :] = out.astype(bf16)
        store(low, low_out, low_sem, m, slot).start()
        l_all = low[slot]
        for c in range(0, hidden, CHUNK):
            x = nn(l_all, ew[:, c:c + CHUNK]) + eb[:, c:c + CHUNK]
            a, d = gelu_pair(x)
            act[slot, :, c:c + CHUNK] = a.astype(bf16)
            gp[m, :, c:c + CHUNK] = d.astype(bf16)
        store(act, act_out, act_sem, m, slot).start()
        a_all = act[slot]
        for c in range(0, width, 256):
            acc[:, c:c + 256] = nn(a_all, rw[:, c:c + 256]) + rb[:, c:c + 256]
        for b in range(0, rows, BLOCK):
            bs = slice(b, b + BLOCK)
            v = acc[bs, :] + mid[bs, :]
            centre = v - jnp.mean(v, -1, keepdims=True)
            inv = lax.rsqrt(jnp.mean(centre * centre, -1, keepdims=True) + epsilon)
            normed = centre * inv
            n2[m, bs, :] = normed.astype(bf16)
            r2[m, bs, :] = jnp.broadcast_to(inv, (BLOCK, 128))
            y_ref[m, bs, :] = (normed * g2[...] + s2[...]).astype(bf16)

        @pl.when(stage < last)
        def _():
            send_y(m).start()

        store(y_ref, y_out, y_sem, m, m).start()

    def norm_back(grad, normed, inv, gain):
        scaled = grad * gain
        return inv * (scaled - jnp.mean(scaled, -1, keepdims=True)
                      - normed * jnp.mean(scaled * normed, -1, keepdims=True))

    def backward(m):
        slot = lax.rem(m, 2)

        @pl.when(stage == last)
        def _():
            load_g(m).wait()

        @pl.when(stage < last)
        def _():
            send_g(m).wait_recv()

        @pl.when(m >= 2)
        def _():
            for src, dst, sem in staged_b:
                store(src, dst, sem, m - 2, slot).wait()

        for b in range(0, rows, BLOCK):
            bs = slice(b, b + BLOCK)
            go = g_ref[m, bs, :].astype(f32)
            normed = n2[m, bs, :].astype(f32)
            mix = norm_back(go, normed, r2[m, bs, 0:1], g2[...])
            mid[bs, :] = mix
            gred[slot, bs, :] = mix.astype(bf16)
            sums[:, o_g2:o_g2 + width] += fold(go * normed)
            sums[:, o_s2:o_s2 + width] += fold(go)
            sums[:, o_rb:o_rb + width] += fold(mix)
        store(gred, gred_out, gred_sem, m, slot).start()
        r_all = gred[slot]
        for c in range(0, hidden, CHUNK):
            ge = nt(r_all, rw[c:c + CHUNK, :]) * gp[m, :, c:c + CHUNK].astype(f32)
            gexp[slot, :, c:c + CHUNK] = ge.astype(bf16)
            sums[:, o_eb + c:o_eb + c + CHUNK] += fold(ge)
        store(gexp, gexp_out, gexp_sem, m, slot).start()
        e_all = gexp[slot]
        for c in range(0, width, 256):
            acc[:, c:c + 256] = nt(e_all, ew[c:c + 256, :])
        for b in range(0, rows, BLOCK):
            bs = slice(b, b + BLOCK)
            gf = acc[bs, :] + mid[bs, :]
            normed = n1[m, bs, :].astype(f32)
            gm = norm_back(gf, normed, r1[m, bs, 0:1], g1[...])
            mid[bs, :] = gm
            gatt[slot, bs, :] = gm.astype(bf16)
            sums[:, o_g1:o_g1 + width] += fold(gf * normed)
            sums[:, o_s1:o_s1 + width] += fold(gf)
            sums[:, o_ob:o_ob + width] += fold(gm)
        store(gatt, gatt_out, gatt_sem, m, slot).start()
        t_all = gatt[slot]
        for c in range(0, width, 256):
            gc_all = nt(t_all, ow[c:c + 256, :]).astype(bf16)
            for g in range(groups):
                rs = slice(g * slots, (g + 1) * slots)
                for half in range(2):
                    p = c // 128 + half
                    q = qkv[m, rs, p * 128:(p + 1) * 128]
                    k = qkv[m, rs, width + p * 128:width + (p + 1) * 128]
                    v = qkv[m, rs, 2 * width + p * 128:2 * width + (p + 1) * 128]
                    shb = shares[m, g * pairs + p]
                    sh = shb.astype(f32)
                    gc2 = stack(gc_all[rs, half * 128:(half + 1) * 128])
                    gs = nt(gc2, v)
                    gv = tn(shb, gc2)
                    gsc = (sh * (gs - jnp.sum(gs * sh, -1, keepdims=True))).astype(bf16)
                    gq = unstack(nn(gsc, k)) * 0.125
                    gk = tn(gsc, stack(q))
                    gproj[slot, rs, p * 128:(p + 1) * 128] = gq.astype(bf16)
                    gproj[slot, rs, width + p * 128:width + (p + 1) * 128] = gk.astype(bf16)
                    gproj[slot, rs, 2 * width + p * 128:2 * width + (p + 1) * 128] = gv.astype(bf16)
                    sums[:, o_q + p * 128:o_q + (p + 1) * 128] += fold(gq)
                    sums[:, o_v + p * 128:o_v + (p + 1) * 128] += fold(gv)
        store(gproj, gproj_out, gproj_sem, m, slot).start()
        p_all = gproj[slot]
        for c in range(0, width, 256):
            gi = nt(p_all, aw[c:c + 256, :]) + mid[:, c:c + 256]
            gin[slot, :, c:c + 256] = gi
            gb_ref[m, :, c:c + 256] = gi.astype(bf16)

        @pl.when(stage > 0)
        def _():
            send_g(m).start()

        store(gin, gin_out, gin_sem, m, slot).start()

    def tick(i, carry):
        @pl.when(i < micro)
        def _():
            forward(i)

        j = i - (last - stage)

        @pl.when((j >= 0) & (j < micro))
        def _():
            backward(j)

        return carry

    lax.fori_loop(0, micro + last, tick, 0)

    for m in range(micro):
        store(h_ref, h_out, hs_sem, m, m).wait()
        store(y_ref, y_out, y_sem, m, m).wait()

        @pl.when(stage < last)
        def _():
            send_y(m).wait_send()

        @pl.when(stage > 0)
        def _():
            send_g(m).wait_send()

    for m in range(max(0, micro - 2), micro):
        for src, dst, sem in staged_f + staged_b:
            store(src, dst, sem, m, m % 2).wait()


def run_pipeline(rows_in, tangents, lengths, regions, weights, vectors):
    total, width = rows_in.shape
    slots = regions.shape[1]
    rows = GROUP * slots
    micro = total // rows
    aw, ow, ew, rw = weights
    hidden = ew.shape[1]
    pairs = width // 128
    wide = 3 * width
    sum_width = 8 * width + hidden
    hbm = pl.BlockSpec(memory_space=pl.ANY)
    vmem = pl.BlockSpec(memory_space=pltpu.VMEM)
    dma = pltpu.SemaphoreType.DMA
    shape = jax.ShapeDtypeStruct
    flops = 4 * total * (4 * width * width + 2 * width * hidden)
    return pl.pallas_call(
        functools.partial(pipeline_kernel, micro),
        out_shape=(
            shape((total, width), bf16), shape((total, width), f32), shape((total, width), bf16),
            shape((total, width), bf16), shape((total, width), bf16), shape((total, hidden), bf16),
            shape((total, width), bf16), shape((total, hidden), bf16), shape((total, width), bf16),
            shape((total, wide), bf16), shape((8, sum_width), f32),
        ),
        in_specs=[hbm, hbm, pl.BlockSpec(memory_space=pltpu.SMEM)] + [vmem] * 13,
        out_specs=(hbm,) * 10 + (vmem,),
        scratch_shapes=[pltpu.VMEM((1, n), f32) for n in (wide, width, width, width, hidden, width, width, width)] + [
            pltpu.VMEM((micro, rows, width), bf16),
            pltpu.VMEM((micro, rows, width), bf16),
            pltpu.VMEM((micro, rows, width), bf16),
            pltpu.VMEM((micro, rows, width), bf16),
            pltpu.VMEM((micro, rows, wide), bf16),
            pltpu.VMEM((micro, GROUP * pairs, 2 * slots, slots), bf16),
            pltpu.VMEM((micro, rows, hidden), bf16),
            pltpu.VMEM((micro, rows, width), bf16),
            pltpu.VMEM((micro, rows, 128), f32),
            pltpu.VMEM((micro, rows, width), bf16),
            pltpu.VMEM((micro, rows, 128), f32),
            pltpu.VMEM((2, rows, width), bf16),
            pltpu.VMEM((2, rows, width), bf16),
            pltpu.VMEM((2, rows, hidden), bf16),
            pltpu.VMEM((2, rows, width), bf16),
            pltpu.VMEM((2, rows, hidden), bf16),
            pltpu.VMEM((2, rows, width), bf16),
            pltpu.VMEM((2, rows, wide), bf16),
            pltpu.VMEM((2, rows, width), f32),
            pltpu.VMEM((rows, width), f32),
            pltpu.VMEM((rows, width), f32),
        ] + [dma((micro,))] * 8 + [dma((2,))] * 8,
        compiler_params=pltpu.CompilerParams(
            collective_id=0, has_side_effects=True, vmem_limit_bytes=63 * 1024 * 1024),
        cost_estimate=pl.CostEstimate(flops=flops, bytes_accessed=40_000_000, transcendentals=total * hidden),
    )(rows_in, tangents, lengths, regions, aw, ow, ew, rw, *vectors)


def sum_kernel(
    dp, act_any, gred_any, low_any, gexp_any, h_any, gproj_any, ctx_any, gatt_any, sums_in,
    total, vector,
    part, left, right, vec_in, *rest,
):
    steps = dp.bit_length() - 1
    plane = steps - 1
    landed = rest[:steps]
    left_sem, right_sem, send_sem, recv_sem, vsend_sem, vrecv_sem = rest[steps:]
    units, rows, cols = part.shape
    me = lax.axis_index("dp")
    hid_blocks = act_any.shape[1] // cols
    wide_blocks = gproj_any.shape[1] // cols
    sources = (
        [(act_any, k, gred_any, 0) for k in range(hid_blocks)]
        + [(low_any, 0, gexp_any, k) for k in range(hid_blocks)]
        + [(h_any, 0, gproj_any, k) for k in range(wide_blocks)]
        + [(ctx_any, 0, gatt_any, 0)]
    )

    def bit_of(mask):
        return lax.rem(me // mask, 2)

    def masks_of(step):
        if step == 0:
            return 1, 1
        return 2 ** (1 + (step - 1) % plane), 2 ** (1 + (step - 1 + plane // 2) % plane)

    def place(unit, step):
        parity = lax.rem(unit, 2)
        first, second = masks_of(step)
        mask = first + parity * (second - first)
        bit = bit_of(first) + parity * (bit_of(second) - bit_of(first))
        return bit, me + mask * (1 - 2 * bit)

    def base(unit, step):
        start, size = 0, rows
        for k in range(step):
            size = size // 2
            start = start + place(unit, k)[0] * size
        return start, size

    def ds(start, size):
        return pl.ds(pl.multiple_of(start, 16), size)

    def reduce_copy(unit, step):
        bit, peer = place(unit, step)
        start, size = base(unit, step)
        half = size // 2
        return pltpu.make_async_remote_copy(
            src_ref=part.at[unit, ds(start + (1 - bit) * half, half)], dst_ref=landed[step].at[unit],
            send_sem=send_sem.at[step, unit], recv_sem=recv_sem.at[step, unit],
            device_id={"dp": peer}, device_id_type=MESH)

    def gather_copy(unit, step):
        peer = place(unit, step)[1]
        start, size = base(unit, step + 1)
        where = 2 * steps - 1 - step
        return pltpu.make_async_remote_copy(
            src_ref=total.at[unit, ds(start, size)], dst_ref=total.at[unit, ds(start, size)],
            send_sem=send_sem.at[where, unit], recv_sem=recv_sem.at[where, unit],
            device_id={"dp": peer}, device_id_type=MESH)

    def gather_arrival(unit, step):
        bit, peer = place(unit, step)
        start, size = base(unit, step)
        half = size // 2
        where = 2 * steps - 1 - step
        there = ds(start + (1 - bit) * half, half)
        return pltpu.make_async_remote_copy(
            src_ref=total.at[unit, there], dst_ref=total.at[unit, there],
            send_sem=send_sem.at[where, unit], recv_sem=recv_sem.at[where, unit],
            device_id={"dp": peer}, device_id_type=MESH)

    def vector_copy(step):
        peer = me + 2 ** step * (1 - 2 * bit_of(2 ** step))
        return pltpu.make_async_remote_copy(
            src_ref=vec_in.at[2 * step], dst_ref=vec_in.at[2 * step + 1],
            send_sem=vsend_sem.at[step], recv_sem=vrecv_sem.at[step],
            device_id={"dp": peer}, device_id_type=MESH)

    def loads(k, slot):
        a, ka, b, kb = sources[k]
        return (
            pltpu.make_async_copy(a.at[:, pl.ds(ka * cols, cols)], left.at[slot], left_sem.at[slot]),
            pltpu.make_async_copy(b.at[:, pl.ds(kb * cols, cols)], right.at[slot], right_sem.at[slot]),
        )

    for copy in loads(0, 0):
        copy.start()
    barrier = pltpu.get_barrier_semaphore()
    for step in range(steps):
        peer = me + 2 ** step * (1 - 2 * bit_of(2 ** step))
        pl.semaphore_signal(barrier, inc=1, device_id={"dp": peer}, device_id_type=MESH)
    v = jnp.sum(sums_in[...], 0, keepdims=True)
    lanes = vec_in.shape[2]
    for r in range(8):
        vec_in[0, r:r + 1, :] = v[:, r * lanes:(r + 1) * lanes]
    pl.semaphore_wait(barrier, steps)

    def add(unit, step):
        start, size = base(unit, step + 1)
        for b in range(0, size, 96):
            n = min(96, size - b)
            rs = ds(start + b, n)
            s = part[unit, rs, :].astype(f32) + landed[step][unit, b:b + n, :].astype(f32)
            if step == steps - 1:
                total[unit, rs, :] = s.astype(bf16)
            else:
                part[unit, rs, :] = s.astype(bf16)

    def when_unit(unit, body):
        @pl.when((unit >= 0) & (unit < units))
        def _():
            body(unit)

    def make(unit):
        for s in range(rows // cols):
            block = unit * (rows // cols) + s
            slot = lax.rem(block, 2)
            for k in range(len(sources)):
                @pl.when(block == k)
                def _():
                    if k + 1 < len(sources):
                        for copy in loads(k + 1, (k + 1) % 2):
                            copy.start()
                    for copy in loads(k, k % 2):
                        copy.wait()
            for r in range(0, cols, 256):
                part[unit, s * cols + r:s * cols + r + 256, :] = tn(left[slot, :, r:r + 256], right[slot]).astype(bf16)
        reduce_copy(unit, 0).start()

    def reduce_next(step):
        def body(unit):
            reduce_copy(unit, step).wait_recv()
            add(unit, step)
            if step + 1 < steps:
                reduce_copy(unit, step + 1).start()
            else:
                gather_copy(unit, step).start()
        return body

    def gather_next(step):
        def body(unit):
            gather_arrival(unit, step).wait_recv()
            if step > 0:
                gather_copy(unit, step - 1).start()
        return body

    lag = 0
    lags = []
    for step in range(steps):
        lag += 1 if step == 0 else 2
        lags.append((lag, reduce_next(step)))
    for step in reversed(range(steps)):
        lag += 2
        lags.append((lag, gather_next(step)))

    def tick(t, carry):
        when_unit(t, make)
        for behind, body in lags:
            when_unit(t - behind, body)
        for step in range(steps):
            @pl.when(t == 2 + 2 * step)
            def _():
                if step > 0:
                    vector_copy(step - 1).wait_recv()
                    vec_in[2 * step] = vec_in[2 * step - 2] + vec_in[2 * step - 1]
                vector_copy(step).start()

        return carry

    lax.fori_loop(0, units + lag, tick, 0)
    vector_copy(steps - 1).wait_recv()
    vector[...] = vec_in[2 * steps - 2] + vec_in[2 * steps - 1]

    def finish(unit, carry):
        for step in range(steps):
            reduce_copy(unit, step).wait_send()
            gather_copy(unit, step).wait_send()
        return carry

    lax.fori_loop(0, units, finish, 0)
    for step in range(steps):
        vector_copy(step).wait_send()


def write_kernel(hid_blocks, wide_blocks, total, vector, aw_g, ab_g, ow_g, ob_g, g1_g, s1_g, ew_g, eb_g, rw_g, rb_g, g2_g, s2_g):
    t = pl.program_id(0)
    first, second = hid_blocks, 2 * hid_blocks
    third = second + wide_blocks

    @pl.when(t == 0)
    def _():
        piece = vector.shape[1] // 3
        at = 0
        for out in (g2_g, s2_g, rb_g, eb_g, g1_g, s1_g, ob_g, ab_g):
            for k in range(out.shape[1] // piece):
                r, c = at // 3, at % 3
                out[:, k * piece:(k + 1) * piece] = vector[r:r + 1, c * piece:(c + 1) * piece]
                at += 1

    @pl.when(t < first)
    def _():
        rw_g[...] = total[...].astype(f32)

    @pl.when((t >= first) & (t < second))
    def _():
        ew_g[...] = total[...].astype(f32)

    @pl.when((t >= second) & (t < third))
    def _():
        aw_g[...] = total[...].astype(f32)

    @pl.when(t >= third)
    def _():
        ow_g[...] = total[...].astype(f32)


def run_sums(parts, sums, dp):
    act, gred, low, gexp, h, gproj, ctx, gatt = parts
    total_rows, width = h.shape
    hidden, wide = act.shape[1], gproj.shape[1]
    hid_blocks, wide_blocks = hidden // width, wide // width
    blocks = 2 * hid_blocks + wide_blocks + 1
    steps = dp.bit_length() - 1
    span = 1
    while span * width % (16 * dp):
        span *= 2
    units, unit_rows = blocks // span, span * width
    lanes = sums.shape[1] // 8
    hbm = pl.BlockSpec(memory_space=pl.ANY)
    vmem = pl.BlockSpec(memory_space=pltpu.VMEM)
    dma = pltpu.SemaphoreType.DMA
    shape = jax.ShapeDtypeStruct
    total, vector = pl.pallas_call(
        functools.partial(sum_kernel, dp),
        out_shape=(shape((units, unit_rows, width), bf16), shape((8, lanes), f32)),
        in_specs=[hbm] * 8 + [vmem],
        out_specs=(vmem, vmem),
        scratch_shapes=[
            pltpu.VMEM((units, unit_rows, width), bf16),
            pltpu.VMEM((2, total_rows, width), bf16),
            pltpu.VMEM((2, total_rows, width), bf16),
            pltpu.VMEM((2 * steps, 8, lanes), f32),
        ] + [pltpu.VMEM((units, unit_rows // 2 ** (k + 1), width), bf16) for k in range(steps)] + [
            dma((2,)), dma((2,)), dma((2 * steps, units)), dma((2 * steps, units)), dma((steps,)), dma((steps,)),
        ],
        compiler_params=pltpu.CompilerParams(
            collective_id=1, has_side_effects=True, vmem_limit_bytes=63 * 1024 * 1024),
    )(act, gred, low, gexp, h, gproj, ctx, gatt, sums)

    def one(count):
        return shape((1, count), f32), pl.BlockSpec((1, count), lambda t: (0, 0))

    a, b = hid_blocks, 2 * hid_blocks
    outs = [
        (shape((width, wide), f32), pl.BlockSpec((width, width), lambda t: (0, jnp.clip(t - b, 0, wide_blocks - 1)))),
        one(2 * width),
        (shape((width, width), f32), pl.BlockSpec((width, width), lambda t: (0, 0))),
        one(width), one(width), one(width),
        (shape((width, hidden), f32), pl.BlockSpec((width, width), lambda t: (0, jnp.clip(t - a, 0, hid_blocks - 1)))),
        one(hidden),
        (shape((hidden, width), f32), pl.BlockSpec((width, width), lambda t: (jnp.clip(t, 0, hid_blocks - 1), 0))),
        one(width), one(width), one(width),
    ]
    return pl.pallas_call(
        functools.partial(write_kernel, hid_blocks, wide_blocks),
        grid=(blocks,),
        out_shape=tuple(o[0] for o in outs),
        in_specs=[pl.BlockSpec((None, width, width), lambda t: (t, 0, 0)), pl.BlockSpec((8, lanes), lambda t: (0, 0))],
        out_specs=tuple(o[1] for o in outs),
        compiler_params=pltpu.CompilerParams(vmem_limit_bytes=60 * 1024 * 1024),
    )(total.reshape(blocks, width, width), vector)


def local(
    layer_input, lengths, regions, cotangent,
    attend_weight, attend_bias, output_weight, output_bias, first_gain, first_shift,
    expand_weight, expand_bias, reduce_weight, reduce_bias, second_gain, second_shift,
):
    seqs, slots, width = layer_input.shape
    total = seqs * slots
    vectors = (attend_bias, output_bias, first_gain, first_shift, expand_bias, reduce_bias, second_gain, second_shift)
    weights = (attend_weight[0], output_weight[0], expand_weight[0], reduce_weight[0])
    y, gin, h, ctx, low, act, gred, gexp, gatt, gproj, sums = run_pipeline(
        layer_input.reshape(total, width), cotangent.reshape(total, width), lengths, regions, weights, vectors)
    grads = run_sums((act, gred, low, gexp, h, gproj, ctx, gatt), sums, lax.axis_size("dp"))
    return (y.reshape(1, seqs, slots, width), gin.reshape(1, seqs, slots, width)) + tuple(
        g[None] if g.shape[0] > 1 else g for g in grads)


def solution(mesh):
    rows = P("dp", None, None)
    cube = P("pipe", None, None)
    flat = P("pipe", None)
    grads = P("pipe", "dp", None, None)
    return jax.shard_map(
        local,
        mesh=mesh,
        in_specs=(rows, P("dp"), P("dp", None), rows, cube, flat, cube, flat, flat, flat, cube, flat, cube, flat, flat, flat),
        out_specs=(grads, grads, cube, flat, cube, flat, flat, flat, cube, flat, cube, flat, flat, flat),
        check_vma=False,
    )
```

```python
import functools

import jax
import jax.numpy as jnp
from jax import lax
from jax.experimental import pallas as pl
from jax.experimental.pallas import tpu as pltpu
from jax.sharding import PartitionSpec as P

HEADS = 12
GROUP = 2
BLOCK = 32
CHUNK = 512
epsilon = 1e-05
neg_large = -1000000000.0
MESH = pl.DeviceIdType.MESH
f32 = jnp.float32
bf16 = jnp.bfloat16


def nn(left, right):
    return jnp.dot(left, right, preferred_element_type=f32)


def nt(left, right):
    return lax.dot_general(left, right, (((1,), (1,)), ((), ())), preferred_element_type=f32)


def tn(left, right):
    return lax.dot_general(left, right, (((0,), (0,)), ((), ())), preferred_element_type=f32)


def gelu_pair(x):
    phi = 0.5 + 0.5 * lax.erf(x * 0.7071067811865476)
    return x * phi, phi + (x * 0.3989422804014327) * jnp.exp2((x * x) * -0.7213475204444817)


def fold(v):
    rows, cols = v.shape
    return jnp.sum(v.reshape(rows // 8, 8, cols), 0)


def pipeline_kernel(
    micro,
    x_any, ct_any, lengths, regions, aw, ow, ew, rw, ab_in, ob_in, g1_in, s1_in, eb_in, rb_in, g2_in, s2_in,
    y_out, gin_out, h_out, ctx_out, low_out, act_out, gred_out, gexp_out, gatt_out, gproj_out, sums,
    usable, gctx, ab, ob, g1, s1, eb, rb, g2, s2,
    h_ref, g_ref, y_ref, gb_ref, qkv, shares, gp, n1, r1, n2, r2,
    ctx, low, act, gred, gexp, gatt, gproj, gin, acc, mid,
    h_sem, g_sem, ysend_sem, yrecv_sem, gsend_sem, grecv_sem, y_sem, hs_sem,
    ctx_sem, low_sem, act_sem, gred_sem, gexp_sem, gatt_sem, gproj_sem, gin_sem,
):
    stage = lax.axis_index("pipe")
    count = lax.axis_size("pipe")
    last = count - 1
    slots = regions.shape[1]
    rows = h_ref.shape[1]
    groups = rows // slots
    width = h_ref.shape[2]
    hidden = ew.shape[1]
    pairs = width // 128
    before = jnp.maximum(stage - 1, 0)
    after = jnp.minimum(stage + 1, last)

    def send_y(m):
        return pltpu.make_async_remote_copy(
            src_ref=y_ref.at[m], dst_ref=h_ref.at[m], send_sem=ysend_sem.at[m], recv_sem=yrecv_sem.at[m],
            device_id={"pipe": after}, device_id_type=MESH)

    def send_g(m):
        return pltpu.make_async_remote_copy(
            src_ref=gb_ref.at[m], dst_ref=g_ref.at[m], send_sem=gsend_sem.at[m], recv_sem=grecv_sem.at[m],
            device_id={"pipe": before}, device_id_type=MESH)

    def load_h(m):
        return pltpu.make_async_copy(x_any.at[pl.ds(m * rows, rows)], h_ref.at[m], h_sem.at[m])

    def load_g(m):
        return pltpu.make_async_copy(ct_any.at[pl.ds(m * rows, rows)], g_ref.at[m], g_sem.at[m])

    def store(src, dst, sem, m, slot):
        return pltpu.make_async_copy(src.at[slot], dst.at[pl.ds(m * rows, rows)], sem.at[slot])

    @pl.when(stage == 0)
    def _():
        for m in range(micro):
            load_h(m).start()

    @pl.when(stage == last)
    def _():
        for m in range(micro):
            load_g(m).start()

    barrier = pltpu.get_barrier_semaphore()

    @pl.when(stage > 0)
    def _():
        pl.semaphore_signal(barrier, inc=1, device_id={"pipe": before}, device_id_type=MESH)

    @pl.when(stage < last)
    def _():
        pl.semaphore_signal(barrier, inc=1, device_id={"pipe": after}, device_id_type=MESH)

    inside = (stage > 0) & (stage < last)

    @pl.when(inside)
    def _():
        pl.semaphore_wait(barrier, 2)

    @pl.when(jnp.logical_not(inside))
    def _():
        pl.semaphore_wait(barrier, 1)

    sums[...] = jnp.zeros_like(sums)
    ab[:, :width] = ab_in[:, :width].astype(f32)
    ab[:, width:2 * width] = jnp.zeros((1, width), f32)
    ab[:, 2 * width:] = ab_in[:, width:].astype(f32)
    for dst, src in ((ob, ob_in), (g1, g1_in), (s1, s1_in), (eb, eb_in), (rb, rb_in), (g2, g2_in), (s2, s2_in)):
        dst[...] = src[...].astype(f32)
    position = lax.broadcasted_iota(jnp.int32, (1, slots), 1)
    for seq in range(regions.shape[0]):
        known = (position < lengths[seq]) | (regions[seq:seq + 1, :] == 1)
        usable[seq] = jnp.broadcast_to(known.astype(f32), (8, slots))
    lane = lax.broadcasted_iota(jnp.int32, (slots, 128), 1)
    first_half = lane < 64

    def stack(v):
        zero = jnp.zeros_like(v)
        return jnp.concatenate([jnp.where(first_half, v, zero), jnp.where(first_half, zero, v)], 0)

    def unstack(v):
        return jnp.where(first_half, v[:slots], v[slots:])

    o_g2, o_s2, o_rb = 0, width, 2 * width
    o_eb = 3 * width
    o_g1 = o_eb + hidden
    o_s1 = o_g1 + width
    o_ob = o_s1 + width
    o_q = o_ob + width
    o_v = o_q + width

    staged_f = ((ctx, ctx_out, ctx_sem), (low, low_out, low_sem), (act, act_out, act_sem))
    staged_b = ((gred, gred_out, gred_sem), (gexp, gexp_out, gexp_sem), (gatt, gatt_out, gatt_sem),
                (gproj, gproj_out, gproj_sem), (gin, gin_out, gin_sem))

    combos = [(g, p) for p in range(pairs) for g in range(groups)]
    blocks = [slice(b, b + BLOCK) for b in range(0, rows, BLOCK)]

    def part_of(m, g, p, which):
        at = which * width + p * 128
        return qkv[m, g * slots:(g + 1) * slots, at:at + 128]

    def stats():
        means = [jnp.mean(acc[bs, :], -1, keepdims=True) for bs in blocks]
        parts = [acc[bs, :] - mean for bs, mean in zip(blocks, means)]
        return means, [lax.rsqrt(jnp.mean(c * c, -1, keepdims=True) + epsilon) for c in parts]

    def forward(m):
        slot = lax.rem(m, 2)

        @pl.when(stage == 0)
        def _():
            load_h(m).wait()

        @pl.when(stage > 0)
        def _():
            send_y(m).wait_recv()

        store(h_ref, h_out, hs_sem, m, m).start()

        @pl.when(m >= 2)
        def _():
            for src, dst, sem in staged_f:
                store(src, dst, sem, m - 2, slot).wait()

        h = h_ref[m]
        for c in range(0, 3 * width, 256):
            p = nn(h, aw[:, c:c + 256]) + ab[:, c:c + 256]
            if c < width:
                p = p * 0.125
            qkv[m, :, c:c + 256] = p.astype(bf16)
        oks = [usable[m * groups + g, 0:1, :] > 0 for g in range(groups)]
        ss = [jnp.where(oks[g], nt(stack(part_of(m, g, p, 0)), part_of(m, g, p, 1)), neg_large) for g, p in combos]
        tops = [jnp.max(s, -1, keepdims=True) for s in ss]
        es = [jnp.exp(s - top) for s, top in zip(ss, tops)]
        invs = [1.0 / jnp.sum(e, -1, keepdims=True) for e in es]
        for (g, p), e, inv in zip(combos, es, invs):
            shares[m, g * pairs + p] = (e * inv).astype(bf16)
        os = [nn(shares[m, g * pairs + p], part_of(m, g, p, 2)) for g, p in combos]
        for (g, p), o in zip(combos, os):
            ctx[slot, g * slots:(g + 1) * slots, p * 128:(p + 1) * 128] = unstack(o).astype(bf16)
        store(ctx, ctx_out, ctx_sem, m, slot).start()
        c_all = ctx[slot]
        for c in range(0, width, 256):
            acc[:, c:c + 256] = nn(c_all, ow[:, c:c + 256]) + ob[:, c:c + 256]
        for bs in blocks:
            acc[bs, :] += h_ref[m, bs, :].astype(f32)
        for bs, mean, inv in zip(blocks, *stats()):
            normed = (acc[bs, :] - mean) * inv
            out = normed * g1[...] + s1[...]
            n1[m, bs, :] = normed.astype(bf16)
            r1[m, bs, :] = jnp.broadcast_to(inv, (BLOCK, 128))
            mid[bs, :] = out
            low[slot, bs, :] = out.astype(bf16)
        store(low, low_out, low_sem, m, slot).start()
        l_all = low[slot]
        for c in range(0, hidden, CHUNK):
            x = nn(l_all, ew[:, c:c + CHUNK]) + eb[:, c:c + CHUNK]
            a, d = gelu_pair(x)
            act[slot, :, c:c + CHUNK] = a.astype(bf16)
            gp[m, :, c:c + CHUNK] = d.astype(bf16)
        store(act, act_out, act_sem, m, slot).start()
        a_all = act[slot]
        for c in range(0, width, 256):
            acc[:, c:c + 256] = nn(a_all, rw[:, c:c + 256]) + rb[:, c:c + 256]
        for bs in blocks:
            acc[bs, :] += mid[bs, :]
        for bs, mean, inv in zip(blocks, *stats()):
            normed = (acc[bs, :] - mean) * inv
            n2[m, bs, :] = normed.astype(bf16)
            r2[m, bs, :] = jnp.broadcast_to(inv, (BLOCK, 128))
            y_ref[m, bs, :] = (normed * g2[...] + s2[...]).astype(bf16)

        @pl.when(stage < last)
        def _():
            send_y(m).start()

        store(y_ref, y_out, y_sem, m, m).start()

    def norm_back(grad, normed, inv, gain, first, second):
        return inv * (grad * gain - first - normed * second)

    def norm_sums(grad, normed, gain):
        scaled = grad * gain
        return jnp.mean(scaled, -1, keepdims=True), jnp.mean(scaled * normed, -1, keepdims=True)

    def backward(m):
        slot = lax.rem(m, 2)

        @pl.when(stage == last)
        def _():
            load_g(m).wait()

        @pl.when(stage < last)
        def _():
            send_g(m).wait_recv()

        @pl.when(m >= 2)
        def _():
            for src, dst, sem in staged_b:
                store(src, dst, sem, m - 2, slot).wait()

        pairs_of = [norm_sums(g_ref[m, bs, :].astype(f32), n2[m, bs, :].astype(f32), g2[...]) for bs in blocks]
        for bs, (one, two) in zip(blocks, pairs_of):
            go = g_ref[m, bs, :].astype(f32)
            normed = n2[m, bs, :].astype(f32)
            mix = norm_back(go, normed, r2[m, bs, 0:1], g2[...], one, two)
            mid[bs, :] = mix
            gred[slot, bs, :] = mix.astype(bf16)
            sums[:, o_g2:o_g2 + width] += fold(go * normed)
            sums[:, o_s2:o_s2 + width] += fold(go)
            sums[:, o_rb:o_rb + width] += fold(mix)
        store(gred, gred_out, gred_sem, m, slot).start()
        r_all = gred[slot]
        for c in range(0, hidden, CHUNK):
            ge = nt(r_all, rw[c:c + CHUNK, :]) * gp[m, :, c:c + CHUNK].astype(f32)
            gexp[slot, :, c:c + CHUNK] = ge.astype(bf16)
            sums[:, o_eb + c:o_eb + c + CHUNK] += fold(ge)
        store(gexp, gexp_out, gexp_sem, m, slot).start()
        e_all = gexp[slot]
        for c in range(0, width, 256):
            acc[:, c:c + 256] = nt(e_all, ew[c:c + 256, :])
        for bs in blocks:
            acc[bs, :] += mid[bs, :]
        pairs_of = [norm_sums(acc[bs, :], n1[m, bs, :].astype(f32), g1[...]) for bs in blocks]
        for bs, (one, two) in zip(blocks, pairs_of):
            gf = acc[bs, :]
            normed = n1[m, bs, :].astype(f32)
            gm = norm_back(gf, normed, r1[m, bs, 0:1], g1[...], one, two)
            mid[bs, :] = gm
            gatt[slot, bs, :] = gm.astype(bf16)
            sums[:, o_g1:o_g1 + width] += fold(gf * normed)
            sums[:, o_s1:o_s1 + width] += fold(gf)
            sums[:, o_ob:o_ob + width] += fold(gm)
        store(gatt, gatt_out, gatt_sem, m, slot).start()
        t_all = gatt[slot]
        for c in range(0, width, 256):
            gctx[:, c:c + 256] = nt(t_all, ow[c:c + 256, :]).astype(bf16)

        def gc_of(g, p):
            return stack(gctx[g * slots:(g + 1) * slots, p * 128:(p + 1) * 128])

        def put(g, p, which, v):
            at = which * width + p * 128
            gproj[slot, g * slots:(g + 1) * slots, at:at + 128] = v.astype(bf16)

        gss = [nt(gc_of(g, p), part_of(m, g, p, 2)) for g, p in combos]
        gvs = [tn(shares[m, g * pairs + p], gc_of(g, p)) for g, p in combos]
        dots = [jnp.sum(gs * shares[m, g * pairs + p].astype(f32), -1, keepdims=True) for (g, p), gs in zip(combos, gss)]
        gscs = [(shares[m, g * pairs + p].astype(f32) * (gs - d)).astype(bf16)
                for (g, p), gs, d in zip(combos, gss, dots)]
        gqs = [unstack(nn(gsc, part_of(m, g, p, 1))) * 0.125 for (g, p), gsc in zip(combos, gscs)]
        gks = [tn(gsc, stack(part_of(m, g, p, 0))) for (g, p), gsc in zip(combos, gscs)]
        for (g, p), gq, gk, gv in zip(combos, gqs, gks, gvs):
            put(g, p, 0, gq)
            put(g, p, 1, gk)
            put(g, p, 2, gv)
            sums[:, o_q + p * 128:o_q + (p + 1) * 128] += fold(gq)
            sums[:, o_v + p * 128:o_v + (p + 1) * 128] += fold(gv)
        store(gproj, gproj_out, gproj_sem, m, slot).start()
        p_all = gproj[slot]
        for c in range(0, width, 256):
            gi = nt(p_all, aw[c:c + 256, :]) + mid[:, c:c + 256]
            gin[slot, :, c:c + 256] = gi
            gb_ref[m, :, c:c + 256] = gi.astype(bf16)

        @pl.when(stage > 0)
        def _():
            send_g(m).start()

        store(gin, gin_out, gin_sem, m, slot).start()

    lag = jnp.where(stage == last, 0, micro - 1)

    def tick(i, carry):
        @pl.when(i < micro)
        def _():
            forward(i)

        j = i - lag

        @pl.when((j >= 0) & (j < micro))
        def _():
            backward(j)

        return carry

    lax.fori_loop(0, 2 * micro - 1, tick, 0)

    for m in range(micro):
        store(h_ref, h_out, hs_sem, m, m).wait()
        store(y_ref, y_out, y_sem, m, m).wait()

        @pl.when(stage < last)
        def _():
            send_y(m).wait_send()

        @pl.when(stage > 0)
        def _():
            send_g(m).wait_send()

    for m in range(max(0, micro - 2), micro):
        for src, dst, sem in staged_f + staged_b:
            store(src, dst, sem, m, m % 2).wait()


def run_pipeline(rows_in, tangents, lengths, regions, weights, vectors):
    total, width = rows_in.shape
    slots = regions.shape[1]
    rows = GROUP * slots
    micro = total // rows
    aw, ow, ew, rw = weights
    hidden = ew.shape[1]
    pairs = width // 128
    wide = 3 * width
    sum_width = 8 * width + hidden
    hbm = pl.BlockSpec(memory_space=pl.ANY)
    vmem = pl.BlockSpec(memory_space=pltpu.VMEM)
    dma = pltpu.SemaphoreType.DMA
    shape = jax.ShapeDtypeStruct
    flops = 4 * total * (4 * width * width + 2 * width * hidden)
    return pl.pallas_call(
        functools.partial(pipeline_kernel, micro),
        out_shape=(
            shape((total, width), bf16), shape((total, width), f32), shape((total, width), bf16),
            shape((total, width), bf16), shape((total, width), bf16), shape((total, hidden), bf16),
            shape((total, width), bf16), shape((total, hidden), bf16), shape((total, width), bf16),
            shape((total, wide), bf16), shape((8, sum_width), f32),
        ),
        in_specs=[hbm, hbm, pl.BlockSpec(memory_space=pltpu.SMEM)] + [vmem] * 13,
        out_specs=(hbm,) * 10 + (vmem,),
        scratch_shapes=[pltpu.VMEM((regions.shape[0], 8, slots), f32), pltpu.VMEM((rows, width), bf16)] + [pltpu.VMEM((1, n), f32) for n in (wide, width, width, width, hidden, width, width, width)] + [
            pltpu.VMEM((micro, rows, width), bf16),
            pltpu.VMEM((micro, rows, width), bf16),
            pltpu.VMEM((micro, rows, width), bf16),
            pltpu.VMEM((micro, rows, width), bf16),
            pltpu.VMEM((micro, rows, wide), bf16),
            pltpu.VMEM((micro, GROUP * pairs, 2 * slots, slots), bf16),
            pltpu.VMEM((micro, rows, hidden), bf16),
            pltpu.VMEM((micro, rows, width), bf16),
            pltpu.VMEM((micro, rows, 128), f32),
            pltpu.VMEM((micro, rows, width), bf16),
            pltpu.VMEM((micro, rows, 128), f32),
            pltpu.VMEM((2, rows, width), bf16),
            pltpu.VMEM((2, rows, width), bf16),
            pltpu.VMEM((2, rows, hidden), bf16),
            pltpu.VMEM((2, rows, width), bf16),
            pltpu.VMEM((2, rows, hidden), bf16),
            pltpu.VMEM((2, rows, width), bf16),
            pltpu.VMEM((2, rows, wide), bf16),
            pltpu.VMEM((2, rows, width), f32),
            pltpu.VMEM((rows, width), f32),
            pltpu.VMEM((rows, width), f32),
        ] + [dma((micro,))] * 8 + [dma((2,))] * 8,
        compiler_params=pltpu.CompilerParams(
            collective_id=0, has_side_effects=True, vmem_limit_bytes=63 * 1024 * 1024),
        cost_estimate=pl.CostEstimate(flops=flops, bytes_accessed=40_000_000, transcendentals=total * hidden),
    )(rows_in, tangents, lengths, regions, aw, ow, ew, rw, *vectors)


def sum_kernel(
    dp, act_any, gred_any, low_any, gexp_any, h_any, gproj_any, ctx_any, gatt_any, sums_in,
    total, vector,
    part, left, right, vec_in, *rest,
):
    steps = dp.bit_length() - 1
    plane = steps - 1
    landed = rest[:steps]
    left_sem, right_sem, send_sem, recv_sem, vsend_sem, vrecv_sem = rest[steps:]
    units, rows, cols = part.shape
    me = lax.axis_index("dp")
    hid_blocks = act_any.shape[1] // cols
    wide_blocks = gproj_any.shape[1] // cols
    sources = (
        [(act_any, k, gred_any, 0) for k in range(hid_blocks)]
        + [(low_any, 0, gexp_any, k) for k in range(hid_blocks)]
        + [(h_any, 0, gproj_any, k) for k in range(wide_blocks)]
        + [(ctx_any, 0, gatt_any, 0)]
    )

    def bit_of(mask):
        return lax.rem(me // mask, 2)

    def masks_of(step):
        if step == 0:
            return 1, 1
        return 2 ** (1 + (step - 1) % plane), 2 ** (1 + (step - 1 + plane // 2) % plane)

    def place(unit, step):
        parity = lax.rem(unit, 2)
        first, second = masks_of(step)
        mask = first + parity * (second - first)
        bit = bit_of(first) + parity * (bit_of(second) - bit_of(first))
        return bit, me + mask * (1 - 2 * bit)

    def base(unit, step):
        start, size = 0, rows
        for k in range(step):
            size = size // 2
            start = start + place(unit, k)[0] * size
        return start, size

    def ds(start, size):
        return pl.ds(pl.multiple_of(start, 16), size)

    def reduce_copy(unit, step):
        bit, peer = place(unit, step)
        start, size = base(unit, step)
        half = size // 2
        return pltpu.make_async_remote_copy(
            src_ref=part.at[unit, ds(start + (1 - bit) * half, half)], dst_ref=landed[step].at[unit],
            send_sem=send_sem.at[step, unit], recv_sem=recv_sem.at[step, unit],
            device_id={"dp": peer}, device_id_type=MESH)

    def gather_copy(unit, step):
        peer = place(unit, step)[1]
        start, size = base(unit, step + 1)
        where = 2 * steps - 1 - step
        return pltpu.make_async_remote_copy(
            src_ref=total.at[unit, ds(start, size)], dst_ref=total.at[unit, ds(start, size)],
            send_sem=send_sem.at[where, unit], recv_sem=recv_sem.at[where, unit],
            device_id={"dp": peer}, device_id_type=MESH)

    def gather_arrival(unit, step):
        bit, peer = place(unit, step)
        start, size = base(unit, step)
        half = size // 2
        where = 2 * steps - 1 - step
        there = ds(start + (1 - bit) * half, half)
        return pltpu.make_async_remote_copy(
            src_ref=total.at[unit, there], dst_ref=total.at[unit, there],
            send_sem=send_sem.at[where, unit], recv_sem=recv_sem.at[where, unit],
            device_id={"dp": peer}, device_id_type=MESH)

    def vector_copy(step):
        peer = me + 2 ** step * (1 - 2 * bit_of(2 ** step))
        return pltpu.make_async_remote_copy(
            src_ref=vec_in.at[2 * step], dst_ref=vec_in.at[2 * step + 1],
            send_sem=vsend_sem.at[step], recv_sem=vrecv_sem.at[step],
            device_id={"dp": peer}, device_id_type=MESH)

    def loads(k, slot):
        a, ka, b, kb = sources[k]
        return (
            pltpu.make_async_copy(a.at[:, pl.ds(ka * cols, cols)], left.at[slot], left_sem.at[slot]),
            pltpu.make_async_copy(b.at[:, pl.ds(kb * cols, cols)], right.at[slot], right_sem.at[slot]),
        )

    for copy in loads(0, 0):
        copy.start()
    barrier = pltpu.get_barrier_semaphore()
    for step in range(steps):
        peer = me + 2 ** step * (1 - 2 * bit_of(2 ** step))
        pl.semaphore_signal(barrier, inc=1, device_id={"dp": peer}, device_id_type=MESH)
    v = jnp.sum(sums_in[...], 0, keepdims=True)
    lanes = vec_in.shape[2]
    for r in range(8):
        vec_in[0, r:r + 1, :] = v[:, r * lanes:(r + 1) * lanes]
    pl.semaphore_wait(barrier, steps)

    def add(unit, step):
        start, size = base(unit, step + 1)
        for b in range(0, size, 96):
            n = min(96, size - b)
            rs = ds(start + b, n)
            s = part[unit, rs, :].astype(f32) + landed[step][unit, b:b + n, :].astype(f32)
            if step == steps - 1:
                total[unit, rs, :] = s.astype(bf16)
            else:
                part[unit, rs, :] = s.astype(bf16)

    def when_unit(unit, body):
        @pl.when((unit >= 0) & (unit < units))
        def _():
            body(unit)

    def make(unit):
        for s in range(rows // cols):
            block = unit * (rows // cols) + s
            slot = lax.rem(block, 2)
            for k in range(len(sources)):
                @pl.when(block == k)
                def _():
                    if k + 1 < len(sources):
                        for copy in loads(k + 1, (k + 1) % 2):
                            copy.start()
                    for copy in loads(k, k % 2):
                        copy.wait()
            for r in range(0, cols, 256):
                part[unit, s * cols + r:s * cols + r + 256, :] = tn(left[slot, :, r:r + 256], right[slot]).astype(bf16)
        reduce_copy(unit, 0).start()

    def reduce_next(step):
        def body(unit):
            reduce_copy(unit, step).wait_recv()
            add(unit, step)
            if step + 1 < steps:
                reduce_copy(unit, step + 1).start()
            else:
                gather_copy(unit, step).start()
        return body

    def gather_next(step):
        def body(unit):
            gather_arrival(unit, step).wait_recv()
            if step > 0:
                gather_copy(unit, step - 1).start()
        return body

    lag = 0
    lags = []
    for step in range(steps):
        lag += 1 if step == 0 else 2
        lags.append((lag, reduce_next(step)))
    for step in reversed(range(steps)):
        lag += 2
        lags.append((lag, gather_next(step)))

    def tick(t, carry):
        when_unit(t, make)
        for behind, body in lags:
            when_unit(t - behind, body)
        for step in range(steps):
            @pl.when(t == 2 + 2 * step)
            def _():
                if step > 0:
                    vector_copy(step - 1).wait_recv()
                    vec_in[2 * step] = vec_in[2 * step - 2] + vec_in[2 * step - 1]
                vector_copy(step).start()

        return carry

    lax.fori_loop(0, units + lag, tick, 0)
    vector_copy(steps - 1).wait_recv()
    vector[...] = vec_in[2 * steps - 2] + vec_in[2 * steps - 1]

    def finish(unit, carry):
        for step in range(steps):
            reduce_copy(unit, step).wait_send()
            gather_copy(unit, step).wait_send()
        return carry

    lax.fori_loop(0, units, finish, 0)
    for step in range(steps):
        vector_copy(step).wait_send()


def write_kernel(hid_blocks, wide_blocks, total, vector, aw_g, ab_g, ow_g, ob_g, g1_g, s1_g, ew_g, eb_g, rw_g, rb_g, g2_g, s2_g):
    t = pl.program_id(0)
    first, second = hid_blocks, 2 * hid_blocks
    third = second + wide_blocks

    @pl.when(t == 0)
    def _():
        piece = vector.shape[1] // 3
        at = 0
        for out in (g2_g, s2_g, rb_g, eb_g, g1_g, s1_g, ob_g, ab_g):
            for k in range(out.shape[1] // piece):
                r, c = at // 3, at % 3
                out[:, k * piece:(k + 1) * piece] = vector[r:r + 1, c * piece:(c + 1) * piece]
                at += 1

    @pl.when(t < first)
    def _():
        rw_g[...] = total[...].astype(f32)

    @pl.when((t >= first) & (t < second))
    def _():
        ew_g[...] = total[...].astype(f32)

    @pl.when((t >= second) & (t < third))
    def _():
        aw_g[...] = total[...].astype(f32)

    @pl.when(t >= third)
    def _():
        ow_g[...] = total[...].astype(f32)


def run_sums(parts, sums, dp):
    act, gred, low, gexp, h, gproj, ctx, gatt = parts
    total_rows, width = h.shape
    hidden, wide = act.shape[1], gproj.shape[1]
    hid_blocks, wide_blocks = hidden // width, wide // width
    blocks = 2 * hid_blocks + wide_blocks + 1
    steps = dp.bit_length() - 1
    span = 1
    while span * width % (16 * dp):
        span *= 2
    units, unit_rows = blocks // span, span * width
    lanes = sums.shape[1] // 8
    hbm = pl.BlockSpec(memory_space=pl.ANY)
    vmem = pl.BlockSpec(memory_space=pltpu.VMEM)
    dma = pltpu.SemaphoreType.DMA
    shape = jax.ShapeDtypeStruct
    total, vector = pl.pallas_call(
        functools.partial(sum_kernel, dp),
        out_shape=(shape((units, unit_rows, width), bf16), shape((8, lanes), f32)),
        in_specs=[hbm] * 8 + [vmem],
        out_specs=(vmem, vmem),
        scratch_shapes=[
            pltpu.VMEM((units, unit_rows, width), bf16),
            pltpu.VMEM((2, total_rows, width), bf16),
            pltpu.VMEM((2, total_rows, width), bf16),
            pltpu.VMEM((2 * steps, 8, lanes), f32),
        ] + [pltpu.VMEM((units, unit_rows // 2 ** (k + 1), width), bf16) for k in range(steps)] + [
            dma((2,)), dma((2,)), dma((2 * steps, units)), dma((2 * steps, units)), dma((steps,)), dma((steps,)),
        ],
        compiler_params=pltpu.CompilerParams(
            collective_id=1, has_side_effects=True, vmem_limit_bytes=63 * 1024 * 1024),
    )(act, gred, low, gexp, h, gproj, ctx, gatt, sums)

    def one(count):
        return shape((1, count), f32), pl.BlockSpec((1, count), lambda t: (0, 0))

    a, b = hid_blocks, 2 * hid_blocks
    outs = [
        (shape((width, wide), f32), pl.BlockSpec((width, width), lambda t: (0, jnp.clip(t - b, 0, wide_blocks - 1)))),
        one(2 * width),
        (shape((width, width), f32), pl.BlockSpec((width, width), lambda t: (0, 0))),
        one(width), one(width), one(width),
        (shape((width, hidden), f32), pl.BlockSpec((width, width), lambda t: (0, jnp.clip(t - a, 0, hid_blocks - 1)))),
        one(hidden),
        (shape((hidden, width), f32), pl.BlockSpec((width, width), lambda t: (jnp.clip(t, 0, hid_blocks - 1), 0))),
        one(width), one(width), one(width),
    ]
    return pl.pallas_call(
        functools.partial(write_kernel, hid_blocks, wide_blocks),
        grid=(blocks,),
        out_shape=tuple(o[0] for o in outs),
        in_specs=[pl.BlockSpec((None, width, width), lambda t: (t, 0, 0)), pl.BlockSpec((8, lanes), lambda t: (0, 0))],
        out_specs=tuple(o[1] for o in outs),
        compiler_params=pltpu.CompilerParams(vmem_limit_bytes=60 * 1024 * 1024),
    )(total.reshape(blocks, width, width), vector)


def local(
    layer_input, lengths, regions, cotangent,
    attend_weight, attend_bias, output_weight, output_bias, first_gain, first_shift,
    expand_weight, expand_bias, reduce_weight, reduce_bias, second_gain, second_shift,
):
    seqs, slots, width = layer_input.shape
    total = seqs * slots
    vectors = (attend_bias, output_bias, first_gain, first_shift, expand_bias, reduce_bias, second_gain, second_shift)
    weights = (attend_weight[0], output_weight[0], expand_weight[0], reduce_weight[0])
    y, gin, h, ctx, low, act, gred, gexp, gatt, gproj, sums = run_pipeline(
        layer_input.reshape(total, width), cotangent.reshape(total, width), lengths, regions, weights, vectors)
    grads = run_sums((act, gred, low, gexp, h, gproj, ctx, gatt), sums, lax.axis_size("dp"))
    return (y.reshape(1, seqs, slots, width), gin.reshape(1, seqs, slots, width)) + tuple(
        g[None] if g.shape[0] > 1 else g for g in grads)


def solution(mesh):
    rows = P("dp", None, None)
    cube = P("pipe", None, None)
    flat = P("pipe", None)
    grads = P("pipe", "dp", None, None)
    return jax.shard_map(
        local,
        mesh=mesh,
        in_specs=(rows, P("dp"), P("dp", None), rows, cube, flat, cube, flat, flat, flat, cube, flat, cube, flat, flat, flat),
        out_specs=(grads, grads, cube, flat, cube, flat, flat, flat, cube, flat, cube, flat, flat, flat),
        check_vma=False,
    )
```

```python
import functools

import jax
import jax.numpy as jnp
from jax import lax
from jax.experimental import pallas as pl
from jax.experimental.pallas import tpu as pltpu
from jax.sharding import PartitionSpec as P

HEADS = 12
GROUP = 1
BLOCK = 32
CHUNK = 512
epsilon = 1e-05
neg_large = -1000000000.0
MESH = pl.DeviceIdType.MESH
f32 = jnp.float32
bf16 = jnp.bfloat16


def nn(left, right):
    return jnp.dot(left, right, preferred_element_type=f32)


def nt(left, right):
    return lax.dot_general(left, right, (((1,), (1,)), ((), ())), preferred_element_type=f32)


def tn(left, right):
    return lax.dot_general(left, right, (((0,), (0,)), ((), ())), preferred_element_type=f32)


def gelu_pair(x):
    phi = 0.5 + 0.5 * lax.erf(x * 0.7071067811865476)
    return x * phi, phi + (x * 0.3989422804014327) * jnp.exp2((x * x) * -0.7213475204444817)


def fold(v):
    rows, cols = v.shape
    return jnp.sum(v.reshape(rows // 8, 8, cols), 0)


def pipeline_kernel(
    micro,
    x_any, ct_any, lengths, regions, aw_any, ow_any, ew_any, rw_any, ab_in, ob_in, g1_in, s1_in, eb_in, rb_in, g2_in, s2_in,
    y_out, gin_out, h_out, ctx_out, low_out, act_out, gred_out, gexp_out, gatt_out, gproj_out, sums,
    aw, ow, ew, rw, awt, owt, ewt, rwt, usable, gctx, ab, ob, g1, s1, eb, rb, g2, s2,
    h_ref, g_ref, y_ref, gb_ref, qkv, shares, gp, n1, r1, n2, r2,
    ctx, low, act, gred, gexp, gatt, gproj, gin, acc, mid,
    w_sem, h_sem, g_sem, ysend_sem, yrecv_sem, gsend_sem, grecv_sem, y_sem, hs_sem,
    ctx_sem, low_sem, act_sem, gred_sem, gexp_sem, gatt_sem, gproj_sem, gin_sem,
):
    stage = lax.axis_index("pipe")
    count = lax.axis_size("pipe")
    last = count - 1
    slots = regions.shape[1]
    rows = h_ref.shape[1]
    groups = rows // slots
    width = h_ref.shape[2]
    hidden = ew.shape[1]
    pairs = width // 128
    before = jnp.maximum(stage - 1, 0)
    after = jnp.minimum(stage + 1, last)

    def send_y(m):
        return pltpu.make_async_remote_copy(
            src_ref=y_ref.at[m], dst_ref=h_ref.at[m], send_sem=ysend_sem.at[m], recv_sem=yrecv_sem.at[m],
            device_id={"pipe": after}, device_id_type=MESH)

    def send_g(m):
        return pltpu.make_async_remote_copy(
            src_ref=gb_ref.at[m], dst_ref=g_ref.at[m], send_sem=gsend_sem.at[m], recv_sem=grecv_sem.at[m],
            device_id={"pipe": before}, device_id_type=MESH)

    def load_h(m):
        return pltpu.make_async_copy(x_any.at[pl.ds(m * rows, rows)], h_ref.at[m], h_sem.at[m])

    def load_g(m):
        return pltpu.make_async_copy(ct_any.at[pl.ds(m * rows, rows)], g_ref.at[m], g_sem.at[m])

    def store(src, dst, sem, m, slot):
        return pltpu.make_async_copy(src.at[slot], dst.at[pl.ds(m * rows, rows)], sem.at[slot])

    filled = ((aw_any, aw), (ow_any, ow), (ew_any, ew), (rw_any, rw))

    def load_w(k):
        return pltpu.make_async_copy(filled[k][0], filled[k][1], w_sem.at[k])

    load_w(0).start()

    @pl.when(stage == 0)
    def _():
        for m in range(micro):
            load_h(m).start()

    for k in range(1, 4):
        load_w(k).start()

    @pl.when(stage == last)
    def _():
        for m in range(micro):
            load_g(m).start()

    barrier = pltpu.get_barrier_semaphore()

    @pl.when(stage > 0)
    def _():
        pl.semaphore_signal(barrier, inc=1, device_id={"pipe": before}, device_id_type=MESH)

    @pl.when(stage < last)
    def _():
        pl.semaphore_signal(barrier, inc=1, device_id={"pipe": after}, device_id_type=MESH)

    load_w(0).wait()
    inside = (stage > 0) & (stage < last)

    @pl.when(inside)
    def _():
        pl.semaphore_wait(barrier, 2)

    @pl.when(jnp.logical_not(inside))
    def _():
        pl.semaphore_wait(barrier, 1)

    sums[...] = jnp.zeros_like(sums)
    ab[:, :width] = ab_in[:, :width].astype(f32)
    ab[:, width:2 * width] = jnp.zeros((1, width), f32)
    ab[:, 2 * width:] = ab_in[:, width:].astype(f32)
    for dst, src in ((ob, ob_in), (g1, g1_in), (s1, s1_in), (eb, eb_in), (rb, rb_in), (g2, g2_in), (s2, s2_in)):
        dst[...] = src[...].astype(f32)
    position = lax.broadcasted_iota(jnp.int32, (1, slots), 1)
    for seq in range(regions.shape[0]):
        known = (position < lengths[seq]) | (regions[seq:seq + 1, :] == 1)
        usable[seq] = jnp.broadcast_to(known.astype(f32), (8, slots))
    lane = lax.broadcasted_iota(jnp.int32, (slots, 128), 1)
    first_half = lane < 64

    def stack(v):
        zero = jnp.zeros_like(v)
        return jnp.concatenate([jnp.where(first_half, v, zero), jnp.where(first_half, zero, v)], 0)

    def unstack(v):
        return jnp.where(first_half, v[:slots], v[slots:])

    o_g2, o_s2, o_rb = 0, width, 2 * width
    o_eb = 3 * width
    o_g1 = o_eb + hidden
    o_s1 = o_g1 + width
    o_ob = o_s1 + width
    o_q = o_ob + width
    o_v = o_q + width

    staged_f = ((ctx, ctx_out, ctx_sem), (low, low_out, low_sem), (act, act_out, act_sem))
    staged_b = ((gred, gred_out, gred_sem), (gexp, gexp_out, gexp_sem), (gatt, gatt_out, gatt_sem),
                (gproj, gproj_out, gproj_sem), (gin, gin_out, gin_sem))

    combos = [(g, p) for p in range(pairs) for g in range(groups)]
    blocks = [slice(b, b + BLOCK) for b in range(0, rows, BLOCK)]

    def part_of(m, g, p, which):
        at = which * width + p * 128
        return qkv[m, g * slots:(g + 1) * slots, at:at + 128]

    def stats():
        means = [jnp.mean(acc[bs, :], -1, keepdims=True) for bs in blocks]
        parts = [acc[bs, :] - mean for bs, mean in zip(blocks, means)]
        return means, [lax.rsqrt(jnp.mean(c * c, -1, keepdims=True) + epsilon) for c in parts]

    def forward(m):
        slot = lax.rem(m, 2)

        @pl.when(stage == 0)
        def _():
            load_h(m).wait()

        @pl.when(stage > 0)
        def _():
            send_y(m).wait_recv()

        store(h_ref, h_out, hs_sem, m, m).start()

        @pl.when(m >= 2)
        def _():
            for src, dst, sem in staged_f:
                store(src, dst, sem, m - 2, slot).wait()

        h = h_ref[m]
        for c in range(0, 3 * width, 256):
            p = nn(h, aw[:, c:c + 256]) + ab[:, c:c + 256]
            if c < width:
                p = p * 0.125
            qkv[m, :, c:c + 256] = p.astype(bf16)
        oks = [usable[m * groups + g, 0:1, :] > 0 for g in range(groups)]
        ss = [jnp.where(oks[g], nt(stack(part_of(m, g, p, 0)), part_of(m, g, p, 1)), neg_large) for g, p in combos]
        tops = [jnp.max(s, -1, keepdims=True) for s in ss]
        es = [jnp.exp(s - top) for s, top in zip(ss, tops)]
        invs = [1.0 / jnp.sum(e, -1, keepdims=True) for e in es]
        for (g, p), e, inv in zip(combos, es, invs):
            shares[m, g * pairs + p] = (e * inv).astype(bf16)
        os = [nn(shares[m, g * pairs + p], part_of(m, g, p, 2)) for g, p in combos]
        for (g, p), o in zip(combos, os):
            ctx[slot, g * slots:(g + 1) * slots, p * 128:(p + 1) * 128] = unstack(o).astype(bf16)
        store(ctx, ctx_out, ctx_sem, m, slot).start()

        @pl.when((m == 0) & (stage == 0))
        def _():
            for k in range(1, 4):
                load_w(k).wait()

        c_all = ctx[slot]
        for c in range(0, width, 256):
            acc[:, c:c + 256] = nn(c_all, ow[:, c:c + 256]) + ob[:, c:c + 256]
        for bs in blocks:
            acc[bs, :] += h_ref[m, bs, :].astype(f32)
        for bs, mean, inv in zip(blocks, *stats()):
            normed = (acc[bs, :] - mean) * inv
            out = normed * g1[...] + s1[...]
            n1[m, bs, :] = normed.astype(bf16)
            r1[m, bs, :] = jnp.broadcast_to(inv, (BLOCK, 128))
            mid[bs, :] = out
            low[slot, bs, :] = out.astype(bf16)
        store(low, low_out, low_sem, m, slot).start()
        l_all = low[slot]
        for c in range(0, hidden, CHUNK):
            x = nn(l_all, ew[:, c:c + CHUNK]) + eb[:, c:c + CHUNK]
            a, d = gelu_pair(x)
            act[slot, :, c:c + CHUNK] = a.astype(bf16)
            gp[m, :, c:c + CHUNK] = d.astype(bf16)
        store(act, act_out, act_sem, m, slot).start()
        a_all = act[slot]
        for c in range(0, width, 256):
            acc[:, c:c + 256] = nn(a_all, rw[:, c:c + 256]) + rb[:, c:c + 256]
        for bs in blocks:
            acc[bs, :] += mid[bs, :]
        for bs, mean, inv in zip(blocks, *stats()):
            normed = (acc[bs, :] - mean) * inv
            n2[m, bs, :] = normed.astype(bf16)
            r2[m, bs, :] = jnp.broadcast_to(inv, (BLOCK, 128))
            y_ref[m, bs, :] = (normed * g2[...] + s2[...]).astype(bf16)

        @pl.when(stage < last)
        def _():
            send_y(m).start()

        store(y_ref, y_out, y_sem, m, m).start()

    def norm_back(grad, normed, inv, gain, first, second):
        return inv * (grad * gain - first - normed * second)

    def norm_sums(grad, normed, gain):
        scaled = grad * gain
        return jnp.mean(scaled, -1, keepdims=True), jnp.mean(scaled * normed, -1, keepdims=True)

    def backward(m):
        slot = lax.rem(m, 2)

        @pl.when(stage == last)
        def _():
            load_g(m).wait()

        @pl.when(stage < last)
        def _():
            send_g(m).wait_recv()

        @pl.when(m >= 2)
        def _():
            for src, dst, sem in staged_b:
                store(src, dst, sem, m - 2, slot).wait()

        pairs_of = [norm_sums(g_ref[m, bs, :].astype(f32), n2[m, bs, :].astype(f32), g2[...]) for bs in blocks]
        for bs, (one, two) in zip(blocks, pairs_of):
            go = g_ref[m, bs, :].astype(f32)
            normed = n2[m, bs, :].astype(f32)
            mix = norm_back(go, normed, r2[m, bs, 0:1], g2[...], one, two)
            mid[bs, :] = mix
            gred[slot, bs, :] = mix.astype(bf16)
            sums[:, o_g2:o_g2 + width] += fold(go * normed)
            sums[:, o_s2:o_s2 + width] += fold(go)
            sums[:, o_rb:o_rb + width] += fold(mix)
        store(gred, gred_out, gred_sem, m, slot).start()
        r_all = gred[slot]
        for c in range(0, hidden, CHUNK):
            ge = nn(r_all, rwt[:, c:c + CHUNK]) * gp[m, :, c:c + CHUNK].astype(f32)
            gexp[slot, :, c:c + CHUNK] = ge.astype(bf16)
            sums[:, o_eb + c:o_eb + c + CHUNK] += fold(ge)
        store(gexp, gexp_out, gexp_sem, m, slot).start()
        e_all = gexp[slot]
        for c in range(0, width, 256):
            acc[:, c:c + 256] = nn(e_all, ewt[:, c:c + 256])
        for bs in blocks:
            acc[bs, :] += mid[bs, :]
        pairs_of = [norm_sums(acc[bs, :], n1[m, bs, :].astype(f32), g1[...]) for bs in blocks]
        for bs, (one, two) in zip(blocks, pairs_of):
            gf = acc[bs, :]
            normed = n1[m, bs, :].astype(f32)
            gm = norm_back(gf, normed, r1[m, bs, 0:1], g1[...], one, two)
            mid[bs, :] = gm
            gatt[slot, bs, :] = gm.astype(bf16)
            sums[:, o_g1:o_g1 + width] += fold(gf * normed)
            sums[:, o_s1:o_s1 + width] += fold(gf)
            sums[:, o_ob:o_ob + width] += fold(gm)
        store(gatt, gatt_out, gatt_sem, m, slot).start()
        t_all = gatt[slot]
        for c in range(0, width, 256):
            gctx[:, c:c + 256] = nn(t_all, owt[:, c:c + 256]).astype(bf16)

        def gc_of(g, p):
            return stack(gctx[g * slots:(g + 1) * slots, p * 128:(p + 1) * 128])

        def put(g, p, which, v):
            at = which * width + p * 128
            gproj[slot, g * slots:(g + 1) * slots, at:at + 128] = v.astype(bf16)

        gss = [nt(gc_of(g, p), part_of(m, g, p, 2)) for g, p in combos]
        gvs = [tn(shares[m, g * pairs + p], gc_of(g, p)) for g, p in combos]
        dots = [jnp.sum(gs * shares[m, g * pairs + p].astype(f32), -1, keepdims=True) for (g, p), gs in zip(combos, gss)]
        gscs = [(shares[m, g * pairs + p].astype(f32) * (gs - d)).astype(bf16)
                for (g, p), gs, d in zip(combos, gss, dots)]
        gqs = [unstack(nn(gsc, part_of(m, g, p, 1))) * 0.125 for (g, p), gsc in zip(combos, gscs)]
        gks = [tn(gsc, stack(part_of(m, g, p, 0))) for (g, p), gsc in zip(combos, gscs)]
        for (g, p), gq, gk, gv in zip(combos, gqs, gks, gvs):
            put(g, p, 0, gq)
            put(g, p, 1, gk)
            put(g, p, 2, gv)
            sums[:, o_q + p * 128:o_q + (p + 1) * 128] += fold(gq)
            sums[:, o_v + p * 128:o_v + (p + 1) * 128] += fold(gv)
        store(gproj, gproj_out, gproj_sem, m, slot).start()
        p_all = gproj[slot]
        for c in range(0, width, 256):
            gi = nn(p_all, awt[:, c:c + 256]) + mid[:, c:c + 256]
            gin[slot, :, c:c + 256] = gi
            gb_ref[m, :, c:c + 256] = gi.astype(bf16)

        @pl.when(stage > 0)
        def _():
            send_g(m).start()

        store(gin, gin_out, gin_sem, m, slot).start()

    lag = jnp.where(stage == last, 0, micro - 1)

    def turn():
        @pl.when(stage > 0)
        def _():
            for k in range(1, 4):
                load_w(k).wait()

        one = (lax.broadcasted_iota(jnp.int32, (256, 256), 0) == lax.broadcasted_iota(jnp.int32, (256, 256), 1)).astype(f32).astype(bf16)
        for src, dst in ((aw, awt), (ow, owt), (ew, ewt), (rw, rwt)):
            def across(k, carry, src=src, dst=dst):
                cols = pl.ds(pl.multiple_of(k * 256, 256), 256)
                for r in range(0, dst.shape[0], 256):
                    dst[r:r + 256, cols] = nt(one, src[cols, r:r + 256]).astype(bf16)
                return carry

            lax.fori_loop(0, src.shape[0] // 256, across, 0)

    def tick(t, carry):
        @pl.when((t >= 1) & (t <= micro))
        def _():
            forward(jnp.clip(t - 1, 0, micro - 1))

        @pl.when(t == jnp.where(stage > 0, 0, lag + 1))
        def _():
            turn()

        @pl.when((t >= lag + 1) & (t <= lag + micro))
        def _():
            backward(jnp.clip(t - 1 - lag, 0, micro - 1))

        return carry

    lax.fori_loop(0, 2 * micro, tick, 0)

    for m in range(micro):
        store(h_ref, h_out, hs_sem, m, m).wait()
        store(y_ref, y_out, y_sem, m, m).wait()

        @pl.when(stage < last)
        def _():
            send_y(m).wait_send()

        @pl.when(stage > 0)
        def _():
            send_g(m).wait_send()

    for m in range(max(0, micro - 2), micro):
        for src, dst, sem in staged_f + staged_b:
            store(src, dst, sem, m, m % 2).wait()


def run_pipeline(rows_in, tangents, lengths, regions, weights, vectors):
    total, width = rows_in.shape
    slots = regions.shape[1]
    rows = GROUP * slots
    micro = total // rows
    aw, ow, ew, rw = weights
    hidden = ew.shape[1]
    pairs = width // 128
    wide = 3 * width
    sum_width = 8 * width + hidden
    hbm = pl.BlockSpec(memory_space=pl.ANY)
    vmem = pl.BlockSpec(memory_space=pltpu.VMEM)
    dma = pltpu.SemaphoreType.DMA
    shape = jax.ShapeDtypeStruct
    flops = 4 * total * (4 * width * width + 2 * width * hidden)
    return pl.pallas_call(
        functools.partial(pipeline_kernel, micro),
        out_shape=(
            shape((total, width), bf16), shape((total, width), f32), shape((total, width), bf16),
            shape((total, width), bf16), shape((total, width), bf16), shape((total, hidden), bf16),
            shape((total, width), bf16), shape((total, hidden), bf16), shape((total, width), bf16),
            shape((total, wide), bf16), shape((8, sum_width), f32),
        ),
        in_specs=[hbm, hbm, pl.BlockSpec(memory_space=pltpu.SMEM), vmem] + [hbm] * 4 + [vmem] * 8,
        out_specs=(hbm,) * 10 + (vmem,),
        scratch_shapes=[pltpu.VMEM(w.shape, bf16) for w in weights] + [pltpu.VMEM(w.shape[::-1], bf16) for w in weights] + [pltpu.VMEM((regions.shape[0], 8, slots), f32), pltpu.VMEM((rows, width), bf16)] + [pltpu.VMEM((1, n), f32) for n in (wide, width, width, width, hidden, width, width, width)] + [
            pltpu.VMEM((micro, rows, width), bf16),
            pltpu.VMEM((micro, rows, width), bf16),
            pltpu.VMEM((micro, rows, width), bf16),
            pltpu.VMEM((micro, rows, width), bf16),
            pltpu.VMEM((micro, rows, wide), bf16),
            pltpu.VMEM((micro, GROUP * pairs, 2 * slots, slots), bf16),
            pltpu.VMEM((micro, rows, hidden), bf16),
            pltpu.VMEM((micro, rows, width), bf16),
            pltpu.VMEM((micro, rows, 128), f32),
            pltpu.VMEM((micro, rows, width), bf16),
            pltpu.VMEM((micro, rows, 128), f32),
            pltpu.VMEM((2, rows, width), bf16),
            pltpu.VMEM((2, rows, width), bf16),
            pltpu.VMEM((2, rows, hidden), bf16),
            pltpu.VMEM((2, rows, width), bf16),
            pltpu.VMEM((2, rows, hidden), bf16),
            pltpu.VMEM((2, rows, width), bf16),
            pltpu.VMEM((2, rows, wide), bf16),
            pltpu.VMEM((2, rows, width), f32),
            pltpu.VMEM((rows, width), f32),
            pltpu.VMEM((rows, width), f32),
        ] + [dma((4,))] + [dma((micro,))] * 8 + [dma((2,))] * 8,
        compiler_params=pltpu.CompilerParams(
            collective_id=0, has_side_effects=True, vmem_limit_bytes=63 * 1024 * 1024),
        cost_estimate=pl.CostEstimate(flops=flops, bytes_accessed=40_000_000, transcendentals=total * hidden),
    )(rows_in, tangents, lengths, regions, aw, ow, ew, rw, *vectors)


def sum_kernel(
    dp, act_any, gred_any, low_any, gexp_any, h_any, gproj_any, ctx_any, gatt_any, sums_in,
    total, vector,
    part, left, right, vec_in, *rest,
):
    steps = dp.bit_length() - 1
    plane = steps - 1
    landed = rest[:steps]
    left_sem, right_sem, send_sem, recv_sem, vsend_sem, vrecv_sem = rest[steps:]
    units, rows, cols = part.shape
    me = lax.axis_index("dp")
    hid_blocks = act_any.shape[1] // cols
    wide_blocks = gproj_any.shape[1] // cols
    sources = (
        [(act_any, k, gred_any, 0) for k in range(hid_blocks)]
        + [(low_any, 0, gexp_any, k) for k in range(hid_blocks)]
        + [(h_any, 0, gproj_any, k) for k in range(wide_blocks)]
        + [(ctx_any, 0, gatt_any, 0)]
    )

    def bit_of(mask):
        return lax.rem(me // mask, 2)

    def masks_of(step):
        if step == 0:
            return 1, 1
        return 2 ** (1 + (step - 1) % plane), 2 ** (1 + (step - 1 + plane // 2) % plane)

    def place(unit, step):
        parity = lax.rem(unit, 2)
        first, second = masks_of(step)
        mask = first + parity * (second - first)
        bit = bit_of(first) + parity * (bit_of(second) - bit_of(first))
        return bit, me + mask * (1 - 2 * bit)

    def base(unit, step):
        start, size = 0, rows
        for k in range(step):
            size = size // 2
            start = start + place(unit, k)[0] * size
        return start, size

    def ds(start, size):
        return pl.ds(pl.multiple_of(start, 16), size)

    def reduce_copy(unit, step):
        bit, peer = place(unit, step)
        start, size = base(unit, step)
        half = size // 2
        return pltpu.make_async_remote_copy(
            src_ref=part.at[unit, ds(start + (1 - bit) * half, half)], dst_ref=landed[step].at[unit],
            send_sem=send_sem.at[step, unit], recv_sem=recv_sem.at[step, unit],
            device_id={"dp": peer}, device_id_type=MESH)

    def gather_copy(unit, step):
        peer = place(unit, step)[1]
        start, size = base(unit, step + 1)
        where = 2 * steps - 1 - step
        return pltpu.make_async_remote_copy(
            src_ref=total.at[unit, ds(start, size)], dst_ref=total.at[unit, ds(start, size)],
            send_sem=send_sem.at[where, unit], recv_sem=recv_sem.at[where, unit],
            device_id={"dp": peer}, device_id_type=MESH)

    def gather_arrival(unit, step):
        bit, peer = place(unit, step)
        start, size = base(unit, step)
        half = size // 2
        where = 2 * steps - 1 - step
        there = ds(start + (1 - bit) * half, half)
        return pltpu.make_async_remote_copy(
            src_ref=total.at[unit, there], dst_ref=total.at[unit, there],
            send_sem=send_sem.at[where, unit], recv_sem=recv_sem.at[where, unit],
            device_id={"dp": peer}, device_id_type=MESH)

    def vector_copy(step):
        peer = me + 2 ** step * (1 - 2 * bit_of(2 ** step))
        return pltpu.make_async_remote_copy(
            src_ref=vec_in.at[2 * step], dst_ref=vec_in.at[2 * step + 1],
            send_sem=vsend_sem.at[step], recv_sem=vrecv_sem.at[step],
            device_id={"dp": peer}, device_id_type=MESH)

    def loads(k, slot):
        a, ka, b, kb = sources[k]
        return (
            pltpu.make_async_copy(a.at[:, pl.ds(ka * cols, cols)], left.at[slot], left_sem.at[slot]),
            pltpu.make_async_copy(b.at[:, pl.ds(kb * cols, cols)], right.at[slot], right_sem.at[slot]),
        )

    for copy in loads(0, 0):
        copy.start()
    barrier = pltpu.get_barrier_semaphore()
    for step in range(steps):
        peer = me + 2 ** step * (1 - 2 * bit_of(2 ** step))
        pl.semaphore_signal(barrier, inc=1, device_id={"dp": peer}, device_id_type=MESH)
    v = jnp.sum(sums_in[...], 0, keepdims=True)
    lanes = vec_in.shape[2]
    for r in range(8):
        vec_in[0, r:r + 1, :] = v[:, r * lanes:(r + 1) * lanes]
    pl.semaphore_wait(barrier, steps)

    def add(unit, step):
        start, size = base(unit, step + 1)
        for b in range(0, size, 96):
            n = min(96, size - b)
            rs = ds(start + b, n)
            s = part[unit, rs, :].astype(f32) + landed[step][unit, b:b + n, :].astype(f32)
            if step == steps - 1:
                total[unit, rs, :] = s.astype(bf16)
            else:
                part[unit, rs, :] = s.astype(bf16)

    def when_unit(unit, body):
        @pl.when((unit >= 0) & (unit < units))
        def _():
            body(unit)

    def make(unit):
        for s in range(rows // cols):
            block = unit * (rows // cols) + s
            slot = lax.rem(block, 2)
            for k in range(len(sources)):
                @pl.when(block == k)
                def _():
                    if k + 1 < len(sources):
                        for copy in loads(k + 1, (k + 1) % 2):
                            copy.start()
                    for copy in loads(k, k % 2):
                        copy.wait()
            for r in range(0, cols, 256):
                part[unit, s * cols + r:s * cols + r + 256, :] = tn(left[slot, :, r:r + 256], right[slot]).astype(bf16)
        reduce_copy(unit, 0).start()

    def reduce_next(step):
        def body(unit):
            reduce_copy(unit, step).wait_recv()
            add(unit, step)
            if step + 1 < steps:
                reduce_copy(unit, step + 1).start()
            else:
                gather_copy(unit, step).start()
        return body

    def gather_next(step):
        def body(unit):
            gather_arrival(unit, step).wait_recv()
            if step > 0:
                gather_copy(unit, step - 1).start()
        return body

    lag = 0
    lags = []
    for step in range(steps):
        lag += 1 if step == 0 else 2
        lags.append((lag, reduce_next(step)))
    for step in reversed(range(steps)):
        lag += 2
        lags.append((lag, gather_next(step)))

    def tick(t, carry):
        when_unit(t, make)
        for behind, body in lags:
            when_unit(t - behind, body)
        for step in range(steps):
            @pl.when(t == 2 + 2 * step)
            def _():
                if step > 0:
                    vector_copy(step - 1).wait_recv()
                    vec_in[2 * step] = vec_in[2 * step - 2] + vec_in[2 * step - 1]
                vector_copy(step).start()

        return carry

    lax.fori_loop(0, units + lag, tick, 0)
    vector_copy(steps - 1).wait_recv()
    vector[...] = vec_in[2 * steps - 2] + vec_in[2 * steps - 1]

    def finish(unit, carry):
        for step in range(steps):
            reduce_copy(unit, step).wait_send()
            gather_copy(unit, step).wait_send()
        return carry

    lax.fori_loop(0, units, finish, 0)
    for step in range(steps):
        vector_copy(step).wait_send()


def write_kernel(hid_blocks, wide_blocks, total, vector, aw_g, ab_g, ow_g, ob_g, g1_g, s1_g, ew_g, eb_g, rw_g, rb_g, g2_g, s2_g):
    t = pl.program_id(0)
    first, second = hid_blocks, 2 * hid_blocks
    third = second + wide_blocks

    @pl.when(t == 0)
    def _():
        piece = vector.shape[1] // 3
        at = 0
        for out in (g2_g, s2_g, rb_g, eb_g, g1_g, s1_g, ob_g, ab_g):
            for k in range(out.shape[1] // piece):
                r, c = at // 3, at % 3
                out[:, k * piece:(k + 1) * piece] = vector[r:r + 1, c * piece:(c + 1) * piece]
                at += 1

    @pl.when(t < first)
    def _():
        rw_g[...] = total[...].astype(f32)

    @pl.when((t >= first) & (t < second))
    def _():
        ew_g[...] = total[...].astype(f32)

    @pl.when((t >= second) & (t < third))
    def _():
        aw_g[...] = total[...].astype(f32)

    @pl.when(t >= third)
    def _():
        ow_g[...] = total[...].astype(f32)


def run_sums(parts, sums, dp):
    act, gred, low, gexp, h, gproj, ctx, gatt = parts
    total_rows, width = h.shape
    hidden, wide = act.shape[1], gproj.shape[1]
    hid_blocks, wide_blocks = hidden // width, wide // width
    blocks = 2 * hid_blocks + wide_blocks + 1
    steps = dp.bit_length() - 1
    span = 1
    while span * width % (16 * dp):
        span *= 2
    units, unit_rows = blocks // span, span * width
    lanes = sums.shape[1] // 8
    hbm = pl.BlockSpec(memory_space=pl.ANY)
    vmem = pl.BlockSpec(memory_space=pltpu.VMEM)
    dma = pltpu.SemaphoreType.DMA
    shape = jax.ShapeDtypeStruct
    total, vector = pl.pallas_call(
        functools.partial(sum_kernel, dp),
        out_shape=(shape((units, unit_rows, width), bf16), shape((8, lanes), f32)),
        in_specs=[hbm] * 8 + [vmem],
        out_specs=(vmem, vmem),
        scratch_shapes=[
            pltpu.VMEM((units, unit_rows, width), bf16),
            pltpu.VMEM((2, total_rows, width), bf16),
            pltpu.VMEM((2, total_rows, width), bf16),
            pltpu.VMEM((2 * steps, 8, lanes), f32),
        ] + [pltpu.VMEM((units, unit_rows // 2 ** (k + 1), width), bf16) for k in range(steps)] + [
            dma((2,)), dma((2,)), dma((2 * steps, units)), dma((2 * steps, units)), dma((steps,)), dma((steps,)),
        ],
        compiler_params=pltpu.CompilerParams(
            collective_id=1, has_side_effects=True, vmem_limit_bytes=63 * 1024 * 1024),
    )(act, gred, low, gexp, h, gproj, ctx, gatt, sums)

    def one(count):
        return shape((1, count), f32), pl.BlockSpec((1, count), lambda t: (0, 0))

    a, b = hid_blocks, 2 * hid_blocks
    outs = [
        (shape((width, wide), f32), pl.BlockSpec((width, width), lambda t: (0, jnp.clip(t - b, 0, wide_blocks - 1)))),
        one(2 * width),
        (shape((width, width), f32), pl.BlockSpec((width, width), lambda t: (0, 0))),
        one(width), one(width), one(width),
        (shape((width, hidden), f32), pl.BlockSpec((width, width), lambda t: (0, jnp.clip(t - a, 0, hid_blocks - 1)))),
        one(hidden),
        (shape((hidden, width), f32), pl.BlockSpec((width, width), lambda t: (jnp.clip(t, 0, hid_blocks - 1), 0))),
        one(width), one(width), one(width),
    ]
    return pl.pallas_call(
        functools.partial(write_kernel, hid_blocks, wide_blocks),
        grid=(blocks,),
        out_shape=tuple(o[0] for o in outs),
        in_specs=[pl.BlockSpec((None, width, width), lambda t: (t, 0, 0)), pl.BlockSpec((8, lanes), lambda t: (0, 0))],
        out_specs=tuple(o[1] for o in outs),
        compiler_params=pltpu.CompilerParams(vmem_limit_bytes=60 * 1024 * 1024),
    )(total.reshape(blocks, width, width), vector)


def local(
    layer_input, lengths, regions, cotangent,
    attend_weight, attend_bias, output_weight, output_bias, first_gain, first_shift,
    expand_weight, expand_bias, reduce_weight, reduce_bias, second_gain, second_shift,
):
    seqs, slots, width = layer_input.shape
    total = seqs * slots
    vectors = (attend_bias, output_bias, first_gain, first_shift, expand_bias, reduce_bias, second_gain, second_shift)
    weights = (attend_weight[0], output_weight[0], expand_weight[0], reduce_weight[0])
    y, gin, h, ctx, low, act, gred, gexp, gatt, gproj, sums = run_pipeline(
        layer_input.reshape(total, width), cotangent.reshape(total, width), lengths, regions, weights, vectors)
    grads = run_sums((act, gred, low, gexp, h, gproj, ctx, gatt), sums, lax.axis_size("dp"))
    return (y.reshape(1, seqs, slots, width), gin.reshape(1, seqs, slots, width)) + tuple(
        g[None] if g.shape[0] > 1 else g for g in grads)


def solution(mesh):
    rows = P("dp", None, None)
    cube = P("pipe", None, None)
    flat = P("pipe", None)
    grads = P("pipe", "dp", None, None)
    return jax.shard_map(
        local,
        mesh=mesh,
        in_specs=(rows, P("dp"), P("dp", None), rows, cube, flat, cube, flat, flat, flat, cube, flat, cube, flat, flat, flat),
        out_specs=(grads, grads, cube, flat, cube, flat, flat, flat, cube, flat, cube, flat, flat, flat),
        check_vma=False,
    )
```

```python
import functools

import jax
import jax.numpy as jnp
from jax import lax
from jax.experimental import pallas as pl
from jax.experimental.pallas import tpu as pltpu
from jax.sharding import PartitionSpec as P

HEADS = 12
GROUP = 1
BLOCK = 32
CHUNK = 512
PARTS = 4
epsilon = 1e-05
neg_large = -1000000000.0
MESH = pl.DeviceIdType.MESH
f32 = jnp.float32
bf16 = jnp.bfloat16


def nn(left, right):
    return jnp.dot(left, right, preferred_element_type=f32)


def nt(left, right):
    return lax.dot_general(left, right, (((1,), (1,)), ((), ())), preferred_element_type=f32)


def tn(left, right):
    return lax.dot_general(left, right, (((0,), (0,)), ((), ())), preferred_element_type=f32)


def gelu_pair(x):
    phi = 0.5 + 0.5 * lax.erf(x * 0.7071067811865476)
    return x * phi, phi + (x * 0.3989422804014327) * jnp.exp2((x * x) * -0.7213475204444817)


def fold(v):
    rows, cols = v.shape
    return jnp.sum(v.reshape(rows // 8, 8, cols), 0)


def pipeline_kernel(
    micro,
    x_any, ct_any, lengths, regions, aw_any, ow_any, ew_any, rw_any, ab_in, ob_in, g1_in, s1_in, eb_in, rb_in, g2_in, s2_in,
    y_out, gin_out, h_out, ctx_out, low_out, act_out, gred_out, gexp_out, gatt_out, gproj_out, sums,
    aw, ow, ew, rw, awt, owt, ewt, rwt, usable, gctx, ab, ob, g1, s1, eb, rb, g2, s2,
    h_ref, g_ref, y_ref, gb_ref, qkv, shares, gp, n1, r1, n2, r2,
    ctx, low, act, gred, gexp, gatt, gproj, gin, acc, mid,
    w_sem, h_sem, g_sem, ysend_sem, yrecv_sem, gsend_sem, grecv_sem, y_sem, hs_sem,
    ctx_sem, low_sem, act_sem, gred_sem, gexp_sem, gatt_sem, gproj_sem, gin_sem,
):
    stage = lax.axis_index("pipe")
    count = lax.axis_size("pipe")
    last = count - 1
    slots = regions.shape[1]
    rows = h_ref.shape[1]
    groups = rows // slots
    width = h_ref.shape[2]
    hidden = ew.shape[1]
    pairs = width // 128
    before = jnp.maximum(stage - 1, 0)
    after = jnp.minimum(stage + 1, last)

    def send_y(m):
        return pltpu.make_async_remote_copy(
            src_ref=y_ref.at[m], dst_ref=h_ref.at[m], send_sem=ysend_sem.at[m], recv_sem=yrecv_sem.at[m],
            device_id={"pipe": after}, device_id_type=MESH)

    def send_g(m):
        return pltpu.make_async_remote_copy(
            src_ref=gb_ref.at[m], dst_ref=g_ref.at[m], send_sem=gsend_sem.at[m], recv_sem=grecv_sem.at[m],
            device_id={"pipe": before}, device_id_type=MESH)

    def load_h(m):
        return pltpu.make_async_copy(x_any.at[pl.ds(m * rows, rows)], h_ref.at[m], h_sem.at[m])

    def load_g(m):
        return pltpu.make_async_copy(ct_any.at[pl.ds(m * rows, rows)], g_ref.at[m], g_sem.at[m])

    def store(src, dst, sem, m, slot):
        return pltpu.make_async_copy(src.at[slot], dst.at[pl.ds(m * rows, rows)], sem.at[slot])

    filled = ((aw_any, aw), (ow_any, ow), (ew_any, ew), (rw_any, rw))

    def load_w(k):
        return pltpu.make_async_copy(filled[k][0], filled[k][1], w_sem.at[k])

    load_w(0).start()

    @pl.when(stage == 0)
    def _():
        for m in range(micro):
            load_h(m).start()

    for k in range(1, 4):
        load_w(k).start()

    @pl.when(stage == last)
    def _():
        for m in range(micro):
            load_g(m).start()

    barrier = pltpu.get_barrier_semaphore()

    @pl.when(stage > 0)
    def _():
        pl.semaphore_signal(barrier, inc=1, device_id={"pipe": before}, device_id_type=MESH)

    @pl.when(stage < last)
    def _():
        pl.semaphore_signal(barrier, inc=1, device_id={"pipe": after}, device_id_type=MESH)

    load_w(0).wait()
    inside = (stage > 0) & (stage < last)

    @pl.when(inside)
    def _():
        pl.semaphore_wait(barrier, 2)

    @pl.when(jnp.logical_not(inside))
    def _():
        pl.semaphore_wait(barrier, 1)

    sums[...] = jnp.zeros_like(sums)
    ab[:, :width] = ab_in[:, :width].astype(f32)
    ab[:, width:2 * width] = jnp.zeros((1, width), f32)
    ab[:, 2 * width:] = ab_in[:, width:].astype(f32)
    for dst, src in ((ob, ob_in), (g1, g1_in), (s1, s1_in), (eb, eb_in), (rb, rb_in), (g2, g2_in), (s2, s2_in)):
        dst[...] = src[...].astype(f32)
    position = lax.broadcasted_iota(jnp.int32, (1, slots), 1)
    for seq in range(regions.shape[0]):
        known = (position < lengths[seq]) | (regions[seq:seq + 1, :] == 1)
        usable[seq] = jnp.broadcast_to(known.astype(f32), (8, slots))
    lane = lax.broadcasted_iota(jnp.int32, (slots, 128), 1)
    first_half = lane < 64

    def stack(v):
        zero = jnp.zeros_like(v)
        return jnp.concatenate([jnp.where(first_half, v, zero), jnp.where(first_half, zero, v)], 0)

    def unstack(v):
        return jnp.where(first_half, v[:slots], v[slots:])

    o_g2, o_s2, o_rb = 0, width, 2 * width
    o_eb = 3 * width
    o_g1 = o_eb + hidden
    o_s1 = o_g1 + width
    o_ob = o_s1 + width
    o_q = o_ob + width
    o_v = o_q + width

    staged_f = ((ctx, ctx_out, ctx_sem), (low, low_out, low_sem), (act, act_out, act_sem))
    staged_b = ((gred, gred_out, gred_sem), (gexp, gexp_out, gexp_sem), (gatt, gatt_out, gatt_sem),
                (gproj, gproj_out, gproj_sem), (gin, gin_out, gin_sem))

    combos = [(g, p) for p in range(pairs) for g in range(groups)]
    blocks = [slice(b, b + BLOCK) for b in range(0, rows, BLOCK)]

    def part_of(m, g, p, which):
        at = which * width + p * 128
        return qkv[m, g * slots:(g + 1) * slots, at:at + 128]

    def stats():
        means = [jnp.mean(acc[bs, :], -1, keepdims=True) for bs in blocks]
        parts = [acc[bs, :] - mean for bs, mean in zip(blocks, means)]
        return means, [lax.rsqrt(jnp.mean(c * c, -1, keepdims=True) + epsilon) for c in parts]

    def forward(m):
        slot = lax.rem(m, 2)

        @pl.when(stage == 0)
        def _():
            load_h(m).wait()

        @pl.when(stage > 0)
        def _():
            send_y(m).wait_recv()

        store(h_ref, h_out, hs_sem, m, m).start()

        @pl.when(m >= 2)
        def _():
            for src, dst, sem in staged_f:
                store(src, dst, sem, m - 2, slot).wait()

        h = h_ref[m]
        for c in range(0, 3 * width, 256):
            p = nn(h, aw[:, c:c + 256]) + ab[:, c:c + 256]
            if c < width:
                p = p * 0.125
            qkv[m, :, c:c + 256] = p.astype(bf16)
        oks = [usable[m * groups + g, 0:1, :] > 0 for g in range(groups)]
        ss = [jnp.where(oks[g], nt(stack(part_of(m, g, p, 0)), part_of(m, g, p, 1)), neg_large) for g, p in combos]
        tops = [jnp.max(s, -1, keepdims=True) for s in ss]
        es = [jnp.exp(s - top) for s, top in zip(ss, tops)]
        invs = [1.0 / jnp.sum(e, -1, keepdims=True) for e in es]
        for (g, p), e, inv in zip(combos, es, invs):
            shares[m, g * pairs + p] = (e * inv).astype(bf16)
        os = [nn(shares[m, g * pairs + p], part_of(m, g, p, 2)) for g, p in combos]
        for (g, p), o in zip(combos, os):
            ctx[slot, g * slots:(g + 1) * slots, p * 128:(p + 1) * 128] = unstack(o).astype(bf16)
        store(ctx, ctx_out, ctx_sem, m, slot).start()

        @pl.when((m == 0) & (stage == 0))
        def _():
            for k in range(1, 4):
                load_w(k).wait()

        c_all = ctx[slot]
        for c in range(0, width, 256):
            acc[:, c:c + 256] = nn(c_all, ow[:, c:c + 256]) + ob[:, c:c + 256]
        for bs in blocks:
            acc[bs, :] += h_ref[m, bs, :].astype(f32)
        for bs, mean, inv in zip(blocks, *stats()):
            normed = (acc[bs, :] - mean) * inv
            out = normed * g1[...] + s1[...]
            n1[m, bs, :] = normed.astype(bf16)
            r1[m, bs, :] = jnp.broadcast_to(inv, (BLOCK, 128))
            mid[bs, :] = out
            low[slot, bs, :] = out.astype(bf16)
        store(low, low_out, low_sem, m, slot).start()
        l_all = low[slot]
        for c in range(0, hidden, CHUNK):
            x = nn(l_all, ew[:, c:c + CHUNK]) + eb[:, c:c + CHUNK]
            a, d = gelu_pair(x)
            act[slot, :, c:c + CHUNK] = a.astype(bf16)
            gp[m, :, c:c + CHUNK] = d.astype(bf16)
        store(act, act_out, act_sem, m, slot).start()
        a_all = act[slot]
        for c in range(0, width, 256):
            acc[:, c:c + 256] = nn(a_all, rw[:, c:c + 256]) + rb[:, c:c + 256]
        for bs in blocks:
            acc[bs, :] += mid[bs, :]
        for bs, mean, inv in zip(blocks, *stats()):
            normed = (acc[bs, :] - mean) * inv
            n2[m, bs, :] = normed.astype(bf16)
            r2[m, bs, :] = jnp.broadcast_to(inv, (BLOCK, 128))
            y_ref[m, bs, :] = (normed * g2[...] + s2[...]).astype(bf16)

        @pl.when(stage < last)
        def _():
            send_y(m).start()

        store(y_ref, y_out, y_sem, m, m).start()

    def norm_back(grad, normed, inv, gain, first, second):
        return inv * (grad * gain - first - normed * second)

    def norm_sums(grad, normed, gain):
        scaled = grad * gain
        return jnp.mean(scaled, -1, keepdims=True), jnp.mean(scaled * normed, -1, keepdims=True)

    def backward(m):
        slot = lax.rem(m, 2)

        @pl.when(stage == last)
        def _():
            load_g(m).wait()

        @pl.when(stage < last)
        def _():
            send_g(m).wait_recv()

        @pl.when(m >= 2)
        def _():
            for src, dst, sem in staged_b:
                store(src, dst, sem, m - 2, slot).wait()

        pairs_of = [norm_sums(g_ref[m, bs, :].astype(f32), n2[m, bs, :].astype(f32), g2[...]) for bs in blocks]
        for bs, (one, two) in zip(blocks, pairs_of):
            go = g_ref[m, bs, :].astype(f32)
            normed = n2[m, bs, :].astype(f32)
            mix = norm_back(go, normed, r2[m, bs, 0:1], g2[...], one, two)
            mid[bs, :] = mix
            gred[slot, bs, :] = mix.astype(bf16)
            sums[:, o_g2:o_g2 + width] += fold(go * normed)
            sums[:, o_s2:o_s2 + width] += fold(go)
            sums[:, o_rb:o_rb + width] += fold(mix)
        store(gred, gred_out, gred_sem, m, slot).start()
        r_all = gred[slot]
        for c in range(0, hidden, CHUNK):
            ge = nn(r_all, rwt[:, c:c + CHUNK]) * gp[m, :, c:c + CHUNK].astype(f32)
            gexp[slot, :, c:c + CHUNK] = ge.astype(bf16)
            sums[:, o_eb + c:o_eb + c + CHUNK] += fold(ge)
        store(gexp, gexp_out, gexp_sem, m, slot).start()
        e_all = gexp[slot]
        for c in range(0, width, 256):
            acc[:, c:c + 256] = nn(e_all, ewt[:, c:c + 256])
        for bs in blocks:
            acc[bs, :] += mid[bs, :]
        pairs_of = [norm_sums(acc[bs, :], n1[m, bs, :].astype(f32), g1[...]) for bs in blocks]
        for bs, (one, two) in zip(blocks, pairs_of):
            gf = acc[bs, :]
            normed = n1[m, bs, :].astype(f32)
            gm = norm_back(gf, normed, r1[m, bs, 0:1], g1[...], one, two)
            mid[bs, :] = gm
            gatt[slot, bs, :] = gm.astype(bf16)
            sums[:, o_g1:o_g1 + width] += fold(gf * normed)
            sums[:, o_s1:o_s1 + width] += fold(gf)
            sums[:, o_ob:o_ob + width] += fold(gm)
        store(gatt, gatt_out, gatt_sem, m, slot).start()
        t_all = gatt[slot]
        for c in range(0, width, 256):
            gctx[:, c:c + 256] = nn(t_all, owt[:, c:c + 256]).astype(bf16)

        def gc_of(g, p):
            return stack(gctx[g * slots:(g + 1) * slots, p * 128:(p + 1) * 128])

        def put(g, p, which, v):
            at = which * width + p * 128
            gproj[slot, g * slots:(g + 1) * slots, at:at + 128] = v.astype(bf16)

        gss = [nt(gc_of(g, p), part_of(m, g, p, 2)) for g, p in combos]
        gvs = [tn(shares[m, g * pairs + p], gc_of(g, p)) for g, p in combos]
        dots = [jnp.sum(gs * shares[m, g * pairs + p].astype(f32), -1, keepdims=True) for (g, p), gs in zip(combos, gss)]
        gscs = [(shares[m, g * pairs + p].astype(f32) * (gs - d)).astype(bf16)
                for (g, p), gs, d in zip(combos, gss, dots)]
        gqs = [unstack(nn(gsc, part_of(m, g, p, 1))) * 0.125 for (g, p), gsc in zip(combos, gscs)]
        gks = [tn(gsc, stack(part_of(m, g, p, 0))) for (g, p), gsc in zip(combos, gscs)]
        for (g, p), gq, gk, gv in zip(combos, gqs, gks, gvs):
            put(g, p, 0, gq)
            put(g, p, 1, gk)
            put(g, p, 2, gv)
            sums[:, o_q + p * 128:o_q + (p + 1) * 128] += fold(gq)
            sums[:, o_v + p * 128:o_v + (p + 1) * 128] += fold(gv)
        store(gproj, gproj_out, gproj_sem, m, slot).start()
        p_all = gproj[slot]
        for c in range(0, width, 256):
            gi = nn(p_all, awt[:, c:c + 256]) + mid[:, c:c + 256]
            gin[slot, :, c:c + 256] = gi
            gb_ref[m, :, c:c + 256] = gi.astype(bf16)

        @pl.when(stage > 0)
        def _():
            send_g(m).start()

        store(gin, gin_out, gin_sem, m, slot).start()

    lag = jnp.where(stage == last, 0, micro - 1)

    def turn():
        @pl.when(stage > 0)
        def _():
            for k in range(1, 4):
                load_w(k).wait()

        one = (lax.broadcasted_iota(jnp.int32, (256, 256), 0) == lax.broadcasted_iota(jnp.int32, (256, 256), 1)).astype(f32).astype(bf16)
        for src, dst in ((aw, awt), (ow, owt), (ew, ewt), (rw, rwt)):
            def across(k, carry, src=src, dst=dst):
                cols = pl.ds(pl.multiple_of(k * 256, 256), 256)
                for r in range(0, dst.shape[0], 256):
                    dst[r:r + 256, cols] = nt(one, src[cols, r:r + 256]).astype(bf16)
                return carry

            lax.fori_loop(0, src.shape[0] // 256, across, 0)

    def tick(t, carry):
        @pl.when((t >= 1) & (t <= micro))
        def _():
            forward(jnp.clip(t - 1, 0, micro - 1))

        @pl.when(t == jnp.where(stage > 0, 0, lag + 1))
        def _():
            turn()

        @pl.when((t >= lag + 1) & (t <= lag + micro))
        def _():
            backward(jnp.clip(t - 1 - lag, 0, micro - 1))

        return carry

    lax.fori_loop(0, 2 * micro, tick, 0)

    for m in range(micro):
        store(h_ref, h_out, hs_sem, m, m).wait()
        store(y_ref, y_out, y_sem, m, m).wait()

        @pl.when(stage < last)
        def _():
            send_y(m).wait_send()

        @pl.when(stage > 0)
        def _():
            send_g(m).wait_send()

    for m in range(max(0, micro - 2), micro):
        for src, dst, sem in staged_f + staged_b:
            store(src, dst, sem, m, m % 2).wait()


def run_pipeline(rows_in, tangents, lengths, regions, weights, vectors):
    total, width = rows_in.shape
    slots = regions.shape[1]
    rows = GROUP * slots
    micro = total // rows
    aw, ow, ew, rw = weights
    hidden = ew.shape[1]
    pairs = width // 128
    wide = 3 * width
    sum_width = 8 * width + hidden
    hbm = pl.BlockSpec(memory_space=pl.ANY)
    vmem = pl.BlockSpec(memory_space=pltpu.VMEM)
    dma = pltpu.SemaphoreType.DMA
    shape = jax.ShapeDtypeStruct
    flops = 4 * total * (4 * width * width + 2 * width * hidden)
    return pl.pallas_call(
        functools.partial(pipeline_kernel, micro),
        out_shape=(
            shape((total, width), bf16), shape((total, width), f32), shape((total, width), bf16),
            shape((total, width), bf16), shape((total, width), bf16), shape((total, hidden), bf16),
            shape((total, width), bf16), shape((total, hidden), bf16), shape((total, width), bf16),
            shape((total, wide), bf16), shape((8, sum_width), f32),
        ),
        in_specs=[hbm, hbm, pl.BlockSpec(memory_space=pltpu.SMEM), vmem] + [hbm] * 4 + [vmem] * 8,
        out_specs=(hbm,) * 10 + (vmem,),
        scratch_shapes=[pltpu.VMEM(w.shape, bf16) for w in weights] + [pltpu.VMEM(w.shape[::-1], bf16) for w in weights] + [pltpu.VMEM((regions.shape[0], 8, slots), f32), pltpu.VMEM((rows, width), bf16)] + [pltpu.VMEM((1, n), f32) for n in (wide, width, width, width, hidden, width, width, width)] + [
            pltpu.VMEM((micro, rows, width), bf16),
            pltpu.VMEM((micro, rows, width), bf16),
            pltpu.VMEM((micro, rows, width), bf16),
            pltpu.VMEM((micro, rows, width), bf16),
            pltpu.VMEM((micro, rows, wide), bf16),
            pltpu.VMEM((micro, GROUP * pairs, 2 * slots, slots), bf16),
            pltpu.VMEM((micro, rows, hidden), bf16),
            pltpu.VMEM((micro, rows, width), bf16),
            pltpu.VMEM((micro, rows, 128), f32),
            pltpu.VMEM((micro, rows, width), bf16),
            pltpu.VMEM((micro, rows, 128), f32),
            pltpu.VMEM((2, rows, width), bf16),
            pltpu.VMEM((2, rows, width), bf16),
            pltpu.VMEM((2, rows, hidden), bf16),
            pltpu.VMEM((2, rows, width), bf16),
            pltpu.VMEM((2, rows, hidden), bf16),
            pltpu.VMEM((2, rows, width), bf16),
            pltpu.VMEM((2, rows, wide), bf16),
            pltpu.VMEM((2, rows, width), f32),
            pltpu.VMEM((rows, width), f32),
            pltpu.VMEM((rows, width), f32),
        ] + [dma((4,))] + [dma((micro,))] * 8 + [dma((2,))] * 8,
        compiler_params=pltpu.CompilerParams(
            collective_id=0, has_side_effects=True, vmem_limit_bytes=63 * 1024 * 1024),
        cost_estimate=pl.CostEstimate(flops=flops, bytes_accessed=40_000_000, transcendentals=total * hidden),
    )(rows_in, tangents, lengths, regions, aw, ow, ew, rw, *vectors)


def sum_kernel(
    dp, act_any, gred_any, low_any, gexp_any, h_any, gproj_any, ctx_any, gatt_any, sums_in,
    total, vector,
    part, left, right, vec_in, *rest,
):
    steps = dp.bit_length() - 1
    plane = steps - 1
    landed = rest[:steps]
    left_sem, right_sem, send_sem, recv_sem, vsend_sem, vrecv_sem, out_sem = rest[steps:]
    units, rows, cols = part.shape
    me = lax.axis_index("dp")
    hid_blocks = act_any.shape[1] // cols
    wide_blocks = gproj_any.shape[1] // cols
    sources = (
        [(act_any, k, gred_any, 0) for k in range(hid_blocks)]
        + [(low_any, 0, gexp_any, k) for k in range(hid_blocks)]
        + [(h_any, 0, gproj_any, k) for k in range(wide_blocks)]
        + [(ctx_any, 0, gatt_any, 0)]
    )

    def bit_of(mask):
        return lax.rem(me // mask, 2)

    def masks_of(step):
        if step == 0:
            return 1, 1
        return 2 ** (1 + (step - 1) % plane), 2 ** (1 + (step - 1 + plane // 2) % plane)

    def place(unit, step):
        parity = lax.rem(unit, 2)
        first, second = masks_of(step)
        mask = first + parity * (second - first)
        bit = bit_of(first) + parity * (bit_of(second) - bit_of(first))
        return bit, me + mask * (1 - 2 * bit)

    def base(unit, step):
        start, size = 0, rows
        for k in range(step):
            size = size // 2
            start = start + place(unit, k)[0] * size
        return start, size

    def ds(start, size):
        return pl.ds(pl.multiple_of(start, 16), size)

    def reduce_copy(unit, step):
        bit, peer = place(unit, step)
        start, size = base(unit, step)
        half = size // 2
        return pltpu.make_async_remote_copy(
            src_ref=part.at[unit, ds(start + (1 - bit) * half, half)], dst_ref=landed[step].at[unit],
            send_sem=send_sem.at[step, unit], recv_sem=recv_sem.at[step, unit],
            device_id={"dp": peer}, device_id_type=MESH)

    def gather_copy(unit, step):
        peer = place(unit, step)[1]
        start, size = base(unit, step + 1)
        where = 2 * steps - 1 - step
        own = part if step == steps - 1 else total
        return pltpu.make_async_remote_copy(
            src_ref=own.at[unit, ds(start, size)], dst_ref=total.at[unit, ds(start, size)],
            send_sem=send_sem.at[where, unit], recv_sem=recv_sem.at[where, unit],
            device_id={"dp": peer}, device_id_type=MESH)

    def gather_arrival(unit, step):
        bit, peer = place(unit, step)
        start, size = base(unit, step)
        half = size // 2
        where = 2 * steps - 1 - step
        there = ds(start + (1 - bit) * half, half)
        return pltpu.make_async_remote_copy(
            src_ref=total.at[unit, there], dst_ref=total.at[unit, there],
            send_sem=send_sem.at[where, unit], recv_sem=recv_sem.at[where, unit],
            device_id={"dp": peer}, device_id_type=MESH)

    def keep(unit):
        start, size = base(unit, steps)
        rs = ds(start, size)
        return pltpu.make_async_copy(part.at[unit, rs], total.at[unit, rs], out_sem.at[unit])

    def vector_copy(step):
        peer = me + 2 ** step * (1 - 2 * bit_of(2 ** step))
        return pltpu.make_async_remote_copy(
            src_ref=vec_in.at[2 * step], dst_ref=vec_in.at[2 * step + 1],
            send_sem=vsend_sem.at[step], recv_sem=vrecv_sem.at[step],
            device_id={"dp": peer}, device_id_type=MESH)

    def loads(k, slot):
        a, ka, b, kb = sources[k]
        return (
            pltpu.make_async_copy(a.at[:, pl.ds(ka * cols, cols)], left.at[slot], left_sem.at[slot]),
            pltpu.make_async_copy(b.at[:, pl.ds(kb * cols, cols)], right.at[slot], right_sem.at[slot]),
        )

    for copy in loads(0, 0):
        copy.start()
    barrier = pltpu.get_barrier_semaphore()
    for step in range(steps):
        peer = me + 2 ** step * (1 - 2 * bit_of(2 ** step))
        pl.semaphore_signal(barrier, inc=1, device_id={"dp": peer}, device_id_type=MESH)
    v = jnp.sum(sums_in[...], 0, keepdims=True)
    lanes = vec_in.shape[2]
    for r in range(8):
        vec_in[0, r:r + 1, :] = v[:, r * lanes:(r + 1) * lanes]
    pl.semaphore_wait(barrier, steps)

    def add(unit, step):
        start, size = base(unit, step + 1)
        for b in range(0, size, 96):
            n = min(96, size - b)
            rs = ds(start + b, n)
            s = part[unit, rs, :].astype(f32) + landed[step][unit, b:b + n, :].astype(f32)
            part[unit, rs, :] = s.astype(bf16)

    def when_unit(unit, body):
        @pl.when((unit >= 0) & (unit < units))
        def _():
            body(unit)

    def make(unit):
        for s in range(rows // cols):
            block = unit * (rows // cols) + s
            slot = lax.rem(block, 2)
            for k in range(len(sources)):
                @pl.when(block == k)
                def _():
                    if k + 1 < len(sources):
                        for copy in loads(k + 1, (k + 1) % 2):
                            copy.start()
                    for copy in loads(k, k % 2):
                        copy.wait()
            for r in range(0, cols, 256):
                part[unit, s * cols + r:s * cols + r + 256, :] = tn(left[slot, :, r:r + 256], right[slot]).astype(bf16)
        reduce_copy(unit, 0).start()

    def reduce_next(step):
        def body(unit):
            reduce_copy(unit, step).wait_recv()
            add(unit, step)
            if step + 1 < steps:
                reduce_copy(unit, step + 1).start()
            else:
                gather_copy(unit, step).start()
                keep(unit).start()
        return body

    def gather_next(step):
        def body(unit):
            gather_arrival(unit, step).wait_recv()
            if step == steps - 1:
                keep(unit).wait()
            if step > 0:
                gather_copy(unit, step - 1).start()
        return body

    lag = 0
    lags = []
    for step in range(steps):
        lag += 1 if step == 0 else 2
        lags.append((lag, reduce_next(step)))
    for step in reversed(range(steps)):
        lag += 2
        lags.append((lag, gather_next(step)))

    def tick(t, carry):
        when_unit(t, make)
        for behind, body in lags:
            when_unit(t - behind, body)
        for step in range(steps):
            @pl.when(t == 2 + 2 * step)
            def _():
                if step > 0:
                    vector_copy(step - 1).wait_recv()
                    vec_in[2 * step] = vec_in[2 * step - 2] + vec_in[2 * step - 1]
                vector_copy(step).start()

        return carry

    lax.fori_loop(0, units + lag, tick, 0)
    vector_copy(steps - 1).wait_recv()
    vector[...] = vec_in[2 * steps - 2] + vec_in[2 * steps - 1]

    def finish(unit, carry):
        for step in range(steps):
            reduce_copy(unit, step).wait_send()
            gather_copy(unit, step).wait_send()
        return carry

    lax.fori_loop(0, units, finish, 0)
    for step in range(steps):
        vector_copy(step).wait_send()


def write_kernel(hid_blocks, wide_blocks, total, vector, y, gin, y_g, gin_g, aw_g, ab_g, ow_g, ob_g, g1_g, s1_g, ew_g, eb_g, rw_g, rb_g, g2_g, s2_g, taken, given, y_buf, gin_buf, move_sem, in_sem, out_sem):
    depth, rows, cols = taken.shape
    places = (
        [(rw_g, k, 0) for k in range(hid_blocks)] + [(ew_g, 0, k) for k in range(hid_blocks)]
        + [(aw_g, 0, k) for k in range(wide_blocks)] + [(ow_g, 0, 0)]
    )
    split, span = cols // rows, total.shape[1] // cols
    chunks = [(block, part) for block in range(len(places)) for part in range(split)]

    def bring(k):
        block, part = chunks[k]
        start = (block % span) * cols + part * rows
        return pltpu.make_async_copy(total.at[block // span, pl.ds(start, rows)], taken.at[k % depth], in_sem.at[k % depth])

    def give(k):
        block, part = chunks[k]
        out, i, j = places[block]
        target = out.at[pl.ds(i * cols + part * rows, rows), pl.ds(j * cols, cols)]
        return pltpu.make_async_copy(given.at[k % depth], target, out_sem.at[k % depth])

    ins = (pltpu.make_async_copy(y, y_buf, move_sem.at[0]), pltpu.make_async_copy(gin, gin_buf, move_sem.at[1]))
    outs = (pltpu.make_async_copy(y_buf, y_g, move_sem.at[2]), pltpu.make_async_copy(gin_buf, gin_g, move_sem.at[3]))
    for k in range(depth):
        bring(k).start()
    for move in ins:
        move.start()
    piece = vector.shape[1] // 3
    at = 0
    for out in (g2_g, s2_g, rb_g, eb_g, g1_g, s1_g, ob_g, ab_g):
        for k in range(out.shape[1] // piece):
            r, c = at // 3, at % 3
            out[:, k * piece:(k + 1) * piece] = vector[r:r + 1, c * piece:(c + 1) * piece]
            at += 1
    for k in range(len(chunks)):
        bring(k).wait()
        if k >= depth:
            give(k - depth).wait()
        given[k % depth] = taken[k % depth].astype(f32)
        give(k).start()
        if k + depth < len(chunks):
            bring(k + depth).start()
        if k == depth:
            for arrived, move in zip(ins, outs):
                arrived.wait()
                move.start()
    for k in range(len(chunks) - depth, len(chunks)):
        give(k).wait()
    for move in outs:
        move.wait()


def run_sums(parts, sums, y, gin, dp):
    act, gred, low, gexp, h, gproj, ctx, gatt = parts
    total_rows, width = h.shape
    hidden, wide = act.shape[1], gproj.shape[1]
    hid_blocks, wide_blocks = hidden // width, wide // width
    blocks = 2 * hid_blocks + wide_blocks + 1
    steps = dp.bit_length() - 1
    span = 1
    while span * width % (16 * dp):
        span *= 2
    units, unit_rows = blocks // span, span * width
    lanes = sums.shape[1] // 8
    hbm = pl.BlockSpec(memory_space=pl.ANY)
    vmem = pl.BlockSpec(memory_space=pltpu.VMEM)
    dma = pltpu.SemaphoreType.DMA
    shape = jax.ShapeDtypeStruct
    total, vector = pl.pallas_call(
        functools.partial(sum_kernel, dp),
        out_shape=(shape((units, unit_rows, width), bf16), shape((8, lanes), f32)),
        in_specs=[hbm] * 8 + [vmem],
        out_specs=(hbm, vmem),
        scratch_shapes=[
            pltpu.VMEM((units, unit_rows, width), bf16),
            pltpu.VMEM((2, total_rows, width), bf16),
            pltpu.VMEM((2, total_rows, width), bf16),
            pltpu.VMEM((2 * steps, 8, lanes), f32),
        ] + [pltpu.VMEM((units, unit_rows // 2 ** (k + 1), width), bf16) for k in range(steps)] + [
            dma((2,)), dma((2,)), dma((2 * steps, units)), dma((2 * steps, units)), dma((steps,)), dma((steps,)), dma((units,)),
        ],
        compiler_params=pltpu.CompilerParams(
            collective_id=1, has_side_effects=True, vmem_limit_bytes=58 * 1024 * 1024),
    )(act, gred, low, gexp, h, gproj, ctx, gatt, sums)

    def one(count):
        return shape((1, count), f32), vmem

    outs = [
        (shape(y.shape, y.dtype), hbm), (shape(gin.shape, gin.dtype), hbm),
        (shape((width, wide), f32), hbm),
        one(2 * width),
        (shape((width, width), f32), hbm),
        one(width), one(width), one(width),
        (shape((width, hidden), f32), hbm),
        one(hidden),
        (shape((hidden, width), f32), hbm),
        one(width), one(width), one(width),
    ]
    return pl.pallas_call(
        functools.partial(write_kernel, hid_blocks, wide_blocks),
        out_shape=tuple(o[0] for o in outs),
        in_specs=[hbm, vmem, hbm, hbm],
        out_specs=tuple(o[1] for o in outs),
        scratch_shapes=[
            pltpu.VMEM((PARTS, width // 2, width), bf16), pltpu.VMEM((PARTS, width // 2, width), f32),
            pltpu.VMEM(y.shape, y.dtype), pltpu.VMEM(gin.shape, gin.dtype),
            dma((4,)), dma((PARTS,)), dma((PARTS,)),
        ],
        compiler_params=pltpu.CompilerParams(vmem_limit_bytes=52 * 1024 * 1024),
    )(total, vector, y, gin)


def local(
    layer_input, lengths, regions, cotangent,
    attend_weight, attend_bias, output_weight, output_bias, first_gain, first_shift,
    expand_weight, expand_bias, reduce_weight, reduce_bias, second_gain, second_shift,
):
    seqs, slots, width = layer_input.shape
    total = seqs * slots
    vectors = (attend_bias, output_bias, first_gain, first_shift, expand_bias, reduce_bias, second_gain, second_shift)
    weights = (attend_weight[0], output_weight[0], expand_weight[0], reduce_weight[0])
    y, gin, h, ctx, low, act, gred, gexp, gatt, gproj, sums = run_pipeline(
        layer_input.reshape(total, width), cotangent.reshape(total, width), lengths, regions, weights, vectors)
    y, gin, *grads = run_sums((act, gred, low, gexp, h, gproj, ctx, gatt), sums, y, gin, lax.axis_size("dp"))
    return (y.reshape(1, seqs, slots, width), gin.reshape(1, seqs, slots, width)) + tuple(
        g[None] if g.shape[0] > 1 else g for g in grads)


def solution(mesh):
    rows = P("dp", None, None)
    cube = P("pipe", None, None)
    flat = P("pipe", None)
    grads = P("pipe", "dp", None, None)
    return jax.shard_map(
        local,
        mesh=mesh,
        in_specs=(rows, P("dp"), P("dp", None), rows, cube, flat, cube, flat, flat, flat, cube, flat, cube, flat, flat, flat),
        out_specs=(grads, grads, cube, flat, cube, flat, flat, flat, cube, flat, cube, flat, flat, flat),
        check_vma=False,
    )
```

```python
import functools

import jax
import jax.numpy as jnp
from jax import lax
from jax.experimental import pallas as pl
from jax.experimental.pallas import tpu as pltpu
from jax.sharding import PartitionSpec as P

HEADS = 12
GROUP = 1
BLOCK = 32
CHUNK = 512
PARTS = 4
epsilon = 1e-05
neg_large = -1000000000.0
MESH = pl.DeviceIdType.MESH
f32 = jnp.float32
bf16 = jnp.bfloat16


def nn(left, right):
    return jnp.dot(left, right, preferred_element_type=f32)


def nt(left, right):
    return lax.dot_general(left, right, (((1,), (1,)), ((), ())), preferred_element_type=f32)


def tn(left, right):
    return lax.dot_general(left, right, (((0,), (0,)), ((), ())), preferred_element_type=f32)


def gelu_pair(x):
    phi = 0.5 + 0.5 * lax.erf(x * 0.7071067811865476)
    return x * phi, phi + (x * 0.3989422804014327) * jnp.exp2((x * x) * -0.7213475204444817)


def fold(v):
    rows, cols = v.shape
    return jnp.sum(v.reshape(rows // 8, 8, cols), 0)


def pipeline_kernel(
    micro,
    x_any, ct_any, lengths, regions, aw_any, ow_any, ew_any, rw_any, ab_in, ob_in, g1_in, s1_in, eb_in, rb_in, g2_in, s2_in,
    y_out, gin_out, h_out, ctx_out, low_out, act_out, gred_out, gexp_out, gatt_out, gproj_out, sums,
    aw, ow, ew, rw, awt, owt, ewt, rwt, usable, gctx, fresh, ab, ob, g1, s1, eb, rb, g2, s2,
    h_ref, g_ref, y_ref, gb_ref, qkv, shares, gp, n1, r1, n2, r2,
    ctx, low, act, gred, gexp, gatt, gproj, gin, acc, mid,
    w_sem, h_sem, g_sem, ysend_sem, yrecv_sem, gsend_sem, grecv_sem, y_sem, hs_sem,
    ctx_sem, low_sem, act_sem, gred_sem, gexp_sem, gatt_sem, gproj_sem, gin_sem,
):
    stage = lax.axis_index("pipe")
    count = lax.axis_size("pipe")
    last = count - 1
    slots = regions.shape[1]
    rows = h_ref.shape[1]
    groups = rows // slots
    width = h_ref.shape[2]
    hidden = ew.shape[1]
    pairs = width // 128
    before = jnp.maximum(stage - 1, 0)
    after = jnp.minimum(stage + 1, last)

    def send_y(m):
        return pltpu.make_async_remote_copy(
            src_ref=y_ref.at[m], dst_ref=h_ref.at[m], send_sem=ysend_sem.at[m], recv_sem=yrecv_sem.at[m],
            device_id={"pipe": after}, device_id_type=MESH)

    def send_g(m):
        return pltpu.make_async_remote_copy(
            src_ref=gb_ref.at[m], dst_ref=g_ref.at[m], send_sem=gsend_sem.at[m], recv_sem=grecv_sem.at[m],
            device_id={"pipe": before}, device_id_type=MESH)

    def load_h(m):
        return pltpu.make_async_copy(x_any.at[pl.ds(m * rows, rows)], h_ref.at[m], h_sem.at[m])

    def load_g(m):
        return pltpu.make_async_copy(ct_any.at[pl.ds(m * rows, rows)], g_ref.at[m], g_sem.at[m])

    def store(src, dst, sem, m, slot):
        return pltpu.make_async_copy(src.at[slot], dst.at[pl.ds(m * rows, rows)], sem.at[slot])

    filled = ((aw_any, aw), (ow_any, ow), (ew_any, ew), (rw_any, rw))

    def load_w(k):
        return pltpu.make_async_copy(filled[k][0], filled[k][1], w_sem.at[k])

    load_w(0).start()

    @pl.when(stage == 0)
    def _():
        for m in range(micro):
            load_h(m).start()

    for k in range(1, 4):
        load_w(k).start()

    @pl.when(stage == last)
    def _():
        for m in range(micro):
            load_g(m).start()

    barrier = pltpu.get_barrier_semaphore()

    @pl.when(stage > 0)
    def _():
        pl.semaphore_signal(barrier, inc=1, device_id={"pipe": before}, device_id_type=MESH)

    @pl.when(stage < last)
    def _():
        pl.semaphore_signal(barrier, inc=1, device_id={"pipe": after}, device_id_type=MESH)

    load_w(0).wait()
    inside = (stage > 0) & (stage < last)

    @pl.when(inside)
    def _():
        pl.semaphore_wait(barrier, 2)

    @pl.when(jnp.logical_not(inside))
    def _():
        pl.semaphore_wait(barrier, 1)

    sums[...] = jnp.zeros_like(sums)
    ab[:, :width] = ab_in[:, :width].astype(f32)
    ab[:, width:2 * width] = jnp.zeros((1, width), f32)
    ab[:, 2 * width:] = ab_in[:, width:].astype(f32)
    for dst, src in ((ob, ob_in), (g1, g1_in), (s1, s1_in), (eb, eb_in), (rb, rb_in), (g2, g2_in), (s2, s2_in)):
        dst[...] = src[...].astype(f32)
    position = lax.broadcasted_iota(jnp.int32, (1, slots), 1)
    for seq in range(regions.shape[0]):
        known = (position < lengths[seq]) | (regions[seq:seq + 1, :] == 1)
        usable[seq] = jnp.broadcast_to(known.astype(f32), (8, slots))
    lane = lax.broadcasted_iota(jnp.int32, (slots, 128), 1)
    first_half = lane < 64

    def stack(v):
        zero = jnp.zeros_like(v)
        return jnp.concatenate([jnp.where(first_half, v, zero), jnp.where(first_half, zero, v)], 0)

    def unstack(v):
        return jnp.where(first_half, v[:slots], v[slots:])

    o_g2, o_s2, o_rb = 0, width, 2 * width
    o_eb = 3 * width
    o_g1 = o_eb + hidden
    o_s1 = o_g1 + width
    o_ob = o_s1 + width
    o_q = o_ob + width
    o_v = o_q + width

    staged_f = ((ctx, ctx_out, ctx_sem), (low, low_out, low_sem), (act, act_out, act_sem))
    staged_b = ((gred, gred_out, gred_sem), (gexp, gexp_out, gexp_sem), (gatt, gatt_out, gatt_sem),
                (gproj, gproj_out, gproj_sem), (gin, gin_out, gin_sem))

    combos = [(g, p) for p in range(pairs) for g in range(groups)]
    blocks = [slice(b, b + BLOCK) for b in range(0, rows, BLOCK)]

    def part_of(m, g, p, which):
        at = which * width + p * 128
        return qkv[m, g * slots:(g + 1) * slots, at:at + 128]

    def stats():
        means = [jnp.mean(acc[bs, :], -1, keepdims=True) for bs in blocks]
        parts = [acc[bs, :] - mean for bs, mean in zip(blocks, means)]
        return means, [lax.rsqrt(jnp.mean(c * c, -1, keepdims=True) + epsilon) for c in parts]

    def forward(m):
        slot = lax.rem(m, 2)

        @pl.when(stage == 0)
        def _():
            load_h(m).wait()

        @pl.when(stage > 0)
        def _():
            send_y(m).wait_recv()

        store(h_ref, h_out, hs_sem, m, m).start()

        @pl.when(m >= 2)
        def _():
            for src, dst, sem in staged_f:
                store(src, dst, sem, m - 2, slot).wait()

        h = h_ref[m]
        for c in range(0, 3 * width, 256):
            p = nn(h, aw[:, c:c + 256]) + ab[:, c:c + 256]
            if c < width:
                p = p * 0.125
            qkv[m, :, c:c + 256] = p.astype(bf16)
        oks = [usable[m * groups + g, 0:1, :] > 0 for g in range(groups)]
        ss = [jnp.where(oks[g], nt(stack(part_of(m, g, p, 0)), part_of(m, g, p, 1)), neg_large) for g, p in combos]
        tops = [jnp.max(s, -1, keepdims=True) for s in ss]
        es = [jnp.exp(s - top) for s, top in zip(ss, tops)]
        invs = [1.0 / jnp.sum(e, -1, keepdims=True) for e in es]
        for (g, p), e, inv in zip(combos, es, invs):
            shares[m, g * pairs + p] = (e * inv).astype(bf16)
        os = [nn(shares[m, g * pairs + p], part_of(m, g, p, 2)) for g, p in combos]
        for (g, p), o in zip(combos, os):
            ctx[slot, g * slots:(g + 1) * slots, p * 128:(p + 1) * 128] = unstack(o).astype(bf16)
        store(ctx, ctx_out, ctx_sem, m, slot).start()

        @pl.when((m == 0) & (stage == 0))
        def _():
            for k in range(1, 4):
                load_w(k).wait()

        c_all = ctx[slot]
        for c in range(0, width, 256):
            acc[:, c:c + 256] = nn(c_all, ow[:, c:c + 256]) + ob[:, c:c + 256]
        for bs in blocks:
            acc[bs, :] += h_ref[m, bs, :].astype(f32)
        for bs, mean, inv in zip(blocks, *stats()):
            normed = (acc[bs, :] - mean) * inv
            out = normed * g1[...] + s1[...]
            n1[m, bs, :] = normed.astype(bf16)
            r1[m, bs, :] = jnp.broadcast_to(inv, (BLOCK, 128))
            mid[bs, :] = out
            low[slot, bs, :] = out.astype(bf16)
        store(low, low_out, low_sem, m, slot).start()
        def widen(c):
            fresh[c // CHUNK % 2] = nn(low[slot], ew[:, c:c + CHUNK])

        def narrow(c):
            acc[...] += nn(act[slot, :, c:c + CHUNK], rw[c:c + CHUNK, :])

        widen(0)
        for c in range(0, hidden, CHUNK):
            if c + CHUNK < hidden:
                widen(c + CHUNK)
            if c > 0:
                narrow(c - CHUNK)
            else:
                acc[...] = mid[...] + rb[...]
            a, d = gelu_pair(fresh[c // CHUNK % 2] + eb[:, c:c + CHUNK])
            act[slot, :, c:c + CHUNK] = a.astype(bf16)
            gp[m, :, c:c + CHUNK] = d.astype(bf16)
        store(act, act_out, act_sem, m, slot).start()
        narrow(hidden - CHUNK)
        for bs, mean, inv in zip(blocks, *stats()):
            normed = (acc[bs, :] - mean) * inv
            n2[m, bs, :] = normed.astype(bf16)
            r2[m, bs, :] = jnp.broadcast_to(inv, (BLOCK, 128))
            y_ref[m, bs, :] = (normed * g2[...] + s2[...]).astype(bf16)

        @pl.when(stage < last)
        def _():
            send_y(m).start()

        store(y_ref, y_out, y_sem, m, m).start()

    def norm_back(grad, normed, inv, gain, first, second):
        return inv * (grad * gain - first - normed * second)

    def norm_sums(grad, normed, gain):
        scaled = grad * gain
        return jnp.mean(scaled, -1, keepdims=True), jnp.mean(scaled * normed, -1, keepdims=True)

    def backward(m):
        slot = lax.rem(m, 2)

        @pl.when(stage == last)
        def _():
            load_g(m).wait()

        @pl.when(stage < last)
        def _():
            send_g(m).wait_recv()

        @pl.when(m >= 2)
        def _():
            for src, dst, sem in staged_b:
                store(src, dst, sem, m - 2, slot).wait()

        pairs_of = [norm_sums(g_ref[m, bs, :].astype(f32), n2[m, bs, :].astype(f32), g2[...]) for bs in blocks]
        for bs, (one, two) in zip(blocks, pairs_of):
            go = g_ref[m, bs, :].astype(f32)
            normed = n2[m, bs, :].astype(f32)
            mix = norm_back(go, normed, r2[m, bs, 0:1], g2[...], one, two)
            mid[bs, :] = mix
            gred[slot, bs, :] = mix.astype(bf16)
            sums[:, o_g2:o_g2 + width] += fold(go * normed)
            sums[:, o_s2:o_s2 + width] += fold(go)
            sums[:, o_rb:o_rb + width] += fold(mix)
        store(gred, gred_out, gred_sem, m, slot).start()
        r_all = gred[slot]
        for c in range(0, hidden, CHUNK):
            ge = nn(r_all, rwt[:, c:c + CHUNK]) * gp[m, :, c:c + CHUNK].astype(f32)
            gexp[slot, :, c:c + CHUNK] = ge.astype(bf16)
            sums[:, o_eb + c:o_eb + c + CHUNK] += fold(ge)
        store(gexp, gexp_out, gexp_sem, m, slot).start()
        e_all = gexp[slot]
        for c in range(0, width, 256):
            acc[:, c:c + 256] = nn(e_all, ewt[:, c:c + 256])
        for bs in blocks:
            acc[bs, :] += mid[bs, :]
        pairs_of = [norm_sums(acc[bs, :], n1[m, bs, :].astype(f32), g1[...]) for bs in blocks]
        for bs, (one, two) in zip(blocks, pairs_of):
            gf = acc[bs, :]
            normed = n1[m, bs, :].astype(f32)
            gm = norm_back(gf, normed, r1[m, bs, 0:1], g1[...], one, two)
            mid[bs, :] = gm
            gatt[slot, bs, :] = gm.astype(bf16)
            sums[:, o_g1:o_g1 + width] += fold(gf * normed)
            sums[:, o_s1:o_s1 + width] += fold(gf)
            sums[:, o_ob:o_ob + width] += fold(gm)
        store(gatt, gatt_out, gatt_sem, m, slot).start()
        t_all = gatt[slot]
        for c in range(0, width, 256):
            gctx[:, c:c + 256] = nn(t_all, owt[:, c:c + 256]).astype(bf16)

        def gc_of(g, p):
            return stack(gctx[g * slots:(g + 1) * slots, p * 128:(p + 1) * 128])

        def put(g, p, which, v):
            at = which * width + p * 128
            gproj[slot, g * slots:(g + 1) * slots, at:at + 128] = v.astype(bf16)

        gss = [nt(gc_of(g, p), part_of(m, g, p, 2)) for g, p in combos]
        gvs = [tn(shares[m, g * pairs + p], gc_of(g, p)) for g, p in combos]
        dots = [jnp.sum(gs * shares[m, g * pairs + p].astype(f32), -1, keepdims=True) for (g, p), gs in zip(combos, gss)]
        gscs = [(shares[m, g * pairs + p].astype(f32) * (gs - d)).astype(bf16)
                for (g, p), gs, d in zip(combos, gss, dots)]
        gqs = [unstack(nn(gsc, part_of(m, g, p, 1))) * 0.125 for (g, p), gsc in zip(combos, gscs)]
        gks = [tn(gsc, stack(part_of(m, g, p, 0))) for (g, p), gsc in zip(combos, gscs)]
        for (g, p), gq, gk, gv in zip(combos, gqs, gks, gvs):
            put(g, p, 0, gq)
            put(g, p, 1, gk)
            put(g, p, 2, gv)
            sums[:, o_q + p * 128:o_q + (p + 1) * 128] += fold(gq)
            sums[:, o_v + p * 128:o_v + (p + 1) * 128] += fold(gv)
        store(gproj, gproj_out, gproj_sem, m, slot).start()
        p_all = gproj[slot]
        for c in range(0, width, 256):
            gi = nn(p_all, awt[:, c:c + 256]) + mid[:, c:c + 256]
            gin[slot, :, c:c + 256] = gi
            gb_ref[m, :, c:c + 256] = gi.astype(bf16)

        @pl.when(stage > 0)
        def _():
            send_g(m).start()

        store(gin, gin_out, gin_sem, m, slot).start()

    lag = jnp.where(stage == last, 0, micro - 1)

    def turn():
        @pl.when(stage > 0)
        def _():
            for k in range(1, 4):
                load_w(k).wait()

        one = (lax.broadcasted_iota(jnp.int32, (256, 256), 0) == lax.broadcasted_iota(jnp.int32, (256, 256), 1)).astype(f32).astype(bf16)
        for src, dst in ((aw, awt), (ow, owt), (ew, ewt), (rw, rwt)):
            def across(k, carry, src=src, dst=dst):
                cols = pl.ds(pl.multiple_of(k * 256, 256), 256)
                for r in range(0, dst.shape[0], 256):
                    dst[r:r + 256, cols] = nt(one, src[cols, r:r + 256]).astype(bf16)
                return carry

            lax.fori_loop(0, src.shape[0] // 256, across, 0)

    def tick(t, carry):
        @pl.when((t >= 1) & (t <= micro))
        def _():
            forward(jnp.clip(t - 1, 0, micro - 1))

        @pl.when(t == jnp.where(stage > 0, 0, lag + 1))
        def _():
            turn()

        @pl.when((t >= lag + 1) & (t <= lag + micro))
        def _():
            backward(jnp.clip(t - 1 - lag, 0, micro - 1))

        return carry

    lax.fori_loop(0, 2 * micro, tick, 0)

    for m in range(micro):
        store(h_ref, h_out, hs_sem, m, m).wait()
        store(y_ref, y_out, y_sem, m, m).wait()

        @pl.when(stage < last)
        def _():
            send_y(m).wait_send()

        @pl.when(stage > 0)
        def _():
            send_g(m).wait_send()

    for m in range(max(0, micro - 2), micro):
        for src, dst, sem in staged_f + staged_b:
            store(src, dst, sem, m, m % 2).wait()


def run_pipeline(rows_in, tangents, lengths, regions, weights, vectors):
    total, width = rows_in.shape
    slots = regions.shape[1]
    rows = GROUP * slots
    micro = total // rows
    aw, ow, ew, rw = weights
    hidden = ew.shape[1]
    pairs = width // 128
    wide = 3 * width
    sum_width = 8 * width + hidden
    hbm = pl.BlockSpec(memory_space=pl.ANY)
    vmem = pl.BlockSpec(memory_space=pltpu.VMEM)
    dma = pltpu.SemaphoreType.DMA
    shape = jax.ShapeDtypeStruct
    flops = 4 * total * (4 * width * width + 2 * width * hidden)
    return pl.pallas_call(
        functools.partial(pipeline_kernel, micro),
        out_shape=(
            shape((total, width), bf16), shape((total, width), f32), shape((total, width), bf16),
            shape((total, width), bf16), shape((total, width), bf16), shape((total, hidden), bf16),
            shape((total, width), bf16), shape((total, hidden), bf16), shape((total, width), bf16),
            shape((total, wide), bf16), shape((8, sum_width), f32),
        ),
        in_specs=[hbm, hbm, pl.BlockSpec(memory_space=pltpu.SMEM), vmem] + [hbm] * 4 + [vmem] * 8,
        out_specs=(hbm,) * 10 + (vmem,),
        scratch_shapes=[pltpu.VMEM(w.shape, bf16) for w in weights] + [pltpu.VMEM(w.shape[::-1], bf16) for w in weights] + [pltpu.VMEM((regions.shape[0], 8, slots), f32), pltpu.VMEM((rows, width), bf16), pltpu.VMEM((2, rows, CHUNK), f32)] + [pltpu.VMEM((1, n), f32) for n in (wide, width, width, width, hidden, width, width, width)] + [
            pltpu.VMEM((micro, rows, width), bf16),
            pltpu.VMEM((micro, rows, width), bf16),
            pltpu.VMEM((micro, rows, width), bf16),
            pltpu.VMEM((micro, rows, width), bf16),
            pltpu.VMEM((micro, rows, wide), bf16),
            pltpu.VMEM((micro, GROUP * pairs, 2 * slots, slots), bf16),
            pltpu.VMEM((micro, rows, hidden), bf16),
            pltpu.VMEM((micro, rows, width), bf16),
            pltpu.VMEM((micro, rows, 128), f32),
            pltpu.VMEM((micro, rows, width), bf16),
            pltpu.VMEM((micro, rows, 128), f32),
            pltpu.VMEM((2, rows, width), bf16),
            pltpu.VMEM((2, rows, width), bf16),
            pltpu.VMEM((2, rows, hidden), bf16),
            pltpu.VMEM((2, rows, width), bf16),
            pltpu.VMEM((2, rows, hidden), bf16),
            pltpu.VMEM((2, rows, width), bf16),
            pltpu.VMEM((2, rows, wide), bf16),
            pltpu.VMEM((2, rows, width), f32),
            pltpu.VMEM((rows, width), f32),
            pltpu.VMEM((rows, width), f32),
        ] + [dma((4,))] + [dma((micro,))] * 8 + [dma((2,))] * 8,
        compiler_params=pltpu.CompilerParams(
            collective_id=0, has_side_effects=True, vmem_limit_bytes=63 * 1024 * 1024),
        cost_estimate=pl.CostEstimate(flops=flops, bytes_accessed=40_000_000, transcendentals=total * hidden),
    )(rows_in, tangents, lengths, regions, aw, ow, ew, rw, *vectors)


def sum_kernel(
    dp, act_any, gred_any, low_any, gexp_any, h_any, gproj_any, ctx_any, gatt_any, sums_in,
    total, vector,
    part, left, right, vec_in, *rest,
):
    steps = dp.bit_length() - 1
    plane = steps - 1
    landed = rest[:steps]
    left_sem, right_sem, send_sem, recv_sem, vsend_sem, vrecv_sem, out_sem = rest[steps:]
    units, rows, cols = part.shape
    me = lax.axis_index("dp")
    hid_blocks = act_any.shape[1] // cols
    wide_blocks = gproj_any.shape[1] // cols
    sources = (
        [(act_any, k, gred_any, 0) for k in range(hid_blocks)]
        + [(low_any, 0, gexp_any, k) for k in range(hid_blocks)]
        + [(h_any, 0, gproj_any, k) for k in range(wide_blocks)]
        + [(ctx_any, 0, gatt_any, 0)]
    )

    def bit_of(mask):
        return lax.rem(me // mask, 2)

    def masks_of(step):
        if step == 0:
            return 1, 1
        return 2 ** (1 + (step - 1) % plane), 2 ** (1 + (step - 1 + plane // 2) % plane)

    def place(unit, step):
        parity = lax.rem(unit, 2)
        first, second = masks_of(step)
        mask = first + parity * (second - first)
        bit = bit_of(first) + parity * (bit_of(second) - bit_of(first))
        return bit, me + mask * (1 - 2 * bit)

    def base(unit, step):
        start, size = 0, rows
        for k in range(step):
            size = size // 2
            start = start + place(unit, k)[0] * size
        return start, size

    def ds(start, size):
        return pl.ds(pl.multiple_of(start, 16), size)

    def reduce_copy(unit, step):
        bit, peer = place(unit, step)
        start, size = base(unit, step)
        half = size // 2
        return pltpu.make_async_remote_copy(
            src_ref=part.at[unit, ds(start + (1 - bit) * half, half)], dst_ref=landed[step].at[unit],
            send_sem=send_sem.at[step, unit], recv_sem=recv_sem.at[step, unit],
            device_id={"dp": peer}, device_id_type=MESH)

    def gather_copy(unit, step):
        peer = place(unit, step)[1]
        start, size = base(unit, step + 1)
        where = 2 * steps - 1 - step
        own = part if step == steps - 1 else total
        return pltpu.make_async_remote_copy(
            src_ref=own.at[unit, ds(start, size)], dst_ref=total.at[unit, ds(start, size)],
            send_sem=send_sem.at[where, unit], recv_sem=recv_sem.at[where, unit],
            device_id={"dp": peer}, device_id_type=MESH)

    def gather_arrival(unit, step):
        bit, peer = place(unit, step)
        start, size = base(unit, step)
        half = size // 2
        where = 2 * steps - 1 - step
        there = ds(start + (1 - bit) * half, half)
        return pltpu.make_async_remote_copy(
            src_ref=total.at[unit, there], dst_ref=total.at[unit, there],
            send_sem=send_sem.at[where, unit], recv_sem=recv_sem.at[where, unit],
            device_id={"dp": peer}, device_id_type=MESH)

    def keep(unit):
        start, size = base(unit, steps)
        rs = ds(start, size)
        return pltpu.make_async_copy(part.at[unit, rs], total.at[unit, rs], out_sem.at[unit])

    def vector_copy(step):
        peer = me + 2 ** step * (1 - 2 * bit_of(2 ** step))
        return pltpu.make_async_remote_copy(
            src_ref=vec_in.at[2 * step], dst_ref=vec_in.at[2 * step + 1],
            send_sem=vsend_sem.at[step], recv_sem=vrecv_sem.at[step],
            device_id={"dp": peer}, device_id_type=MESH)

    def loads(k, slot):
        a, ka, b, kb = sources[k]
        return (
            pltpu.make_async_copy(a.at[:, pl.ds(ka * cols, cols)], left.at[slot], left_sem.at[slot]),
            pltpu.make_async_copy(b.at[:, pl.ds(kb * cols, cols)], right.at[slot], right_sem.at[slot]),
        )

    for copy in loads(0, 0):
        copy.start()
    barrier = pltpu.get_barrier_semaphore()
    for step in range(steps):
        peer = me + 2 ** step * (1 - 2 * bit_of(2 ** step))
        pl.semaphore_signal(barrier, inc=1, device_id={"dp": peer}, device_id_type=MESH)
    v = jnp.sum(sums_in[...], 0, keepdims=True)
    lanes = vec_in.shape[2]
    for r in range(8):
        vec_in[0, r:r + 1, :] = v[:, r * lanes:(r + 1) * lanes]
    pl.semaphore_wait(barrier, steps)

    def add(unit, step):
        start, size = base(unit, step + 1)
        for b in range(0, size, 96):
            n = min(96, size - b)
            rs = ds(start + b, n)
            s = part[unit, rs, :].astype(f32) + landed[step][unit, b:b + n, :].astype(f32)
            part[unit, rs, :] = s.astype(bf16)

    def when_unit(unit, body):
        @pl.when((unit >= 0) & (unit < units))
        def _():
            body(unit)

    def make(unit):
        for s in range(rows // cols):
            block = unit * (rows // cols) + s
            slot = lax.rem(block, 2)
            for k in range(len(sources)):
                @pl.when(block == k)
                def _():
                    if k + 1 < len(sources):
                        for copy in loads(k + 1, (k + 1) % 2):
                            copy.start()
                    for copy in loads(k, k % 2):
                        copy.wait()
            for r in range(0, cols, 256):
                part[unit, s * cols + r:s * cols + r + 256, :] = tn(left[slot, :, r:r + 256], right[slot]).astype(bf16)
        reduce_copy(unit, 0).start()

    def reduce_next(step):
        def body(unit):
            reduce_copy(unit, step).wait_recv()
            add(unit, step)
            if step + 1 < steps:
                reduce_copy(unit, step + 1).start()
            else:
                gather_copy(unit, step).start()
                keep(unit).start()
        return body

    def gather_next(step):
        def body(unit):
            gather_arrival(unit, step).wait_recv()
            if step == steps - 1:
                keep(unit).wait()
            if step > 0:
                gather_copy(unit, step - 1).start()
        return body

    lag = 0
    lags = []
    for step in range(steps):
        lag += 1 if step == 0 else 2
        lags.append((lag, reduce_next(step)))
    for step in reversed(range(steps)):
        lag += 2
        lags.append((lag, gather_next(step)))

    def tick(t, carry):
        when_unit(t, make)
        for behind, body in lags:
            when_unit(t - behind, body)
        for step in range(steps):
            @pl.when(t == 2 + 2 * step)
            def _():
                if step > 0:
                    vector_copy(step - 1).wait_recv()
                    vec_in[2 * step] = vec_in[2 * step - 2] + vec_in[2 * step - 1]
                vector_copy(step).start()

        return carry

    lax.fori_loop(0, units + lag, tick, 0)
    vector_copy(steps - 1).wait_recv()
    vector[...] = vec_in[2 * steps - 2] + vec_in[2 * steps - 1]

    def finish(unit, carry):
        for step in range(steps):
            reduce_copy(unit, step).wait_send()
            gather_copy(unit, step).wait_send()
        return carry

    lax.fori_loop(0, units, finish, 0)
    for step in range(steps):
        vector_copy(step).wait_send()


def write_kernel(hid_blocks, wide_blocks, total, vector_any, y, gin, y_g, gin_g, aw_g, ab_g, ow_g, ob_g, g1_g, s1_g, ew_g, eb_g, rw_g, rb_g, g2_g, s2_g, taken, given, y_buf, gin_buf, vector, move_sem, in_sem, out_sem):
    depth, rows, cols = taken.shape
    places = (
        [(rw_g, k, 0) for k in range(hid_blocks)] + [(ew_g, 0, k) for k in range(hid_blocks)]
        + [(aw_g, 0, k) for k in range(wide_blocks)] + [(ow_g, 0, 0)]
    )
    split, span = cols // rows, total.shape[1] // cols
    chunks = [(block, part) for block in range(len(places)) for part in range(split)]

    def bring(k):
        block, part = chunks[k]
        start = (block % span) * cols + part * rows
        return pltpu.make_async_copy(total.at[block // span, pl.ds(start, rows)], taken.at[k % depth], in_sem.at[k % depth])

    def give(k):
        block, part = chunks[k]
        out, i, j = places[block]
        target = out.at[pl.ds(i * cols + part * rows, rows), pl.ds(j * cols, cols)]
        return pltpu.make_async_copy(given.at[k % depth], target, out_sem.at[k % depth])

    ins = (pltpu.make_async_copy(y, y_buf, move_sem.at[0]), pltpu.make_async_copy(gin, gin_buf, move_sem.at[1]))
    outs = (pltpu.make_async_copy(y_buf, y_g, move_sem.at[2]), pltpu.make_async_copy(gin_buf, gin_g, move_sem.at[3]))
    vector_copy = pltpu.make_async_copy(vector_any, vector, move_sem.at[4])
    vector_copy.start()
    for k in range(depth):
        bring(k).start()
    for move in ins:
        move.start()
    vector_copy.wait()
    piece = vector.shape[1] // 3
    at = 0
    for out in (g2_g, s2_g, rb_g, eb_g, g1_g, s1_g, ob_g, ab_g):
        for k in range(out.shape[1] // piece):
            r, c = at // 3, at % 3
            out[:, k * piece:(k + 1) * piece] = vector[r:r + 1, c * piece:(c + 1) * piece]
            at += 1
    for k in range(len(chunks)):
        bring(k).wait()
        if k >= depth:
            give(k - depth).wait()
        given[k % depth] = taken[k % depth].astype(f32)
        give(k).start()
        if k + depth < len(chunks):
            bring(k + depth).start()
        if k == depth:
            for arrived, move in zip(ins, outs):
                arrived.wait()
                move.start()
    for k in range(len(chunks) - depth, len(chunks)):
        give(k).wait()
    for move in outs:
        move.wait()


def run_sums(parts, sums, y, gin, dp):
    act, gred, low, gexp, h, gproj, ctx, gatt = parts
    total_rows, width = h.shape
    hidden, wide = act.shape[1], gproj.shape[1]
    hid_blocks, wide_blocks = hidden // width, wide // width
    blocks = 2 * hid_blocks + wide_blocks + 1
    steps = dp.bit_length() - 1
    span = 1
    while span * width % (16 * dp):
        span *= 2
    units, unit_rows = blocks // span, span * width
    lanes = sums.shape[1] // 8
    hbm = pl.BlockSpec(memory_space=pl.ANY)
    vmem = pl.BlockSpec(memory_space=pltpu.VMEM)
    dma = pltpu.SemaphoreType.DMA
    shape = jax.ShapeDtypeStruct
    total, vector = pl.pallas_call(
        functools.partial(sum_kernel, dp),
        out_shape=(shape((units, unit_rows, width), bf16), shape((8, lanes), f32)),
        in_specs=[hbm] * 8 + [vmem],
        out_specs=(hbm, vmem),
        scratch_shapes=[
            pltpu.VMEM((units, unit_rows, width), bf16),
            pltpu.VMEM((2, total_rows, width), bf16),
            pltpu.VMEM((2, total_rows, width), bf16),
            pltpu.VMEM((2 * steps, 8, lanes), f32),
        ] + [pltpu.VMEM((units, unit_rows // 2 ** (k + 1), width), bf16) for k in range(steps)] + [
            dma((2,)), dma((2,)), dma((2 * steps, units)), dma((2 * steps, units)), dma((steps,)), dma((steps,)), dma((units,)),
        ],
        compiler_params=pltpu.CompilerParams(
            collective_id=1, has_side_effects=True, vmem_limit_bytes=58 * 1024 * 1024),
    )(act, gred, low, gexp, h, gproj, ctx, gatt, sums)

    def one(count):
        return shape((1, count), f32), vmem

    outs = [
        (shape(y.shape, y.dtype), hbm), (shape(gin.shape, gin.dtype), hbm),
        (shape((width, wide), f32), hbm),
        one(2 * width),
        (shape((width, width), f32), hbm),
        one(width), one(width), one(width),
        (shape((width, hidden), f32), hbm),
        one(hidden),
        (shape((hidden, width), f32), hbm),
        one(width), one(width), one(width),
    ]
    return pl.pallas_call(
        functools.partial(write_kernel, hid_blocks, wide_blocks),
        out_shape=tuple(o[0] for o in outs),
        in_specs=[hbm] * 4,
        out_specs=tuple(o[1] for o in outs),
        scratch_shapes=[
            pltpu.VMEM((PARTS, width // 2, width), bf16), pltpu.VMEM((PARTS, width // 2, width), f32),
            pltpu.VMEM(y.shape, y.dtype), pltpu.VMEM(gin.shape, gin.dtype),
            pltpu.VMEM((8, lanes), f32), dma((5,)), dma((PARTS,)), dma((PARTS,)),
        ],
        compiler_params=pltpu.CompilerParams(vmem_limit_bytes=52 * 1024 * 1024),
    )(total, vector, y, gin)


def local(
    layer_input, lengths, regions, cotangent,
    attend_weight, attend_bias, output_weight, output_bias, first_gain, first_shift,
    expand_weight, expand_bias, reduce_weight, reduce_bias, second_gain, second_shift,
):
    seqs, slots, width = layer_input.shape
    total = seqs * slots
    vectors = (attend_bias, output_bias, first_gain, first_shift, expand_bias, reduce_bias, second_gain, second_shift)
    weights = (attend_weight[0], output_weight[0], expand_weight[0], reduce_weight[0])
    y, gin, h, ctx, low, act, gred, gexp, gatt, gproj, sums = run_pipeline(
        layer_input.reshape(total, width), cotangent.reshape(total, width), lengths, regions, weights, vectors)
    y, gin, *grads = run_sums((act, gred, low, gexp, h, gproj, ctx, gatt), sums, y, gin, lax.axis_size("dp"))
    return (y.reshape(1, seqs, slots, width), gin.reshape(1, seqs, slots, width)) + tuple(
        g[None] if g.shape[0] > 1 else g for g in grads)


def solution(mesh):
    rows = P("dp", None, None)
    cube = P("pipe", None, None)
    flat = P("pipe", None)
    grads = P("pipe", "dp", None, None)
    return jax.shard_map(
        local,
        mesh=mesh,
        in_specs=(rows, P("dp"), P("dp", None), rows, cube, flat, cube, flat, flat, flat, cube, flat, cube, flat, flat, flat),
        out_specs=(grads, grads, cube, flat, cube, flat, flat, flat, cube, flat, cube, flat, flat, flat),
        check_vma=False,
    )
```

```python
import functools

import jax
import jax.numpy as jnp
from jax import lax
from jax.experimental import pallas as pl
from jax.experimental.pallas import tpu as pltpu
from jax.sharding import PartitionSpec as P

HEADS = 12
GROUP = 1
BLOCK = 32
CHUNK = 512
PARTS = 4
epsilon = 1e-05
neg_large = -1000000000.0
MESH = pl.DeviceIdType.MESH
f32 = jnp.float32
bf16 = jnp.bfloat16


def nn(left, right):
    return jnp.dot(left, right, preferred_element_type=f32)


def nt(left, right):
    return lax.dot_general(left, right, (((1,), (1,)), ((), ())), preferred_element_type=f32)


def tn(left, right):
    return lax.dot_general(left, right, (((0,), (0,)), ((), ())), preferred_element_type=f32)


def gelu_pair(x):
    phi = 0.5 + 0.5 * lax.erf(x * 0.7071067811865476)
    return x * phi, phi + (x * 0.3989422804014327) * jnp.exp2((x * x) * -0.7213475204444817)


def fold(v):
    rows, cols = v.shape
    return jnp.sum(v.reshape(rows // 8, 8, cols), 0)


def pipeline_kernel(
    micro,
    x_any, ct_any, lengths, regions, aw_any, ow_any, ew_any, rw_any, ab_in, ob_in, g1_in, s1_in, eb_in, rb_in, g2_in, s2_in,
    y_out, gin_out, h_out, ctx_out, low_out, act_out, gred_out, gexp_out, gatt_out, gproj_out, sums,
    aw, ow, ew, rw, awt, owt, ewt, rwt, usable, gctx, fresh, ab, ob, g1, s1, eb, rb, g2, s2,
    h_ref, g_ref, y_ref, gb_ref, qkv, shares, gp, n1, r1, n2, r2,
    ctx, low, act, gred, gexp, gatt, gproj, gin, acc, mid,
    w_sem, h_sem, g_sem, ysend_sem, yrecv_sem, gsend_sem, grecv_sem, y_sem, hs_sem,
    ctx_sem, low_sem, act_sem, gred_sem, gexp_sem, gatt_sem, gproj_sem, gin_sem,
):
    stage = lax.axis_index("pipe")
    count = lax.axis_size("pipe")
    last = count - 1
    slots = regions.shape[1]
    rows = h_ref.shape[1]
    groups = rows // slots
    width = h_ref.shape[2]
    hidden = ew.shape[1]
    pairs = width // 128
    before = jnp.maximum(stage - 1, 0)
    after = jnp.minimum(stage + 1, last)

    def send_y(m):
        return pltpu.make_async_remote_copy(
            src_ref=y_ref.at[m], dst_ref=h_ref.at[m], send_sem=ysend_sem.at[m], recv_sem=yrecv_sem.at[m],
            device_id={"pipe": after}, device_id_type=MESH)

    def send_g(m):
        return pltpu.make_async_remote_copy(
            src_ref=gb_ref.at[m], dst_ref=g_ref.at[m], send_sem=gsend_sem.at[m], recv_sem=grecv_sem.at[m],
            device_id={"pipe": before}, device_id_type=MESH)

    def load_h(m):
        return pltpu.make_async_copy(x_any.at[pl.ds(m * rows, rows)], h_ref.at[m], h_sem.at[m])

    def load_g(m):
        return pltpu.make_async_copy(ct_any.at[pl.ds(m * rows, rows)], g_ref.at[m], g_sem.at[m])

    def store(src, dst, sem, m, slot):
        return pltpu.make_async_copy(src.at[slot], dst.at[pl.ds(m * rows, rows)], sem.at[slot])

    filled = ((aw_any, aw), (ow_any, ow), (ew_any, ew), (rw_any, rw))

    def load_w(k):
        return pltpu.make_async_copy(filled[k][0], filled[k][1], w_sem.at[k])

    load_w(0).start()

    @pl.when(stage == 0)
    def _():
        for m in range(micro):
            load_h(m).start()

    for k in range(1, 4):
        load_w(k).start()

    @pl.when(stage == last)
    def _():
        for m in range(micro):
            load_g(m).start()

    barrier = pltpu.get_barrier_semaphore()

    @pl.when(stage > 0)
    def _():
        pl.semaphore_signal(barrier, inc=1, device_id={"pipe": before}, device_id_type=MESH)

    @pl.when(stage < last)
    def _():
        pl.semaphore_signal(barrier, inc=1, device_id={"pipe": after}, device_id_type=MESH)

    load_w(0).wait()
    inside = (stage > 0) & (stage < last)

    @pl.when(inside)
    def _():
        pl.semaphore_wait(barrier, 2)

    @pl.when(jnp.logical_not(inside))
    def _():
        pl.semaphore_wait(barrier, 1)

    sums[...] = jnp.zeros_like(sums)
    ab[:, :width] = ab_in[:, :width].astype(f32)
    ab[:, width:2 * width] = jnp.zeros((1, width), f32)
    ab[:, 2 * width:] = ab_in[:, width:].astype(f32)
    for dst, src in ((ob, ob_in), (g1, g1_in), (s1, s1_in), (eb, eb_in), (rb, rb_in), (g2, g2_in), (s2, s2_in)):
        dst[...] = src[...].astype(f32)
    position = lax.broadcasted_iota(jnp.int32, (1, slots), 1)
    for seq in range(regions.shape[0]):
        known = (position < lengths[seq]) | (regions[seq:seq + 1, :] == 1)
        usable[seq] = jnp.broadcast_to(known.astype(f32), (8, slots))
    lane = lax.broadcasted_iota(jnp.int32, (slots, 128), 1)
    first_half = lane < 64

    def stack(v):
        zero = jnp.zeros_like(v)
        return jnp.concatenate([jnp.where(first_half, v, zero), jnp.where(first_half, zero, v)], 0)

    def unstack(v):
        return jnp.where(first_half, v[:slots], v[slots:])

    o_g2, o_s2, o_rb = 0, width, 2 * width
    o_eb = 3 * width
    o_g1 = o_eb + hidden
    o_s1 = o_g1 + width
    o_ob = o_s1 + width
    o_q = o_ob + width
    o_v = o_q + width

    staged_f = ((ctx, ctx_out, ctx_sem), (low, low_out, low_sem), (act, act_out, act_sem))
    staged_b = ((gred, gred_out, gred_sem), (gexp, gexp_out, gexp_sem), (gatt, gatt_out, gatt_sem),
                (gproj, gproj_out, gproj_sem), (gin, gin_out, gin_sem))

    combos = [(g, p) for p in range(pairs) for g in range(groups)]
    blocks = [slice(b, b + BLOCK) for b in range(0, rows, BLOCK)]

    def part_of(m, g, p, which):
        at = which * width + p * 128
        return qkv[m, g * slots:(g + 1) * slots, at:at + 128]

    def stats():
        means = [jnp.mean(acc[bs, :], -1, keepdims=True) for bs in blocks]
        parts = [acc[bs, :] - mean for bs, mean in zip(blocks, means)]
        return means, [lax.rsqrt(jnp.mean(c * c, -1, keepdims=True) + epsilon) for c in parts]

    def forward(m):
        slot = lax.rem(m, 2)

        @pl.when(stage == 0)
        def _():
            load_h(m).wait()

        @pl.when(stage > 0)
        def _():
            send_y(m).wait_recv()

        store(h_ref, h_out, hs_sem, m, m).start()

        @pl.when(m >= 2)
        def _():
            for src, dst, sem in staged_f:
                store(src, dst, sem, m - 2, slot).wait()

        h = h_ref[m]
        for c in range(0, 3 * width, 256):
            p = nn(h, aw[:, c:c + 256]) + ab[:, c:c + 256]
            if c < width:
                p = p * 0.125
            qkv[m, :, c:c + 256] = p.astype(bf16)
        oks = [usable[m * groups + g, 0:1, :] > 0 for g in range(groups)]
        ss = [jnp.where(oks[g], nt(stack(part_of(m, g, p, 0)), part_of(m, g, p, 1)), neg_large) for g, p in combos]
        tops = [jnp.max(s, -1, keepdims=True) for s in ss]
        es = [jnp.exp(s - top) for s, top in zip(ss, tops)]
        invs = [1.0 / jnp.sum(e, -1, keepdims=True) for e in es]
        for (g, p), e, inv in zip(combos, es, invs):
            shares[m, g * pairs + p] = (e * inv).astype(bf16)
        os = [nn(shares[m, g * pairs + p], part_of(m, g, p, 2)) for g, p in combos]
        for (g, p), o in zip(combos, os):
            ctx[slot, g * slots:(g + 1) * slots, p * 128:(p + 1) * 128] = unstack(o).astype(bf16)
        store(ctx, ctx_out, ctx_sem, m, slot).start()

        @pl.when((m == 0) & (stage == 0))
        def _():
            for k in range(1, 4):
                load_w(k).wait()

        c_all = ctx[slot]
        for c in range(0, width, 256):
            acc[:, c:c + 256] = nn(c_all, ow[:, c:c + 256]) + ob[:, c:c + 256]
        for bs in blocks:
            acc[bs, :] += h_ref[m, bs, :].astype(f32)
        for bs, mean, inv in zip(blocks, *stats()):
            normed = (acc[bs, :] - mean) * inv
            out = normed * g1[...] + s1[...]
            n1[m, bs, :] = normed.astype(bf16)
            r1[m, bs, :] = jnp.broadcast_to(inv, (BLOCK, 128))
            mid[bs, :] = out
            low[slot, bs, :] = out.astype(bf16)
        store(low, low_out, low_sem, m, slot).start()
        def widen(c):
            fresh[c // CHUNK % 2] = nn(low[slot], ew[:, c:c + CHUNK])

        def narrow(c):
            acc[...] += nn(act[slot, :, c:c + CHUNK], rw[c:c + CHUNK, :])

        widen(0)
        for c in range(0, hidden, CHUNK):
            if c + CHUNK < hidden:
                widen(c + CHUNK)
            if c > 0:
                narrow(c - CHUNK)
            else:
                acc[...] = mid[...] + rb[...]
            a, d = gelu_pair(fresh[c // CHUNK % 2] + eb[:, c:c + CHUNK])
            act[slot, :, c:c + CHUNK] = a.astype(bf16)
            gp[m, :, c:c + CHUNK] = d.astype(bf16)
        store(act, act_out, act_sem, m, slot).start()
        narrow(hidden - CHUNK)
        for bs, mean, inv in zip(blocks, *stats()):
            normed = (acc[bs, :] - mean) * inv
            n2[m, bs, :] = normed.astype(bf16)
            r2[m, bs, :] = jnp.broadcast_to(inv, (BLOCK, 128))
            y_ref[m, bs, :] = (normed * g2[...] + s2[...]).astype(bf16)

        @pl.when(stage < last)
        def _():
            send_y(m).start()

        store(y_ref, y_out, y_sem, m, m).start()

    def norm_back(grad, normed, inv, gain, first, second):
        return inv * (grad * gain - first - normed * second)

    def norm_sums(grad, normed, gain):
        scaled = grad * gain
        return jnp.mean(scaled, -1, keepdims=True), jnp.mean(scaled * normed, -1, keepdims=True)

    def backward(m):
        slot = lax.rem(m, 2)

        @pl.when(stage == last)
        def _():
            load_g(m).wait()

        @pl.when(stage < last)
        def _():
            send_g(m).wait_recv()

        @pl.when(m >= 2)
        def _():
            for src, dst, sem in staged_b:
                store(src, dst, sem, m - 2, slot).wait()

        pairs_of = [norm_sums(g_ref[m, bs, :].astype(f32), n2[m, bs, :].astype(f32), g2[...]) for bs in blocks]
        for bs, (one, two) in zip(blocks, pairs_of):
            go = g_ref[m, bs, :].astype(f32)
            normed = n2[m, bs, :].astype(f32)
            mix = norm_back(go, normed, r2[m, bs, 0:1], g2[...], one, two)
            mid[bs, :] = mix
            gred[slot, bs, :] = mix.astype(bf16)
            sums[:, o_g2:o_g2 + width] += fold(go * normed)
            sums[:, o_s2:o_s2 + width] += fold(go)
            sums[:, o_rb:o_rb + width] += fold(mix)
        store(gred, gred_out, gred_sem, m, slot).start()
        def widen(c):
            fresh[c // CHUNK % 2] = nn(gred[slot], rwt[:, c:c + CHUNK])

        def narrow(c):
            acc[...] += nn(gexp[slot, :, c:c + CHUNK], ewt[c:c + CHUNK, :])

        widen(0)
        for c in range(0, hidden, CHUNK):
            if c + CHUNK < hidden:
                widen(c + CHUNK)
            if c > 0:
                narrow(c - CHUNK)
            else:
                acc[...] = mid[...]
            ge = fresh[c // CHUNK % 2] * gp[m, :, c:c + CHUNK].astype(f32)
            gexp[slot, :, c:c + CHUNK] = ge.astype(bf16)
            sums[:, o_eb + c:o_eb + c + CHUNK] += fold(ge)
        store(gexp, gexp_out, gexp_sem, m, slot).start()
        narrow(hidden - CHUNK)
        pairs_of = [norm_sums(acc[bs, :], n1[m, bs, :].astype(f32), g1[...]) for bs in blocks]
        for bs, (one, two) in zip(blocks, pairs_of):
            gf = acc[bs, :]
            normed = n1[m, bs, :].astype(f32)
            gm = norm_back(gf, normed, r1[m, bs, 0:1], g1[...], one, two)
            mid[bs, :] = gm
            gatt[slot, bs, :] = gm.astype(bf16)
            sums[:, o_g1:o_g1 + width] += fold(gf * normed)
            sums[:, o_s1:o_s1 + width] += fold(gf)
            sums[:, o_ob:o_ob + width] += fold(gm)
        store(gatt, gatt_out, gatt_sem, m, slot).start()
        t_all = gatt[slot]
        for c in range(0, width, 256):
            gctx[:, c:c + 256] = nn(t_all, owt[:, c:c + 256]).astype(bf16)

        def gc_of(g, p):
            return stack(gctx[g * slots:(g + 1) * slots, p * 128:(p + 1) * 128])

        def put(g, p, which, v):
            at = which * width + p * 128
            gproj[slot, g * slots:(g + 1) * slots, at:at + 128] = v.astype(bf16)

        gss = [nt(gc_of(g, p), part_of(m, g, p, 2)) for g, p in combos]
        gvs = [tn(shares[m, g * pairs + p], gc_of(g, p)) for g, p in combos]
        dots = [jnp.sum(gs * shares[m, g * pairs + p].astype(f32), -1, keepdims=True) for (g, p), gs in zip(combos, gss)]
        gscs = [(shares[m, g * pairs + p].astype(f32) * (gs - d)).astype(bf16)
                for (g, p), gs, d in zip(combos, gss, dots)]
        gqs = [unstack(nn(gsc, part_of(m, g, p, 1))) * 0.125 for (g, p), gsc in zip(combos, gscs)]
        gks = [tn(gsc, stack(part_of(m, g, p, 0))) for (g, p), gsc in zip(combos, gscs)]
        for (g, p), gq, gk, gv in zip(combos, gqs, gks, gvs):
            put(g, p, 0, gq)
            put(g, p, 1, gk)
            put(g, p, 2, gv)
            sums[:, o_q + p * 128:o_q + (p + 1) * 128] += fold(gq)
            sums[:, o_v + p * 128:o_v + (p + 1) * 128] += fold(gv)
        store(gproj, gproj_out, gproj_sem, m, slot).start()
        p_all = gproj[slot]
        for c in range(0, width, 256):
            gi = nn(p_all, awt[:, c:c + 256]) + mid[:, c:c + 256]
            gin[slot, :, c:c + 256] = gi
            gb_ref[m, :, c:c + 256] = gi.astype(bf16)

        @pl.when(stage > 0)
        def _():
            send_g(m).start()

        store(gin, gin_out, gin_sem, m, slot).start()

    lag = jnp.where(stage == last, 0, micro - 1)

    def turn():
        @pl.when(stage > 0)
        def _():
            for k in range(1, 4):
                load_w(k).wait()

        one = (lax.broadcasted_iota(jnp.int32, (256, 256), 0) == lax.broadcasted_iota(jnp.int32, (256, 256), 1)).astype(f32).astype(bf16)
        for src, dst in ((aw, awt), (ow, owt), (ew, ewt), (rw, rwt)):
            def across(k, carry, src=src, dst=dst):
                cols = pl.ds(pl.multiple_of(k * 256, 256), 256)
                for r in range(0, dst.shape[0], 256):
                    dst[r:r + 256, cols] = nt(one, src[cols, r:r + 256]).astype(bf16)
                return carry

            lax.fori_loop(0, src.shape[0] // 256, across, 0)

    def tick(t, carry):
        @pl.when((t >= 1) & (t <= micro))
        def _():
            forward(jnp.clip(t - 1, 0, micro - 1))

        @pl.when(t == jnp.where(stage > 0, 0, lag + 1))
        def _():
            turn()

        @pl.when((t >= lag + 1) & (t <= lag + micro))
        def _():
            backward(jnp.clip(t - 1 - lag, 0, micro - 1))

        return carry

    lax.fori_loop(0, 2 * micro, tick, 0)

    for m in range(micro):
        store(h_ref, h_out, hs_sem, m, m).wait()
        store(y_ref, y_out, y_sem, m, m).wait()

        @pl.when(stage < last)
        def _():
            send_y(m).wait_send()

        @pl.when(stage > 0)
        def _():
            send_g(m).wait_send()

    for m in range(max(0, micro - 2), micro):
        for src, dst, sem in staged_f + staged_b:
            store(src, dst, sem, m, m % 2).wait()


def run_pipeline(rows_in, tangents, lengths, regions, weights, vectors):
    total, width = rows_in.shape
    slots = regions.shape[1]
    rows = GROUP * slots
    micro = total // rows
    aw, ow, ew, rw = weights
    hidden = ew.shape[1]
    pairs = width // 128
    wide = 3 * width
    sum_width = 8 * width + hidden
    hbm = pl.BlockSpec(memory_space=pl.ANY)
    vmem = pl.BlockSpec(memory_space=pltpu.VMEM)
    dma = pltpu.SemaphoreType.DMA
    shape = jax.ShapeDtypeStruct
    flops = 4 * total * (4 * width * width + 2 * width * hidden)
    return pl.pallas_call(
        functools.partial(pipeline_kernel, micro),
        out_shape=(
            shape((total, width), bf16), shape((total, width), f32), shape((total, width), bf16),
            shape((total, width), bf16), shape((total, width), bf16), shape((total, hidden), bf16),
            shape((total, width), bf16), shape((total, hidden), bf16), shape((total, width), bf16),
            shape((total, wide), bf16), shape((8, sum_width), f32),
        ),
        in_specs=[hbm, hbm, pl.BlockSpec(memory_space=pltpu.SMEM), vmem] + [hbm] * 4 + [vmem] * 8,
        out_specs=(hbm,) * 10 + (vmem,),
        scratch_shapes=[pltpu.VMEM(w.shape, bf16) for w in weights] + [pltpu.VMEM(w.shape[::-1], bf16) for w in weights] + [pltpu.VMEM((regions.shape[0], 8, slots), f32), pltpu.VMEM((rows, width), bf16), pltpu.VMEM((2, rows, CHUNK), f32)] + [pltpu.VMEM((1, n), f32) for n in (wide, width, width, width, hidden, width, width, width)] + [
            pltpu.VMEM((micro, rows, width), bf16),
            pltpu.VMEM((micro, rows, width), bf16),
            pltpu.VMEM((micro, rows, width), bf16),
            pltpu.VMEM((micro, rows, width), bf16),
            pltpu.VMEM((micro, rows, wide), bf16),
            pltpu.VMEM((micro, GROUP * pairs, 2 * slots, slots), bf16),
            pltpu.VMEM((micro, rows, hidden), bf16),
            pltpu.VMEM((micro, rows, width), bf16),
            pltpu.VMEM((micro, rows, 128), f32),
            pltpu.VMEM((micro, rows, width), bf16),
            pltpu.VMEM((micro, rows, 128), f32),
            pltpu.VMEM((2, rows, width), bf16),
            pltpu.VMEM((2, rows, width), bf16),
            pltpu.VMEM((2, rows, hidden), bf16),
            pltpu.VMEM((2, rows, width), bf16),
            pltpu.VMEM((2, rows, hidden), bf16),
            pltpu.VMEM((2, rows, width), bf16),
            pltpu.VMEM((2, rows, wide), bf16),
            pltpu.VMEM((2, rows, width), f32),
            pltpu.VMEM((rows, width), f32),
            pltpu.VMEM((rows, width), f32),
        ] + [dma((4,))] + [dma((micro,))] * 8 + [dma((2,))] * 8,
        compiler_params=pltpu.CompilerParams(
            collective_id=0, has_side_effects=True, vmem_limit_bytes=63 * 1024 * 1024),
        cost_estimate=pl.CostEstimate(flops=flops, bytes_accessed=40_000_000, transcendentals=total * hidden),
    )(rows_in, tangents, lengths, regions, aw, ow, ew, rw, *vectors)


def sum_kernel(
    dp, act_any, gred_any, low_any, gexp_any, h_any, gproj_any, ctx_any, gatt_any, sums_in,
    total, vector,
    part, left, right, vec_in, *rest,
):
    steps = dp.bit_length() - 1
    plane = steps - 1
    landed = rest[:steps]
    left_sem, right_sem, send_sem, recv_sem, vsend_sem, vrecv_sem, out_sem = rest[steps:]
    units, rows, cols = part.shape
    me = lax.axis_index("dp")
    hid_blocks = act_any.shape[1] // cols
    wide_blocks = gproj_any.shape[1] // cols
    sources = (
        [(act_any, k, gred_any, 0) for k in range(hid_blocks)]
        + [(low_any, 0, gexp_any, k) for k in range(hid_blocks)]
        + [(h_any, 0, gproj_any, k) for k in range(wide_blocks)]
        + [(ctx_any, 0, gatt_any, 0)]
    )

    def bit_of(mask):
        return lax.rem(me // mask, 2)

    def masks_of(step):
        if step == 0:
            return 1, 1
        return 2 ** (1 + (step - 1) % plane), 2 ** (1 + (step - 1 + plane // 2) % plane)

    def place(unit, step):
        parity = lax.rem(unit, 2)
        first, second = masks_of(step)
        mask = first + parity * (second - first)
        bit = bit_of(first) + parity * (bit_of(second) - bit_of(first))
        return bit, me + mask * (1 - 2 * bit)

    def base(unit, step):
        start, size = 0, rows
        for k in range(step):
            size = size // 2
            start = start + place(unit, k)[0] * size
        return start, size

    def ds(start, size):
        return pl.ds(pl.multiple_of(start, 16), size)

    def reduce_copy(unit, step):
        bit, peer = place(unit, step)
        start, size = base(unit, step)
        half = size // 2
        return pltpu.make_async_remote_copy(
            src_ref=part.at[unit, ds(start + (1 - bit) * half, half)], dst_ref=landed[step].at[unit],
            send_sem=send_sem.at[step, unit], recv_sem=recv_sem.at[step, unit],
            device_id={"dp": peer}, device_id_type=MESH)

    def gather_copy(unit, step):
        peer = place(unit, step)[1]
        start, size = base(unit, step + 1)
        where = 2 * steps - 1 - step
        own = part if step == steps - 1 else total
        return pltpu.make_async_remote_copy(
            src_ref=own.at[unit, ds(start, size)], dst_ref=total.at[unit, ds(start, size)],
            send_sem=send_sem.at[where, unit], recv_sem=recv_sem.at[where, unit],
            device_id={"dp": peer}, device_id_type=MESH)

    def gather_arrival(unit, step):
        bit, peer = place(unit, step)
        start, size = base(unit, step)
        half = size // 2
        where = 2 * steps - 1 - step
        there = ds(start + (1 - bit) * half, half)
        return pltpu.make_async_remote_copy(
            src_ref=total.at[unit, there], dst_ref=total.at[unit, there],
            send_sem=send_sem.at[where, unit], recv_sem=recv_sem.at[where, unit],
            device_id={"dp": peer}, device_id_type=MESH)

    def keep(unit):
        start, size = base(unit, steps)
        rs = ds(start, size)
        return pltpu.make_async_copy(part.at[unit, rs], total.at[unit, rs], out_sem.at[unit])

    def vector_copy(step):
        peer = me + 2 ** step * (1 - 2 * bit_of(2 ** step))
        return pltpu.make_async_remote_copy(
            src_ref=vec_in.at[2 * step], dst_ref=vec_in.at[2 * step + 1],
            send_sem=vsend_sem.at[step], recv_sem=vrecv_sem.at[step],
            device_id={"dp": peer}, device_id_type=MESH)

    def loads(k, slot):
        a, ka, b, kb = sources[k]
        return (
            pltpu.make_async_copy(a.at[:, pl.ds(ka * cols, cols)], left.at[slot], left_sem.at[slot]),
            pltpu.make_async_copy(b.at[:, pl.ds(kb * cols, cols)], right.at[slot], right_sem.at[slot]),
        )

    for copy in loads(0, 0):
        copy.start()
    barrier = pltpu.get_barrier_semaphore()
    for step in range(steps):
        peer = me + 2 ** step * (1 - 2 * bit_of(2 ** step))
        pl.semaphore_signal(barrier, inc=1, device_id={"dp": peer}, device_id_type=MESH)
    v = jnp.sum(sums_in[...], 0, keepdims=True)
    lanes = vec_in.shape[2]
    for r in range(8):
        vec_in[0, r:r + 1, :] = v[:, r * lanes:(r + 1) * lanes]
    pl.semaphore_wait(barrier, steps)

    def add(unit, step):
        start, size = base(unit, step + 1)
        for b in range(0, size, 96):
            n = min(96, size - b)
            rs = ds(start + b, n)
            s = part[unit, rs, :].astype(f32) + landed[step][unit, b:b + n, :].astype(f32)
            part[unit, rs, :] = s.astype(bf16)

    def when_unit(unit, body):
        @pl.when((unit >= 0) & (unit < units))
        def _():
            body(unit)

    def make(unit):
        for s in range(rows // cols):
            block = unit * (rows // cols) + s
            slot = lax.rem(block, 2)
            for k in range(len(sources)):
                @pl.when(block == k)
                def _():
                    if k + 1 < len(sources):
                        for copy in loads(k + 1, (k + 1) % 2):
                            copy.start()
                    for copy in loads(k, k % 2):
                        copy.wait()
            for r in range(0, cols, 256):
                part[unit, s * cols + r:s * cols + r + 256, :] = tn(left[slot, :, r:r + 256], right[slot]).astype(bf16)
        reduce_copy(unit, 0).start()

    def reduce_next(step):
        def body(unit):
            reduce_copy(unit, step).wait_recv()
            add(unit, step)
            if step + 1 < steps:
                reduce_copy(unit, step + 1).start()
            else:
                gather_copy(unit, step).start()
                keep(unit).start()
        return body

    def gather_next(step):
        def body(unit):
            gather_arrival(unit, step).wait_recv()
            if step == steps - 1:
                keep(unit).wait()
            if step > 0:
                gather_copy(unit, step - 1).start()
        return body

    lag = 0
    lags = []
    for step in range(steps):
        lag += 1 if step == 0 else 2
        lags.append((lag, reduce_next(step)))
    for step in reversed(range(steps)):
        lag += 2
        lags.append((lag, gather_next(step)))

    def tick(t, carry):
        when_unit(t, make)
        for behind, body in lags:
            when_unit(t - behind, body)
        for step in range(steps):
            @pl.when(t == 2 + 2 * step)
            def _():
                if step > 0:
                    vector_copy(step - 1).wait_recv()
                    vec_in[2 * step] = vec_in[2 * step - 2] + vec_in[2 * step - 1]
                vector_copy(step).start()

        return carry

    lax.fori_loop(0, units + lag, tick, 0)
    vector_copy(steps - 1).wait_recv()
    vector[...] = vec_in[2 * steps - 2] + vec_in[2 * steps - 1]

    def finish(unit, carry):
        for step in range(steps):
            reduce_copy(unit, step).wait_send()
            gather_copy(unit, step).wait_send()
        return carry

    lax.fori_loop(0, units, finish, 0)
    for step in range(steps):
        vector_copy(step).wait_send()


def write_kernel(hid_blocks, wide_blocks, total, vector_any, y, gin, y_g, gin_g, aw_g, ab_g, ow_g, ob_g, g1_g, s1_g, ew_g, eb_g, rw_g, rb_g, g2_g, s2_g, taken, given, y_buf, gin_buf, vector, move_sem, in_sem, out_sem):
    depth, rows, cols = taken.shape
    places = (
        [(rw_g, k, 0) for k in range(hid_blocks)] + [(ew_g, 0, k) for k in range(hid_blocks)]
        + [(aw_g, 0, k) for k in range(wide_blocks)] + [(ow_g, 0, 0)]
    )
    split, span = cols // rows, total.shape[1] // cols
    chunks = [(block, part) for block in range(len(places)) for part in range(split)]

    def bring(k):
        block, part = chunks[k]
        start = (block % span) * cols + part * rows
        return pltpu.make_async_copy(total.at[block // span, pl.ds(start, rows)], taken.at[k % depth], in_sem.at[k % depth])

    def give(k):
        block, part = chunks[k]
        out, i, j = places[block]
        target = out.at[pl.ds(i * cols + part * rows, rows), pl.ds(j * cols, cols)]
        return pltpu.make_async_copy(given.at[k % depth], target, out_sem.at[k % depth])

    ins = (pltpu.make_async_copy(y, y_buf, move_sem.at[0]), pltpu.make_async_copy(gin, gin_buf, move_sem.at[1]))
    outs = (pltpu.make_async_copy(y_buf, y_g, move_sem.at[2]), pltpu.make_async_copy(gin_buf, gin_g, move_sem.at[3]))
    vector_copy = pltpu.make_async_copy(vector_any, vector, move_sem.at[4])
    vector_copy.start()
    for k in range(depth):
        bring(k).start()
    for move in ins:
        move.start()
    vector_copy.wait()
    piece = vector.shape[1] // 3
    at = 0
    for out in (g2_g, s2_g, rb_g, eb_g, g1_g, s1_g, ob_g, ab_g):
        for k in range(out.shape[1] // piece):
            r, c = at // 3, at % 3
            out[:, k * piece:(k + 1) * piece] = vector[r:r + 1, c * piece:(c + 1) * piece]
            at += 1
    for k in range(len(chunks)):
        bring(k).wait()
        if k >= depth:
            give(k - depth).wait()
        given[k % depth] = taken[k % depth].astype(f32)
        give(k).start()
        if k + depth < len(chunks):
            bring(k + depth).start()
        if k == depth:
            for arrived, move in zip(ins, outs):
                arrived.wait()
                move.start()
    for k in range(len(chunks) - depth, len(chunks)):
        give(k).wait()
    for move in outs:
        move.wait()


def run_sums(parts, sums, y, gin, dp):
    act, gred, low, gexp, h, gproj, ctx, gatt = parts
    total_rows, width = h.shape
    hidden, wide = act.shape[1], gproj.shape[1]
    hid_blocks, wide_blocks = hidden // width, wide // width
    blocks = 2 * hid_blocks + wide_blocks + 1
    steps = dp.bit_length() - 1
    span = 1
    while span * width % (16 * dp):
        span *= 2
    units, unit_rows = blocks // span, span * width
    lanes = sums.shape[1] // 8
    hbm = pl.BlockSpec(memory_space=pl.ANY)
    vmem = pl.BlockSpec(memory_space=pltpu.VMEM)
    dma = pltpu.SemaphoreType.DMA
    shape = jax.ShapeDtypeStruct
    total, vector = pl.pallas_call(
        functools.partial(sum_kernel, dp),
        out_shape=(shape((units, unit_rows, width), bf16), shape((8, lanes), f32)),
        in_specs=[hbm] * 8 + [vmem],
        out_specs=(hbm, vmem),
        scratch_shapes=[
            pltpu.VMEM((units, unit_rows, width), bf16),
            pltpu.VMEM((2, total_rows, width), bf16),
            pltpu.VMEM((2, total_rows, width), bf16),
            pltpu.VMEM((2 * steps, 8, lanes), f32),
        ] + [pltpu.VMEM((units, unit_rows // 2 ** (k + 1), width), bf16) for k in range(steps)] + [
            dma((2,)), dma((2,)), dma((2 * steps, units)), dma((2 * steps, units)), dma((steps,)), dma((steps,)), dma((units,)),
        ],
        compiler_params=pltpu.CompilerParams(
            collective_id=1, has_side_effects=True, vmem_limit_bytes=58 * 1024 * 1024),
    )(act, gred, low, gexp, h, gproj, ctx, gatt, sums)

    def one(count):
        return shape((1, count), f32), vmem

    outs = [
        (shape(y.shape, y.dtype), hbm), (shape(gin.shape, gin.dtype), hbm),
        (shape((width, wide), f32), hbm),
        one(2 * width),
        (shape((width, width), f32), hbm),
        one(width), one(width), one(width),
        (shape((width, hidden), f32), hbm),
        one(hidden),
        (shape((hidden, width), f32), hbm),
        one(width), one(width), one(width),
    ]
    return pl.pallas_call(
        functools.partial(write_kernel, hid_blocks, wide_blocks),
        out_shape=tuple(o[0] for o in outs),
        in_specs=[hbm] * 4,
        out_specs=tuple(o[1] for o in outs),
        scratch_shapes=[
            pltpu.VMEM((PARTS, width // 2, width), bf16), pltpu.VMEM((PARTS, width // 2, width), f32),
            pltpu.VMEM(y.shape, y.dtype), pltpu.VMEM(gin.shape, gin.dtype),
            pltpu.VMEM((8, lanes), f32), dma((5,)), dma((PARTS,)), dma((PARTS,)),
        ],
        compiler_params=pltpu.CompilerParams(vmem_limit_bytes=52 * 1024 * 1024),
    )(total, vector, y, gin)


def local(
    layer_input, lengths, regions, cotangent,
    attend_weight, attend_bias, output_weight, output_bias, first_gain, first_shift,
    expand_weight, expand_bias, reduce_weight, reduce_bias, second_gain, second_shift,
):
    seqs, slots, width = layer_input.shape
    total = seqs * slots
    vectors = (attend_bias, output_bias, first_gain, first_shift, expand_bias, reduce_bias, second_gain, second_shift)
    weights = (attend_weight[0], output_weight[0], expand_weight[0], reduce_weight[0])
    y, gin, h, ctx, low, act, gred, gexp, gatt, gproj, sums = run_pipeline(
        layer_input.reshape(total, width), cotangent.reshape(total, width), lengths, regions, weights, vectors)
    y, gin, *grads = run_sums((act, gred, low, gexp, h, gproj, ctx, gatt), sums, y, gin, lax.axis_size("dp"))
    return (y.reshape(1, seqs, slots, width), gin.reshape(1, seqs, slots, width)) + tuple(
        g[None] if g.shape[0] > 1 else g for g in grads)


def solution(mesh):
    rows = P("dp", None, None)
    cube = P("pipe", None, None)
    flat = P("pipe", None)
    grads = P("pipe", "dp", None, None)
    return jax.shard_map(
        local,
        mesh=mesh,
        in_specs=(rows, P("dp"), P("dp", None), rows, cube, flat, cube, flat, flat, flat, cube, flat, cube, flat, flat, flat),
        out_specs=(grads, grads, cube, flat, cube, flat, flat, flat, cube, flat, cube, flat, flat, flat),
        check_vma=False,
    )
```
